32 devices in a mesh: gx: 4 (over z), gy: 4 (over y, x), gz: 2 (over core).
Axes of the slice: x: 2, y: 2, z: 4, core: 2. Of those that a mesh axis runs over, the one named last changes fastest.
Arguments:
- positions: float32 [4, 4, 4, 192], P('gx', 'gy', 'gz'), may hold values from 0 to 1, as said below
- species: int32 [4, 4, 4, 64], P('gx', 'gy', 'gz'), may hold values from 0 to 4
- neighbors: int32 [4, 4, 4, 512], P('gx', 'gy', 'gz'), may hold values from 0 to 1727, as said below
- center_table: bfloat16 [5, 128], replicated, may hold values from -4 to 4
- neighbor_table: bfloat16 [5, 128], replicated, may hold values from -4 to 4
- radial_weight: bfloat16 [8, 128], replicated, may hold values from -2 to 2
- mix_weight: bfloat16 [128, 128], replicated, may hold values from -0.5 to 0.5
- env_weight: bfloat16 [128, 128], replicated, may hold values from -0.5 to 0.5
- update_weight: bfloat16 [384, 128], replicated, may hold values from -0.3125 to 0.3125
- second_weight: bfloat16 [128, 128], replicated, may hold values from -0.5 to 0.5
- readout: float32 [128], replicated, may hold values from -0.5 to 0.5
Outputs:
- atom_energy: float32 [4, 4, 4, 64], P('gx', 'gy', 'gz')
- forces: float32 [4, 4, 4, 192], P('gx', 'gy', 'gz')
The draws below stay inside these ranges and needn't reach their ends.
Inputs may be any that keep to these rules, and one draw needn't show every extreme that they name: `positions`: every coordinate lies inside its block; atoms of a block sit on a jittered sublattice, so any two atoms are at least 0.4 / cube root of 64 apart. `neighbors`: each atom lists 8 different atoms of the 27 blocks around and including its own, never itself; a code is offset index times 64 plus slot.
All inputs are finite; a program needn't handle non-finite values.
Results may differ from the reference program's by a relative error of at most 0.011.
Values may be sent and summed in bfloat16 or wider, within the bound.
No kernel may reach another device: no remote copies, remote signals or barrier semaphores. Data moves between devices by JAX's collectives and lax.ppermute only.
A program may use at most 64 MiB of HBM per device.

```python
import math
import jax
import jax.numpy as jnp
from jax import lax

SLOTS = 64
NEIGH = 8
WIDTH = 128
NBASIS = 8
NSPEC = 5
NX = 4
NY = 4
NZ = 4


def draw_positions(key, part):
    side = 2 if SLOTS == 8 else 3 if SLOTS == 27 else 4
    lattice_ids = jnp.arange(SLOTS, dtype=jnp.int32)
    lattice = jnp.stack([lattice_ids // (side * side), lattice_ids // side % side, lattice_ids % side]).astype(jnp.float32)
    jitter = jax.random.uniform(key, (NX, NY, NZ, 3, SLOTS), jnp.float32, -0.3, 0.3)
    placed = (lattice + 0.5 + jitter) / side
    return placed.reshape(NX, NY, NZ, 3 * SLOTS)


def draw_neighbors(key, part):
    span = 27 * SLOTS - 1
    start_key = jax.random.fold_in(key, 11)
    stride_key = jax.random.fold_in(key, 23)
    starting = jax.random.randint(start_key, (NX, NY, NZ, SLOTS, 1), 0, span, jnp.int32)
    stride = jax.random.randint(stride_key, (NX, NY, NZ, SLOTS, 1), 1, (span - 1) // (NEIGH - 1) + 1, jnp.int32)
    ranks = jnp.arange(NEIGH, dtype=jnp.int32)
    candidate = (starting + ranks * stride) % span
    self_code = 13 * SLOTS + jnp.arange(SLOTS, dtype=jnp.int32)[:, None]
    codes = candidate + (candidate >= self_code).astype(jnp.int32)
    return codes.reshape(NX, NY, NZ, SLOTS * NEIGH)


def place_ends(entries, own_key, low, high):
    spot = [jax.random.randint(jax.random.fold_in(own_key, axis), (), 0, length) for axis, length in enumerate(entries.shape)]
    longest = entries.shape.index(max(entries.shape))
    next_to = spot[:longest] + [(spot[longest] + 1) % entries.shape[longest]] + spot[longest + 1:]
    return entries.at[tuple(spot)].set(low).at[tuple(next_to)].set(high)


def gaussian(own_key, shape, spread, bound, kind=jnp.bfloat16):
    array = jax.random.normal(own_key, shape, jnp.float32) * spread
    return jnp.minimum(jnp.maximum(array, -bound), bound).astype(kind)


def setup_inputs(seed: int = 0) -> dict:
    key_of = jax.random.split(jax.random.key(seed), 12)
    return {
        "positions": draw_positions(jax.random.fold_in(key_of[11], 71), 0),
        "species": place_ends(jax.random.randint(key_of[1], (NX, NY, NZ, SLOTS), 0, NSPEC), jax.random.fold_in(key_of[1], 1), 0, NSPEC - 1).astype(jnp.int32),
        "neighbors": draw_neighbors(jax.random.fold_in(key_of[11], 71), 0),
        "center_table": gaussian(key_of[3], (NSPEC, WIDTH), 1.0, 4.0),
        "neighbor_table": gaussian(key_of[4], (NSPEC, WIDTH), 1.0, 4.0),
        "radial_weight": gaussian(key_of[5], (NBASIS, WIDTH), NBASIS ** -0.5, 2.0),
        "mix_weight": gaussian(key_of[6], (WIDTH, WIDTH), WIDTH ** -0.5, 0.5),
        "env_weight": gaussian(key_of[7], (WIDTH, WIDTH), WIDTH ** -0.5, 0.5),
        "update_weight": gaussian(key_of[8], (3 * WIDTH, WIDTH), (3 * WIDTH) ** -0.5, 0.3125),
        "second_weight": gaussian(key_of[9], (WIDTH, WIDTH), WIDTH ** -0.5, 0.5),
        "readout": gaussian(key_of[10], (WIDTH,), WIDTH ** -0.5, 0.5, jnp.float32),
    }


CUTOFF = 4.0
SHARPNESS = 2.0
HIGH = lax.Precision.HIGHEST

def harmonics(displacement):
    distance = jnp.sqrt(lax.optimization_barrier(jnp.sum(displacement * displacement, axis=0)))
    unit_vec = displacement / distance
    unit_x, unit_y, unit_z = (unit_vec[0], unit_vec[1], unit_vec[2])
    root_three = math.sqrt(3.0)
    angular = jnp.stack([jnp.ones_like(unit_x), unit_x, unit_y, unit_z, root_three * unit_x * unit_y, root_three * unit_y * unit_z, 0.5 * (3.0 * unit_z * unit_z - 1.0), root_three * unit_x * unit_z, 0.5 * root_three * (unit_x * unit_x - unit_y * unit_y)], axis=0)
    return (distance, angular)

def layer_one(displacement, onehot_center, onehot_other, params):
    radial_weight, center_table, neighbor_table, mix_weight, env_weight, update_weight = params
    distance, angular = harmonics(displacement)
    nbasis = radial_weight.shape[0]
    centers = CUTOFF * (jnp.arange(nbasis, dtype=jnp.float32) + 0.5) / nbasis
    cut_ratio = distance / CUTOFF
    envelope = (1.0 - cut_ratio * cut_ratio) ** 2
    radial_basis = jnp.exp(-SHARPNESS * (distance[:, None] - centers[None, :]) ** 2) * envelope[:, None]
    before = jnp.dot(radial_basis.astype(jnp.bfloat16), radial_weight, preferred_element_type=jnp.float32)
    before = before + jnp.dot(onehot_center, center_table, preferred_element_type=jnp.float32)
    before = before + jnp.dot(onehot_other, neighbor_table, preferred_element_type=jnp.float32)
    activated = jax.nn.silu(before).astype(jnp.bfloat16)
    latent = jax.nn.silu(jnp.dot(activated, mix_weight, preferred_element_type=jnp.float32))
    env_terms = jnp.dot(latent.astype(jnp.bfloat16), env_weight, preferred_element_type=jnp.float32)
    channels = latent.shape[1]
    center_count = latent.shape[0] // NEIGH
    env_terms = env_terms.reshape(center_count, NEIGH, channels)
    harmonic_grid = angular.reshape(9, center_count, NEIGH)
    environment = jnp.einsum('akc,mak->amc', env_terms, harmonic_grid, precision=HIGH) / NEIGH
    pieces = []
    for start_m, stop_m in ((0, 1), (1, 4), (4, 9)):
        pieces.append(jnp.einsum('amc,mak->akc', environment[:, start_m:stop_m], harmonic_grid[start_m:stop_m], precision=HIGH))
    invariants = jnp.concatenate(pieces, axis=2).reshape(center_count * NEIGH, 3 * channels)
    invariants = invariants.astype(jnp.bfloat16)
    update = jnp.dot(invariants, update_weight, preferred_element_type=jnp.float32)
    edge_latent = jax.nn.silu(latent + update)
    atom_latent = lax.optimization_barrier(jnp.mean(edge_latent.reshape(center_count, NEIGH, channels), axis=1))
    return (atom_latent, edge_latent)

def layer_two(edge_latent, other_latent, second_weight, readout):
    product = (edge_latent * other_latent).astype(jnp.bfloat16)
    hidden = jax.nn.silu(jnp.dot(product, second_weight, preferred_element_type=jnp.float32))
    edge_energy = jnp.dot(hidden, readout, precision=HIGH)
    return lax.optimization_barrier(jnp.sum(edge_energy.reshape(-1, NEIGH), axis=1))

def edge_model(rel_center, rel_other, offsets, onehot_center, onehot_other, params):
    displacement = (offsets + (rel_other - rel_center[:, :, None])).reshape(3, -1)
    return layer_one(displacement, onehot_center, onehot_other, params)

def one_hot(labels, count):
    return (labels[:, None] == jnp.arange(count, dtype=jnp.int32)[None, :]).astype(jnp.bfloat16)

def slab_lists(neighbors, species_flat, slab):
    codes = lax.dynamic_index_in_dim(neighbors, slab, 0, keepdims=False).reshape(NY, NZ, SLOTS, NEIGH)
    offset_code = codes // SLOTS
    slot_other = codes % SLOTS
    step_x = offset_code // 9 - 1
    step_y = offset_code // 3 % 3 - 1
    step_z = offset_code % 3 - 1
    index_y = jnp.arange(NY, dtype=jnp.int32).reshape(NY, 1, 1, 1)
    index_z = jnp.arange(NZ, dtype=jnp.int32).reshape(1, NZ, 1, 1)
    cell_other = ((slab + step_x) % NX * NY + (index_y + step_y) % NY) * NZ + (index_z + step_z) % NZ
    per_slab = NY * NZ * SLOTS
    other_index = (cell_other * SLOTS + slot_other).reshape(per_slab, NEIGH).astype(jnp.int32)
    own_index = (slab * per_slab + jnp.arange(per_slab, dtype=jnp.int32)).astype(jnp.int32)
    offsets = jnp.stack([step_x, step_y, step_z]).astype(jnp.float32).reshape(3, per_slab, NEIGH)
    center_species = jnp.broadcast_to(species_flat[own_index][:, None], (per_slab, NEIGH)).reshape(-1)
    onehot_center = one_hot(center_species, NSPEC)
    onehot_other = one_hot(species_flat[other_index.reshape(-1)], NSPEC)
    return (own_index, other_index, offsets, onehot_center, onehot_other)

def reference(positions, species, neighbors, center_table, neighbor_table, radial_weight, mix_weight, env_weight, update_weight, second_weight, readout):
    params = (radial_weight, center_table, neighbor_table, mix_weight, env_weight, update_weight)
    total = NX * NY * NZ * SLOTS
    flat_pos = positions.reshape(NX, NY, NZ, 3, SLOTS).transpose(3, 0, 1, 2, 4).reshape(3, total)
    species_flat = species.reshape(total)
    slabs = jnp.arange(NX, dtype=jnp.int32)

    def prepare(slab):
        lists = slab_lists(neighbors, species_flat, slab)
        rel_center = flat_pos[:, lists[0]]
        rel_other = flat_pos[:, lists[1]]
        return (lists, rel_center, rel_other)

    def first_pass(slab):
        lists, rel_center, rel_other = prepare(slab)
        return edge_model(rel_center, rel_other, lists[2], lists[3], lists[4], params)[0]
    atom_latent = lax.map(first_pass, slabs).reshape(total, WIDTH)
    coarse_latent = lax.optimization_barrier(atom_latent.astype(jnp.bfloat16)).astype(jnp.float32)

    def both_layers(slab):
        lists, rel_center, rel_other = prepare(slab)

        def first(center_pos, other_pos):
            return edge_model(center_pos, other_pos, lists[2], lists[3], lists[4], params)
        outputs, back_one = jax.vjp(first, rel_center, rel_other)
        other_latent = coarse_latent[lists[1].reshape(-1)]

        def second(edge_latent, neighbor_latent):
            return layer_two(edge_latent, neighbor_latent, second_weight, readout)
        energy, back_two = jax.vjp(second, outputs[1], other_latent)
        grad_edge, grad_other = back_two(jnp.ones_like(energy))
        return (lists, energy, grad_edge, grad_other, back_one)

    def gather_step(carry, slab):
        lists, energy, grad_edge, grad_other, back_one = both_layers(slab)
        carry = carry.at[lists[1].reshape(-1)].add(grad_other)
        return (carry, energy)
    latent_grad, energies = lax.scan(gather_step, jnp.zeros((total, WIDTH), jnp.float32), slabs)

    def force_step(carry, slab):
        lists, energy, grad_edge, grad_other, back_one = both_layers(slab)
        grad_center, grad_other_pos = back_one((latent_grad[lists[0]], grad_edge))
        carry = carry.at[:, lists[0]].add(grad_center)
        carry = carry.at[:, lists[1].reshape(-1)].add(grad_other_pos.reshape(3, -1))
        return (carry, None)
    motion, unused = lax.scan(force_step, jnp.zeros((3, total), jnp.float32), slabs)
    forces = -motion.reshape(3, NX, NY, NZ, SLOTS).transpose(1, 2, 3, 0, 4).reshape(NX, NY, NZ, 3 * SLOTS)
    atom_energy = energies.reshape(NX, NY, NZ, SLOTS)
    return (atom_energy, forces)
```

```python
import functools
import math

import jax
import jax.numpy as jnp
from jax import lax
from jax.experimental import pallas as pl
from jax.experimental.pallas import tpu as pltpu
from jax.sharding import PartitionSpec as P

NEIGH = 8
ATOMS = 128
EDGES = NEIGH * ATOMS
CHUNKS = 18
CUTOFF = 4.0
SHARPNESS = 2.0
ROOT3 = math.sqrt(3.0)
F32 = jnp.float32
BF16 = jnp.bfloat16
TILE = 256


def shifted(value, axis, step):
    count = lax.axis_size(axis)
    return lax.ppermute(value, axis, [(i, (i + step) % count) for i in range(count)])


def gather_halo(chunk):
    for axis in ("gx", "gy"):
        lower = shifted(chunk, axis, 1)
        upper = shifted(chunk, axis, -1)
        chunk = jnp.concatenate([chunk, lower, upper], axis=0)
    if lax.axis_size("gz") == 2:
        return chunk, shifted(chunk, "gz", 1)
    half = chunk.shape[-1] // 2
    above = shifted(chunk[..., :half], "gz", -1)
    below = shifted(chunk[..., half:], "gz", 1)
    return chunk, jnp.concatenate([above, below], axis=-1)


def reduce_halo(own, other):
    if lax.axis_size("gz") == 2:
        back = shifted(other, "gz", 1)
    else:
        half = other.shape[-1] // 2
        first = shifted(other[..., :half], "gz", 1)
        second = shifted(other[..., half:], "gz", -1)
        back = jnp.concatenate([first, second], axis=-1)
    kind = own.dtype
    own = own.astype(F32) + back.astype(F32)
    for axis, size in (("gy", 3), ("gx", 1)):
        lower = shifted(own[size : 2 * size].astype(kind), axis, -1)
        upper = shifted(own[2 * size :].astype(kind), axis, 1)
        own = own[:size] + lower.astype(F32) + upper.astype(F32)
    return own


def pack_kernel(pos_ref, spec_ref, out_ref):
    out_ref[...] = jnp.zeros(out_ref.shape, F32)
    slots = spec_ref.shape[-1]
    for block in range(2):
        lanes = slice(block * slots, (block + 1) * slots)
        for c in range(3):
            out_ref[0, c : c + 1, lanes] = pos_ref[0, 0, block : block + 1, c * slots : (c + 1) * slots]
        out_ref[0, 3:4, lanes] = spec_ref[0, 0, block : block + 1, :].astype(F32)


def prep_kernel(
    nb_ref, center_ref, neighbor_ref, radial_ref, mix_ref, env_ref, upd_ref, second_ref, readout_ref,
    code_ref, onehot_ref, wcat_ref, mixt_ref, envt_ref, updt_ref, secondt_ref, rocol_ref, pad_ref,
):
    width = nb_ref.shape[-1]
    slots = width // NEIGH
    lane = lax.broadcasted_iota(jnp.int32, (NEIGH, width), 1)
    row = lax.broadcasted_iota(jnp.int32, (NEIGH, width), 0)
    mine = (lane & (NEIGH - 1)) == row
    spot = lax.broadcasted_iota(jnp.int32, (width, ATOMS), 0) // NEIGH
    column = lax.broadcasted_iota(jnp.int32, (width, ATOMS), 1)
    total = jnp.zeros((NEIGH, ATOMS), F32)
    for block in range(2):
        listed = jnp.broadcast_to(nb_ref[0, 0, block : block + 1, :], (NEIGH, width))
        listed = jnp.where(mine, listed, 0)
        high = (listed >> 4).astype(F32).astype(BF16)
        low = (listed & 15).astype(F32).astype(BF16)
        pick = jnp.where(spot + block * slots == column, 1.0, 0.0).astype(BF16)
        total = total + 16.0 * jnp.dot(high, pick, preferred_element_type=F32)
        total = total + jnp.dot(low, pick, preferred_element_type=F32)
    code = (total + 0.5).astype(jnp.int32)
    offset = code >> 6
    slot = code & 63
    step_x = jnp.where(offset >= 18, 1, jnp.where(offset >= 9, 0, -1))
    rest = offset - 9 * (step_x + 1)
    step_y = jnp.where(rest >= 6, 1, jnp.where(rest >= 3, 0, -1))
    step_z = rest - 3 * (step_y + 1) - 1
    block = lax.broadcasted_iota(jnp.int32, (NEIGH, ATOMS), 1) // slots
    level = block + step_z
    outside = jnp.where((level < 0) | (level > 1), 1, 0)
    place_x = jnp.where(step_x == 0, 0, jnp.where(step_x < 0, 1, 2))
    place_y = jnp.where(step_y == 0, 0, jnp.where(step_y < 0, 1, 2))
    chunk = outside * 9 + place_y * 3 + place_x
    target = chunk * ATOMS + (level & 1) * slots + slot
    code_ref[0] = target
    code_ref[1] = step_x
    code_ref[2] = step_y
    code_ref[3] = step_z

    pad_ref[...] = jnp.zeros(pad_ref.shape, F32)
    pad_ref[0:8, :] = radial_ref[...].astype(F32)
    pad_ref[8 : 8 + neighbor_ref.shape[0], :] = neighbor_ref[...].astype(F32)
    pad_ref[16 : 16 + center_ref.shape[0], :] = center_ref[...].astype(F32)
    wcat_ref[...] = pad_ref[...].T[:, :32].astype(BF16)
    mixt_ref[...] = mix_ref[...].astype(F32).T.astype(BF16)
    envt_ref[...] = env_ref[...].astype(F32).T.astype(BF16)
    secondt_ref[...] = second_ref[...].astype(F32).T.astype(BF16)
    for part in range(3):
        span = slice(part * ATOMS, (part + 1) * ATOMS)
        updt_ref[:, span] = upd_ref[span, :].astype(F32).T.astype(BF16)
    rocol_ref[...] = jnp.broadcast_to(readout_ref[...], (ATOMS, ATOMS)).T

    atom = lax.broadcasted_iota(jnp.int32, (ATOMS, ATOMS), 0)
    for k in range(NEIGH):
        aim = jnp.broadcast_to(target[k : k + 1, :], (ATOMS, ATOMS)) - atom

        def fill(c, carry, k=k, aim=aim):
            rows = pl.ds(pl.multiple_of(c * ATOMS, ATOMS), ATOMS)
            hit = jnp.where(aim == c * ATOMS, 1.0, 0.0)
            onehot_ref[rows, k * ATOMS : (k + 1) * ATOMS] = hit.astype(BF16)
            return carry

        lax.fori_loop(0, CHUNKS, fill, 0)


def sigmoid(v):
    return 0.5 * jnp.tanh(0.5 * v) + 0.5


def silu_pair(v):
    s = sigmoid(v)
    value = v * s
    return value, s + value * (1.0 - s)


def angular_rows(ux, uy, uz):
    return [
        None, ux, uy, uz, ROOT3 * ux * uy, ROOT3 * uy * uz, 0.5 * (3.0 * uz * uz - 1.0),
        ROOT3 * ux * uz, 0.5 * ROOT3 * (ux * ux - uy * uy),
    ]


def spread_rows(yb_ref, angular):
    for m in range(1, 9):
        for k in range(NEIGH):
            yb_ref[m * NEIGH + k] = jnp.broadcast_to(angular[m][k : k + 1, :], (8, ATOMS))


def basis_parts(r_row):
    row = lax.broadcasted_iota(jnp.int32, (8, ATOMS), 0).astype(F32)
    centers = CUTOFF * (row + 0.5) / 8.0
    r = jnp.broadcast_to(r_row, (8, ATOMS))
    ratio = r * (1.0 / CUTOFF)
    inner = 1.0 - ratio * ratio
    gap = r - centers
    return jnp.exp(-SHARPNESS * gap * gap), gap, inner, ratio


PIECE = (0, 1, 1, 1, 2, 2, 2, 2, 2)


def forward_kernel(
    own_ref, other_ref, code_ref, wcat_ref, mixt_ref, envt_ref, updt_ref,
    table_ref, edge_ref, dsb_ref, dsl_ref, dse_ref, env_ref, v_ref, geo_ref, yb_ref, inv_ref, lat_ref,
):
    target = code_ref[0]
    chunk = target >> 7
    lane = target & 127
    found = [jnp.zeros((NEIGH, ATOMS), F32) for _ in range(4)]
    for c in range(CHUNKS):
        ref = own_ref if c < 9 else other_ref
        hit = chunk == c
        for f in range(4):
            row = jnp.broadcast_to(ref[c % 9, f : f + 1, :], (NEIGH, ATOMS))
            value = jnp.take_along_axis(row, lane, axis=1)
            found[f] = jnp.where(hit, value, found[f])
    d = [
        code_ref[1 + c].astype(F32) + (found[c] - jnp.broadcast_to(own_ref[0, c : c + 1, :], (NEIGH, ATOMS)))
        for c in range(3)
    ]
    r = jnp.sqrt(d[0] * d[0] + d[1] * d[1] + d[2] * d[2])
    ux, uy, uz = d[0] / r, d[1] / r, d[2] / r
    geo_ref[0] = r
    geo_ref[1] = ux
    geo_ref[2] = uy
    geo_ref[3] = uz
    spread_rows(yb_ref, angular_rows(ux, uy, uz))

    kind = lax.broadcasted_iota(jnp.int32, (8, ATOMS), 0).astype(F32)
    center_hot = jnp.where(jnp.broadcast_to(own_ref[0, 3:4, :], (8, ATOMS)) == kind, 1.0, 0.0)
    zero = jnp.zeros((8, ATOMS), F32)
    columns = []
    for k in range(NEIGH):
        bump, gap, inner, ratio = basis_parts(r[k : k + 1, :])
        other_hot = jnp.where(jnp.broadcast_to(found[3][k : k + 1, :], (8, ATOMS)) == kind, 1.0, 0.0)
        columns.append(jnp.concatenate([bump * (inner * inner), other_hot, center_hot, zero], axis=0).astype(BF16))
    for j in range(EDGES // TILE):
        span = slice(j * TILE, (j + 1) * TILE)
        per = TILE // ATOMS
        x = jnp.concatenate(columns[j * per : (j + 1) * per], axis=1)
        act, ds = silu_pair(jnp.dot(wcat_ref[...], x, preferred_element_type=F32))
        dsb_ref[:, span] = ds
        latent, ds = silu_pair(jnp.dot(mixt_ref[...], act.astype(BF16), preferred_element_type=F32))
        dsl_ref[:, span] = ds
        lat_ref[:, span] = latent
        env_ref[:, span] = jnp.dot(envt_ref[...], latent.astype(BF16), preferred_element_type=F32)
    for t in range(8):
        halves = []
        for h in range(2):
            rows = slice(t * 16 + h * 8, t * 16 + h * 8 + 8)
            env = [env_ref[rows, k * ATOMS : (k + 1) * ATOMS] for k in range(NEIGH)]
            field = []
            for m in range(9):
                terms = [env[k] if m == 0 else env[k] * yb_ref[m * NEIGH + k] for k in range(NEIGH)]
                while len(terms) > 1:
                    terms = [terms[i] + terms[i + 1] for i in range(0, len(terms), 2)]
                field.append(terms[0] * 0.125)
                v_ref[m, rows, :] = field[m]
            out = []
            for k in range(NEIGH):
                sums = [field[0], None, None]
                for m in range(1, 9):
                    term = field[m] * yb_ref[m * NEIGH + k]
                    sums[PIECE[m]] = term if sums[PIECE[m]] is None else sums[PIECE[m]] + term
                out.append(sums)
            halves.append(out)
        for k in range(NEIGH):
            for p in range(3):
                both = jnp.concatenate([halves[0][k][p], halves[1][k][p]], axis=0)
                inv_ref[p * ATOMS + t * 16 : p * ATOMS + t * 16 + 16, k * ATOMS : (k + 1) * ATOMS] = both.astype(BF16)
    mean = jnp.zeros((ATOMS, ATOMS), F32)
    for j in range(EDGES // TILE):
        span = slice(j * TILE, (j + 1) * TILE)
        update = jnp.dot(updt_ref[...], inv_ref[:, span], preferred_element_type=F32)
        edge, ds = silu_pair(lat_ref[:, span] + update)
        edge_ref[:, span] = edge
        dse_ref[:, span] = ds
        for i in range(TILE // ATOMS):
            mean = mean + edge[:, i * ATOMS : (i + 1) * ATOMS]
    table_ref[0] = (mean * 0.125).astype(BF16)


def second_kernel(
    own_ref, other_ref, onehot_ref, edge_ref, second_ref, secondt_ref, rocol_ref,
    energy_ref, grad_edge_ref, back_own_ref, back_other_ref, grad_ref,
):
    table = jnp.concatenate([own_ref[c] for c in range(9)] + [other_ref[c] for c in range(9)], axis=1)
    rocol = rocol_ref[...]
    total = jnp.zeros((ATOMS, ATOMS), F32)
    for j in range(EDGES // TILE):
        span = slice(j * TILE, (j + 1) * TILE)
        other = jnp.dot(table, onehot_ref[:, span], preferred_element_type=F32)
        edge = edge_ref[:, span]
        hidden, ds = silu_pair(jnp.dot(secondt_ref[...], (edge * other).astype(BF16), preferred_element_type=F32))
        for i in range(TILE // ATOMS):
            total = total + hidden[:, i * ATOMS : (i + 1) * ATOMS]
        grad_hidden = ds * jnp.concatenate([rocol] * (TILE // ATOMS), axis=1)
        grad_prod = jnp.dot(second_ref[...], grad_hidden.astype(BF16), preferred_element_type=F32)
        grad_prod = grad_prod.astype(BF16).astype(F32)
        grad_edge_ref[:, span] = grad_prod * other
        grad_ref[:, span] = (grad_prod * edge).astype(BF16)
    energy = jnp.sum(total * rocol, axis=0, keepdims=True)
    slots = energy_ref.shape[-1]
    for block in range(2):
        energy_ref[0, 0, block : block + 1, :] = energy[:, block * slots : (block + 1) * slots]
    grad = grad_ref[...]
    for c in range(CHUNKS):
        rows = slice(c * ATOMS, (c + 1) * ATOMS)
        back = lax.dot_general(
            grad, onehot_ref[rows, :], (((1,), (1,)), ((), ())), preferred_element_type=F32
        )
        ref = back_own_ref if c < 9 else back_other_ref
        ref[c % 9] = back.astype(BF16)


def backward_kernel(
    owned_ref, grad_edge_ref, dse_ref, dsl_ref, dsb_ref, env_ref, v_ref, geo_ref, onehot_ref,
    upd_ref, envw_ref, mix_ref, radial_ref,
    own_ref, other_ref, yb_ref, dinv_ref, denv_ref, dlat_ref, part_ref, force_ref,
):
    r, ux, uy, uz = (geo_ref[i] for i in range(4))
    angular = angular_rows(ux, uy, uz)
    spread_rows(yb_ref, angular)
    share = owned_ref[0] * 0.125
    for j in range(EDGES // TILE):
        span = slice(j * TILE, (j + 1) * TILE)
        d_edge = grad_edge_ref[:, span] + jnp.concatenate([share] * (TILE // ATOMS), axis=1)
        d_pre = d_edge * dse_ref[:, span]
        dlat_ref[:, span] = d_pre
        dinv_ref[:, span] = jnp.dot(upd_ref[...], d_pre.astype(BF16), preferred_element_type=F32).astype(BF16)
    part_ref[...] = jnp.zeros(part_ref.shape, F32)
    for t in range(8):
        wide = [
            [
                dinv_ref[p * ATOMS + t * 16 : p * ATOMS + t * 16 + 16, k * ATOMS : (k + 1) * ATOMS].astype(F32)
                for k in range(NEIGH)
            ]
            for p in range(3)
        ]
        halves = []
        for h in range(2):
            rows = slice(t * 16 + h * 8, t * 16 + h * 8 + 8)
            dinv = [[wide[p][k][h * 8 : h * 8 + 8] for k in range(NEIGH)] for p in range(3)]
            env = [env_ref[rows, k * ATOMS : (k + 1) * ATOMS] for k in range(NEIGH)]
            denv = [None] * NEIGH
            for m in range(9):
                down = dinv[PIECE[m]]
                terms = [down[k] if m == 0 else down[k] * yb_ref[m * NEIGH + k] for k in range(NEIGH)]
                while len(terms) > 1:
                    terms = [terms[i] + terms[i + 1] for i in range(0, len(terms), 2)]
                d_field = terms[0] * 0.125
                if m == 0:
                    denv = [d_field] * NEIGH
                    continue
                field = v_ref[m, rows, :]
                for k in range(NEIGH):
                    spot = m * NEIGH + k
                    part_ref[spot] = part_ref[spot] + (down[k] * field + env[k] * d_field)
                    denv[k] = denv[k] + d_field * yb_ref[spot]
            halves.append(denv)
        for k in range(NEIGH):
            both = jnp.concatenate([halves[0][k], halves[1][k]], axis=0)
            denv_ref[t * 16 : t * 16 + 16, k * ATOMS : (k + 1) * ATOMS] = both.astype(BF16)
    d_r_rows = []
    for j in range(EDGES // TILE):
        span = slice(j * TILE, (j + 1) * TILE)
        d_lat = jnp.dot(envw_ref[...], denv_ref[:, span], preferred_element_type=F32).astype(BF16).astype(F32)
        d_mix = (dlat_ref[:, span] + d_lat) * dsl_ref[:, span]
        d_act = jnp.dot(mix_ref[...], d_mix.astype(BF16), preferred_element_type=F32).astype(BF16).astype(F32)
        d_before = (d_act * dsb_ref[:, span]).astype(BF16)
        d_basis = jnp.dot(radial_ref[...], d_before, preferred_element_type=F32).astype(BF16).astype(F32)
        for i in range(TILE // ATOMS):
            k = j * (TILE // ATOMS) + i
            bump, gap, inner, ratio = basis_parts(r[k : k + 1, :])
            slope = bump * inner * (-2.0 * SHARPNESS * gap * inner - (4.0 / CUTOFF) * ratio)
            d_r_rows.append(jnp.sum(slope * d_basis[:, i * ATOMS : (i + 1) * ATOMS], axis=0, keepdims=True))
    d_r = jnp.concatenate(d_r_rows, axis=0)
    dy = [None]
    for m in range(1, 9):
        rows = [jnp.sum(part_ref[m * NEIGH + k], axis=0, keepdims=True) for k in range(NEIGH)]
        dy.append(jnp.concatenate(rows, axis=0))
    d_ux = dy[1] + ROOT3 * (uy * dy[4] + uz * dy[7] + ux * dy[8])
    d_uy = dy[2] + ROOT3 * (ux * dy[4] + uz * dy[5] - uy * dy[8])
    d_uz = dy[3] + ROOT3 * (uy * dy[5] + ux * dy[7]) + 3.0 * uz * dy[6]
    along = ux * d_ux + uy * d_uy + uz * d_uz
    inverse = 1.0 / r
    radial = d_r - along * inverse
    pull = [d_ux * inverse + ux * radial, d_uy * inverse + uy * radial, d_uz * inverse + uz * radial]
    high = [p.astype(BF16).astype(F32) for p in pull]
    low = [p - h for p, h in zip(pull, high)]
    zero = jnp.zeros((1, ATOMS), F32)
    for k in range(NEIGH):
        rows = [h[k : k + 1, :] for h in high] + [zero] * 5 + [q[k : k + 1, :] for q in low] + [zero] * 5
        force_ref[:, k * ATOMS : (k + 1) * ATOMS] = jnp.concatenate(rows, axis=0).astype(BF16)
    force = force_ref[...]
    center = jnp.concatenate([jnp.sum(p, axis=0, keepdims=True) for p in pull] + [zero] * 5, axis=0)
    for c in range(CHUNKS):
        rows = slice(c * ATOMS, (c + 1) * ATOMS)
        back = lax.dot_general(
            force, onehot_ref[rows, :], (((1,), (1,)), ((), ())), preferred_element_type=F32
        )
        moved = back[:8] + back[8:]
        if c == 0:
            moved = moved - center
        ref = own_ref if c < 9 else other_ref
        ref[c % 9] = moved


def finish_kernel(own_ref, out_ref):
    slots = out_ref.shape[-1] // 3
    for block in range(2):
        for c in range(3):
            out_ref[0, 0, block : block + 1, c * slots : (c + 1) * slots] = -own_ref[
                0, c : c + 1, block * slots : (block + 1) * slots
            ]


def call(kernel, outs, scratch=(), name=None, limit=24 << 20):
    whole = pl.BlockSpec(memory_space=pltpu.VMEM)
    shapes = [jax.ShapeDtypeStruct(shape, kind) for shape, kind in outs]

    def run(*args):
        return pl.pallas_call(
            kernel,
            out_shape=shapes,
            in_specs=[whole] * len(args),
            out_specs=[whole] * len(shapes),
            scratch_shapes=list(scratch),
            compiler_params=pltpu.CompilerParams(vmem_limit_bytes=limit),
            name=name,
        )(*args)

    return run


def on_device(
    positions, species, neighbors, center_table, neighbor_table, radial_weight, mix_weight,
    env_weight, update_weight, second_weight, readout,
):
    slots = species.shape[-1]
    edges = (ATOMS, EDGES)
    square = (ATOMS, ATOMS)
    (packed,) = call(pack_kernel, [((1, 8, ATOMS), F32)], name="pack")(positions, species)
    code, onehot, wcat, mixt, envt, updt, secondt, rocol = call(
        prep_kernel,
        [
            ((4, NEIGH, ATOMS), jnp.int32), ((CHUNKS * ATOMS, EDGES), BF16), ((ATOMS, 32), BF16), (square, BF16),
            (square, BF16), ((ATOMS, 3 * ATOMS), BF16), (square, BF16), (square, F32),
        ],
        [pltpu.VMEM(square, F32)],
        name="prep",
    )(
        neighbors, center_table, neighbor_table, radial_weight, mix_weight, env_weight, update_weight,
        second_weight, readout.reshape(1, ATOMS),
    )
    near, far = gather_halo(packed)
    table, edge, dsb, dsl, dse, env, field, geo = call(
        forward_kernel,
        [
            ((1,) + square, BF16), (edges, F32), (edges, F32), (edges, F32), (edges, F32), (edges, F32),
            ((9,) + square, F32), ((4, NEIGH, ATOMS), F32),
        ],
        [pltpu.VMEM((72, 8, ATOMS), F32), pltpu.VMEM((3 * ATOMS, EDGES), BF16), pltpu.VMEM(edges, F32)],
        name="forward",
    )(near, far, code, wcat, mixt, envt, updt)
    near, far = gather_halo(table)
    energy, grad_edge, back_own, back_other = call(
        second_kernel,
        [((1, 1, 2, slots), F32), (edges, F32), ((9,) + square, BF16), ((9,) + square, BF16)],
        [pltpu.VMEM(edges, BF16)],
        name="second",
    )(near, far, onehot, edge, second_weight, secondt, rocol)
    owned = reduce_halo(back_own, back_other)
    own, other = call(
        backward_kernel,
        [((9, 8, ATOMS), F32), ((9, 8, ATOMS), F32)],
        [
            pltpu.VMEM((72, 8, ATOMS), F32), pltpu.VMEM((3 * ATOMS, EDGES), BF16), pltpu.VMEM(edges, BF16),
            pltpu.VMEM(edges, F32), pltpu.VMEM((72, 8, ATOMS), F32), pltpu.VMEM((16, EDGES), BF16),
        ],
        name="backward",
    )(
        owned, grad_edge, dse, dsl, dsb, env, field, geo, onehot, update_weight, env_weight, mix_weight,
        radial_weight,
    )
    motion = reduce_halo(own, other)
    (forces,) = call(finish_kernel, [((1, 1, 2, 3 * slots), F32)], name="finish")(motion)
    return energy, forces


def solution(mesh):
    split = P("gx", "gy", "gz", None)
    return jax.shard_map(
        on_device,
        mesh=mesh,
        in_specs=(split, split, split) + (P(),) * 8,
        out_specs=(split, split),
        check_vma=False,
    )
```

```python
import functools
import math

import jax
import jax.numpy as jnp
from jax import lax
from jax.experimental import pallas as pl
from jax.experimental.pallas import tpu as pltpu
from jax.sharding import PartitionSpec as P

NEIGH = 8
ATOMS = 128
EDGES = NEIGH * ATOMS
CHUNKS = 18
CUTOFF = 4.0
SHARPNESS = 2.0
ROOT3 = math.sqrt(3.0)
F32 = jnp.float32
BF16 = jnp.bfloat16
TILE = 256


ROUTES = (((1, 0), (0, 2), (1, 2), (2, 1)), ((2, 0), (0, 1), (1, 1), (2, 2)))


def is_paired():
    return lax.axis_size("gz") == 2 and all(
        lax.axis_size(axis) % 2 == 0 and lax.axis_size(axis) >= 4 for axis in ("gx", "gy")
    )


def shifted(value, axis, step):
    count = lax.axis_size(axis)
    return lax.ppermute(value, axis, [(i, (i + step) % count) for i in range(count)])


def partner(index, way, count):
    if way == 0:
        return index
    if way == 1:
        return index ^ 1
    return (index + 1 if index % 2 else index - 1) % count


def swapped(value, slot):
    count_x, count_y = lax.axis_size("gx"), lax.axis_size("gy")
    pairs = []
    for x in range(count_x):
        for y in range(count_y):
            for core in range(2):
                way_x, way_y = ROUTES[core][slot]
                to_x, to_y = partner(x, way_x, count_x), partner(y, way_y, count_y)
                pairs.append(((x * count_y + y) * 2 + core, (to_x * count_y + to_y) * 2 + core))
    return lax.ppermute(value, ("gx", "gy", "gz"), pairs)


def gather_halo(chunk, both=None):
    if is_paired():
        if both is None:
            both = jnp.concatenate([chunk, shifted(chunk, "gz", 1)], axis=0)
        direct = [swapped(both, slot) for slot in range(4)]
        relayed = shifted(jnp.concatenate(direct, axis=0), "gz", 1)
        near = [(slot, row) for slot in range(4) for row in range(2)] + [(4, 0)]
        far = [(5, row) for row in range(8)] + [(4, 1)]
        return direct + [both, relayed], near + far
    for axis in ("gx", "gy"):
        lower = shifted(chunk, axis, 1)
        upper = shifted(chunk, axis, -1)
        chunk = jnp.concatenate([lower, upper, chunk], axis=0)
    order = [(array, row) for array in range(2) for row in range(9)]
    if lax.axis_size("gz") == 2:
        return [chunk, shifted(chunk, "gz", 1)], order
    half = chunk.shape[-1] // 2
    above = shifted(chunk[..., :half], "gz", -1)
    below = shifted(chunk[..., half:], "gz", 1)
    return [chunk, jnp.concatenate([above, below], axis=-1)], order


def reduce_halo(own, other):
    kind = own.dtype
    if is_paired():
        own = own.astype(F32) + shifted(other, "gz", 1).astype(F32)
        came = [swapped(own[2 * slot : 2 * slot + 2].astype(kind), slot).astype(F32) for slot in range(4)]
        both = came[0] + came[1] + came[2] + came[3]
        return own[8:] + both[:1] + shifted(both[1:], "gz", 1)
    if lax.axis_size("gz") == 2:
        back = shifted(other, "gz", 1)
    else:
        half = other.shape[-1] // 2
        first = shifted(other[..., :half], "gz", 1)
        second = shifted(other[..., half:], "gz", -1)
        back = jnp.concatenate([first, second], axis=-1)
    own = own.astype(F32) + back.astype(F32)
    for axis, size in (("gy", 3), ("gx", 1)):
        lower = shifted(own[:size].astype(kind), axis, -1)
        upper = shifted(own[size : 2 * size].astype(kind), axis, 1)
        own = own[2 * size :] + lower.astype(F32) + upper.astype(F32)
    return own


def place_column(step_x, step_y, outside, paired):
    if not paired:
        place_x = jnp.where(step_x == 0, 2, jnp.where(step_x < 0, 0, 1))
        place_y = jnp.where(step_y == 0, 2, jnp.where(step_y < 0, 0, 1))
        return outside * 9 + place_y * 3 + place_x
    core = lax.axis_index("gz")
    up_x = 1 - 2 * (lax.axis_index("gx") & 1)
    up_y = 1 - 2 * (lax.axis_index("gy") & 1)
    way_x = jnp.where(step_x == 0, 0, jnp.where(step_x == up_x, 1, 2))
    way_y = jnp.where(step_y == 0, 0, jnp.where(step_y == up_y, 1, 2))
    way = way_x * 3 + way_y
    chunk = 8 + 9 * outside
    for owner in range(2):
        mine = core == owner
        for slot, (to_x, to_y) in enumerate(ROUTES[owner]):
            spot = jnp.where(mine, 2 * slot + outside, 9 + 2 * slot + 1 - outside)
            chunk = jnp.where(way == to_x * 3 + to_y, spot, chunk)
    return chunk


def fetch(pairs, sems):
    copies = [pltpu.make_async_copy(a, b, sems.at[i]) for i, (a, b) in enumerate(pairs)]
    for copy in copies:
        copy.start()
    for copy in copies:
        copy.wait()


def pack_kernel(*refs):
    out_ref = refs[-1]
    out_ref[...] = jnp.zeros(out_ref.shape, F32)
    for chunk in range(out_ref.shape[0]):
        pos_ref, spec_ref = refs[2 * chunk : 2 * chunk + 2]
        slots = spec_ref.shape[-1]
        for block in range(2):
            lanes = slice(block * slots, (block + 1) * slots)
            for c in range(3):
                out_ref[chunk, c : c + 1, lanes] = pos_ref[0, 0, block : block + 1, c * slots : (c + 1) * slots]
            out_ref[chunk, 3:4, lanes] = spec_ref[0, 0, block : block + 1, :].astype(F32)


def prep_kernel(
    paired,
    nb_hbm, center_hbm, neighbor_hbm, radial_hbm, mix_hbm, env_hbm, upd_hbm, second_hbm, readout_hbm,
    code_ref, onehot_ref, wcat_ref, mixt_ref, envt_ref, updt_ref, secondt_ref, rocol_ref,
    radial_ref, mix_ref, env_ref, upd_ref, second_ref,
    nb_ref, center_ref, neighbor_ref, readout_ref, pad_ref, sems,
):
    fetch(
        (
            (nb_hbm, nb_ref), (center_hbm, center_ref), (neighbor_hbm, neighbor_ref), (radial_hbm, radial_ref),
            (mix_hbm, mix_ref), (env_hbm, env_ref), (upd_hbm, upd_ref), (second_hbm, second_ref),
            (readout_hbm, readout_ref),
        ),
        sems,
    )
    width = nb_ref.shape[-1]
    slots = width // NEIGH
    lane = lax.broadcasted_iota(jnp.int32, (NEIGH, width), 1)
    row = lax.broadcasted_iota(jnp.int32, (NEIGH, width), 0)
    mine = (lane & (NEIGH - 1)) == row
    spot = lax.broadcasted_iota(jnp.int32, (width, ATOMS), 0) // NEIGH
    column = lax.broadcasted_iota(jnp.int32, (width, ATOMS), 1)
    total = jnp.zeros((NEIGH, ATOMS), F32)
    for block in range(2):
        listed = jnp.broadcast_to(nb_ref[0, 0, block : block + 1, :], (NEIGH, width))
        listed = jnp.where(mine, listed, 0)
        high = (listed >> 4).astype(F32).astype(BF16)
        low = (listed & 15).astype(F32).astype(BF16)
        pick = jnp.where(spot + block * slots == column, 1.0, 0.0).astype(BF16)
        total = total + 16.0 * jnp.dot(high, pick, preferred_element_type=F32)
        total = total + jnp.dot(low, pick, preferred_element_type=F32)
    code = (total + 0.5).astype(jnp.int32)
    offset = code >> 6
    slot = code & 63
    step_x = jnp.where(offset >= 18, 1, jnp.where(offset >= 9, 0, -1))
    rest = offset - 9 * (step_x + 1)
    step_y = jnp.where(rest >= 6, 1, jnp.where(rest >= 3, 0, -1))
    step_z = rest - 3 * (step_y + 1) - 1
    block = lax.broadcasted_iota(jnp.int32, (NEIGH, ATOMS), 1) // slots
    level = block + step_z
    outside = jnp.where((level < 0) | (level > 1), 1, 0)
    chunk = place_column(step_x, step_y, outside, paired)
    target = chunk * ATOMS + (level & 1) * slots + slot
    code_ref[0] = target
    code_ref[1] = step_x
    code_ref[2] = step_y
    code_ref[3] = step_z

    pad_ref[...] = jnp.zeros(pad_ref.shape, F32)
    pad_ref[0:8, :] = radial_ref[...].astype(F32)
    pad_ref[8 : 8 + neighbor_ref.shape[0], :] = neighbor_ref[...].astype(F32)
    pad_ref[16 : 16 + center_ref.shape[0], :] = center_ref[...].astype(F32)
    wcat_ref[...] = pad_ref[...].T[:, :32].astype(BF16)
    mixt_ref[...] = mix_ref[...].astype(F32).T.astype(BF16)
    envt_ref[...] = env_ref[...].astype(F32).T.astype(BF16)
    secondt_ref[...] = second_ref[...].astype(F32).T.astype(BF16)
    for part in range(3):
        span = slice(part * ATOMS, (part + 1) * ATOMS)
        updt_ref[:, span] = upd_ref[span, :].astype(F32).T.astype(BF16)
    rocol_ref[...] = jnp.broadcast_to(readout_ref[...], (ATOMS, ATOMS)).T

    atom = lax.broadcasted_iota(jnp.int32, (ATOMS, ATOMS), 0)
    for k in range(NEIGH):
        aim = jnp.broadcast_to(target[k : k + 1, :], (ATOMS, ATOMS)) - atom

        def fill(c, carry, k=k, aim=aim):
            rows = pl.ds(pl.multiple_of(c * ATOMS, ATOMS), ATOMS)
            hit = jnp.where(aim == c * ATOMS, 1.0, 0.0)
            onehot_ref[rows, k * ATOMS : (k + 1) * ATOMS] = hit.astype(BF16)
            return carry

        lax.fori_loop(0, CHUNKS, fill, 0)


def sigmoid(v):
    return 0.5 * jnp.tanh(0.5 * v) + 0.5


def silu_pair(v):
    s = sigmoid(v)
    value = v * s
    return value, s + value * (1.0 - s)


def angular_rows(ux, uy, uz):
    return [
        None, ux, uy, uz, ROOT3 * ux * uy, ROOT3 * uy * uz, 0.5 * (3.0 * uz * uz - 1.0),
        ROOT3 * ux * uz, 0.5 * ROOT3 * (ux * ux - uy * uy),
    ]


def spread_rows(yb_ref, angular):
    for m in range(1, 9):
        for k in range(NEIGH):
            yb_ref[m * NEIGH + k] = jnp.broadcast_to(angular[m][k : k + 1, :], (8, ATOMS))


def basis_parts(r_row):
    row = lax.broadcasted_iota(jnp.int32, (8, ATOMS), 0).astype(F32)
    centers = CUTOFF * (row + 0.5) / 8.0
    r = jnp.broadcast_to(r_row, (8, ATOMS))
    ratio = r * (1.0 / CUTOFF)
    inner = 1.0 - ratio * ratio
    gap = r - centers
    return jnp.exp(-SHARPNESS * gap * gap), gap, inner, ratio


PIECE = (0, 1, 1, 1, 2, 2, 2, 2, 2)


def forward_kernel(parts, order, *refs):
    atoms = [(refs[array], row) for array, row in order]
    (
        code_ref, wcat_ref, mixt_ref, envt_ref, updt_ref,
        table_ref, edge_ref, dsb_ref, dsl_ref, dse_ref, env_ref, v_ref, geo_ref, yb_ref, inv_ref, lat_ref,
    ) = refs[parts:]
    home_ref, home = atoms[8]
    target = code_ref[0]
    chunk = target >> 7
    lane = target & 127
    found = [jnp.zeros((NEIGH, ATOMS), F32) for _ in range(4)]
    for c in range(CHUNKS):
        ref, at = atoms[c]
        hit = chunk == c
        for f in range(4):
            row = jnp.broadcast_to(ref[at, f : f + 1, :], (NEIGH, ATOMS))
            value = jnp.take_along_axis(row, lane, axis=1)
            found[f] = jnp.where(hit, value, found[f])
    d = [
        code_ref[1 + c].astype(F32) + (found[c] - jnp.broadcast_to(home_ref[home, c : c + 1, :], (NEIGH, ATOMS)))
        for c in range(3)
    ]
    r = jnp.sqrt(d[0] * d[0] + d[1] * d[1] + d[2] * d[2])
    ux, uy, uz = d[0] / r, d[1] / r, d[2] / r
    geo_ref[0] = r
    geo_ref[1] = ux
    geo_ref[2] = uy
    geo_ref[3] = uz
    spread_rows(yb_ref, angular_rows(ux, uy, uz))

    kind = lax.broadcasted_iota(jnp.int32, (8, ATOMS), 0).astype(F32)
    center_hot = jnp.where(jnp.broadcast_to(home_ref[home, 3:4, :], (8, ATOMS)) == kind, 1.0, 0.0)
    zero = jnp.zeros((8, ATOMS), F32)
    columns = []
    for k in range(NEIGH):
        bump, gap, inner, ratio = basis_parts(r[k : k + 1, :])
        other_hot = jnp.where(jnp.broadcast_to(found[3][k : k + 1, :], (8, ATOMS)) == kind, 1.0, 0.0)
        columns.append(jnp.concatenate([bump * (inner * inner), other_hot, center_hot, zero], axis=0).astype(BF16))
    for j in range(EDGES // TILE):
        span = slice(j * TILE, (j + 1) * TILE)
        per = TILE // ATOMS
        x = jnp.concatenate(columns[j * per : (j + 1) * per], axis=1)
        act, ds = silu_pair(jnp.dot(wcat_ref[...], x, preferred_element_type=F32))
        dsb_ref[:, span] = ds
        latent, ds = silu_pair(jnp.dot(mixt_ref[...], act.astype(BF16), preferred_element_type=F32))
        dsl_ref[:, span] = ds
        lat_ref[:, span] = latent
        env_ref[:, span] = jnp.dot(envt_ref[...], latent.astype(BF16), preferred_element_type=F32)
    for t in range(8):
        halves = []
        for h in range(2):
            rows = slice(t * 16 + h * 8, t * 16 + h * 8 + 8)
            env = [env_ref[rows, k * ATOMS : (k + 1) * ATOMS] for k in range(NEIGH)]
            field = []
            for m in range(9):
                terms = [env[k] if m == 0 else env[k] * yb_ref[m * NEIGH + k] for k in range(NEIGH)]
                while len(terms) > 1:
                    terms = [terms[i] + terms[i + 1] for i in range(0, len(terms), 2)]
                field.append(terms[0] * 0.125)
                v_ref[m, rows, :] = field[m]
            out = []
            for k in range(NEIGH):
                sums = [field[0], None, None]
                for m in range(1, 9):
                    term = field[m] * yb_ref[m * NEIGH + k]
                    sums[PIECE[m]] = term if sums[PIECE[m]] is None else sums[PIECE[m]] + term
                out.append(sums)
            halves.append(out)
        for k in range(NEIGH):
            for p in range(3):
                both = jnp.concatenate([halves[0][k][p], halves[1][k][p]], axis=0)
                inv_ref[p * ATOMS + t * 16 : p * ATOMS + t * 16 + 16, k * ATOMS : (k + 1) * ATOMS] = both.astype(BF16)
    mean = jnp.zeros((ATOMS, ATOMS), F32)
    for j in range(EDGES // TILE):
        span = slice(j * TILE, (j + 1) * TILE)
        update = jnp.dot(updt_ref[...], inv_ref[:, span], preferred_element_type=F32)
        edge, ds = silu_pair(lat_ref[:, span] + update)
        edge_ref[:, span] = edge
        dse_ref[:, span] = ds
        for i in range(TILE // ATOMS):
            mean = mean + edge[:, i * ATOMS : (i + 1) * ATOMS]
    table_ref[0] = (mean * 0.125).astype(BF16)


def second_kernel(parts, order, *refs):
    (
        onehot_ref, edge_ref, second_ref, secondt_ref, rocol_ref,
        energy_ref, grad_edge_ref, back_own_ref, back_other_ref, grad_ref,
    ) = refs[parts:]
    table = jnp.concatenate([refs[array][row] for array, row in order], axis=1)
    rocol = rocol_ref[...]
    total = jnp.zeros((ATOMS, ATOMS), F32)
    for j in range(EDGES // TILE):
        span = slice(j * TILE, (j + 1) * TILE)
        other = jnp.dot(table, onehot_ref[:, span], preferred_element_type=F32)
        edge = edge_ref[:, span]
        hidden, ds = silu_pair(jnp.dot(secondt_ref[...], (edge * other).astype(BF16), preferred_element_type=F32))
        for i in range(TILE // ATOMS):
            total = total + hidden[:, i * ATOMS : (i + 1) * ATOMS]
        grad_hidden = ds * jnp.concatenate([rocol] * (TILE // ATOMS), axis=1)
        grad_prod = jnp.dot(second_ref[...], grad_hidden.astype(BF16), preferred_element_type=F32)
        grad_prod = grad_prod.astype(BF16).astype(F32)
        grad_edge_ref[:, span] = grad_prod * other
        grad_ref[:, span] = (grad_prod * edge).astype(BF16)
    energy = jnp.sum(total * rocol, axis=0, keepdims=True)
    slots = energy_ref.shape[-1]
    for block in range(2):
        energy_ref[0, 0, block : block + 1, :] = energy[:, block * slots : (block + 1) * slots]
    grad = grad_ref[...]
    for c in range(CHUNKS):
        rows = slice(c * ATOMS, (c + 1) * ATOMS)
        back = lax.dot_general(
            grad, onehot_ref[rows, :], (((1,), (1,)), ((), ())), preferred_element_type=F32
        )
        ref = back_own_ref if c < 9 else back_other_ref
        ref[c % 9] = back.astype(BF16)


def backward_kernel(
    owned_ref, grad_edge_ref, dse_ref, dsl_ref, dsb_ref, env_ref, v_ref, geo_ref, onehot_ref,
    upd_ref, envw_ref, mix_ref, radial_ref,
    own_ref, other_ref, yb_ref, dinv_ref, denv_ref, dlat_ref, part_ref, force_ref,
):
    r, ux, uy, uz = (geo_ref[i] for i in range(4))
    angular = angular_rows(ux, uy, uz)
    spread_rows(yb_ref, angular)
    share = owned_ref[0] * 0.125
    for j in range(EDGES // TILE):
        span = slice(j * TILE, (j + 1) * TILE)
        d_edge = grad_edge_ref[:, span] + jnp.concatenate([share] * (TILE // ATOMS), axis=1)
        d_pre = d_edge * dse_ref[:, span]
        dlat_ref[:, span] = d_pre
        dinv_ref[:, span] = jnp.dot(upd_ref[...], d_pre.astype(BF16), preferred_element_type=F32).astype(BF16)
    part_ref[...] = jnp.zeros(part_ref.shape, F32)
    for t in range(8):
        wide = [
            [
                dinv_ref[p * ATOMS + t * 16 : p * ATOMS + t * 16 + 16, k * ATOMS : (k + 1) * ATOMS].astype(F32)
                for k in range(NEIGH)
            ]
            for p in range(3)
        ]
        halves = []
        for h in range(2):
            rows = slice(t * 16 + h * 8, t * 16 + h * 8 + 8)
            dinv = [[wide[p][k][h * 8 : h * 8 + 8] for k in range(NEIGH)] for p in range(3)]
            env = [env_ref[rows, k * ATOMS : (k + 1) * ATOMS] for k in range(NEIGH)]
            denv = [None] * NEIGH
            for m in range(9):
                down = dinv[PIECE[m]]
                terms = [down[k] if m == 0 else down[k] * yb_ref[m * NEIGH + k] for k in range(NEIGH)]
                while len(terms) > 1:
                    terms = [terms[i] + terms[i + 1] for i in range(0, len(terms), 2)]
                d_field = terms[0] * 0.125
                if m == 0:
                    denv = [d_field] * NEIGH
                    continue
                field = v_ref[m, rows, :]
                for k in range(NEIGH):
                    spot = m * NEIGH + k
                    part_ref[spot] = part_ref[spot] + (down[k] * field + env[k] * d_field)
                    denv[k] = denv[k] + d_field * yb_ref[spot]
            halves.append(denv)
        for k in range(NEIGH):
            both = jnp.concatenate([halves[0][k], halves[1][k]], axis=0)
            denv_ref[t * 16 : t * 16 + 16, k * ATOMS : (k + 1) * ATOMS] = both.astype(BF16)
    d_r_rows = []
    for j in range(EDGES // TILE):
        span = slice(j * TILE, (j + 1) * TILE)
        d_lat = jnp.dot(envw_ref[...], denv_ref[:, span], preferred_element_type=F32).astype(BF16).astype(F32)
        d_mix = (dlat_ref[:, span] + d_lat) * dsl_ref[:, span]
        d_act = jnp.dot(mix_ref[...], d_mix.astype(BF16), preferred_element_type=F32).astype(BF16).astype(F32)
        d_before = (d_act * dsb_ref[:, span]).astype(BF16)
        d_basis = jnp.dot(radial_ref[...], d_before, preferred_element_type=F32).astype(BF16).astype(F32)
        for i in range(TILE // ATOMS):
            k = j * (TILE // ATOMS) + i
            bump, gap, inner, ratio = basis_parts(r[k : k + 1, :])
            slope = bump * inner * (-2.0 * SHARPNESS * gap * inner - (4.0 / CUTOFF) * ratio)
            d_r_rows.append(jnp.sum(slope * d_basis[:, i * ATOMS : (i + 1) * ATOMS], axis=0, keepdims=True))
    d_r = jnp.concatenate(d_r_rows, axis=0)
    dy = [None]
    for m in range(1, 9):
        rows = [jnp.sum(part_ref[m * NEIGH + k], axis=0, keepdims=True) for k in range(NEIGH)]
        dy.append(jnp.concatenate(rows, axis=0))
    d_ux = dy[1] + ROOT3 * (uy * dy[4] + uz * dy[7] + ux * dy[8])
    d_uy = dy[2] + ROOT3 * (ux * dy[4] + uz * dy[5] - uy * dy[8])
    d_uz = dy[3] + ROOT3 * (uy * dy[5] + ux * dy[7]) + 3.0 * uz * dy[6]
    along = ux * d_ux + uy * d_uy + uz * d_uz
    inverse = 1.0 / r
    radial = d_r - along * inverse
    pull = [d_ux * inverse + ux * radial, d_uy * inverse + uy * radial, d_uz * inverse + uz * radial]
    high = [p.astype(BF16).astype(F32) for p in pull]
    low = [p - h for p, h in zip(pull, high)]
    zero = jnp.zeros((1, ATOMS), F32)
    for k in range(NEIGH):
        rows = [h[k : k + 1, :] for h in high] + [zero] * 5 + [q[k : k + 1, :] for q in low] + [zero] * 5
        force_ref[:, k * ATOMS : (k + 1) * ATOMS] = jnp.concatenate(rows, axis=0).astype(BF16)
    force = force_ref[...]
    center = jnp.concatenate([jnp.sum(p, axis=0, keepdims=True) for p in pull] + [zero] * 5, axis=0)
    for c in range(CHUNKS):
        rows = slice(c * ATOMS, (c + 1) * ATOMS)
        back = lax.dot_general(
            force, onehot_ref[rows, :], (((1,), (1,)), ((), ())), preferred_element_type=F32
        )
        moved = back[:8] + back[8:]
        if c == 8:
            moved = moved - center
        ref = own_ref if c < 9 else other_ref
        ref[c % 9] = moved


def finish_kernel(own_ref, out_ref):
    slots = out_ref.shape[-1] // 3
    for block in range(2):
        for c in range(3):
            out_ref[0, 0, block : block + 1, c * slots : (c + 1) * slots] = -own_ref[
                0, c : c + 1, block * slots : (block + 1) * slots
            ]


def call(kernel, outs, scratch=(), name=None, limit=24 << 20, place=pltpu.VMEM, cost=None):
    whole = pl.BlockSpec(memory_space=pltpu.VMEM)
    shapes = [jax.ShapeDtypeStruct(shape, kind) for shape, kind in outs]

    def run(*args):
        return pl.pallas_call(
            kernel,
            out_shape=shapes,
            in_specs=[pl.BlockSpec(memory_space=place)] * len(args),
            out_specs=[whole] * len(shapes),
            scratch_shapes=list(scratch),
            compiler_params=pltpu.CompilerParams(vmem_limit_bytes=limit),
            cost_estimate=cost,
            name=name,
        )(*args)

    return run


def on_device(
    positions, species, neighbors, center_table, neighbor_table, radial_weight, mix_weight,
    env_weight, update_weight, second_weight, readout,
):
    slots = species.shape[-1]
    edges = (ATOMS, EDGES)
    square = (ATOMS, ATOMS)
    readout = readout.reshape(1, ATOMS)

    def like(*arrays):
        return [pltpu.VMEM(array.shape, array.dtype) for array in arrays]

    halves = [positions, species]
    if is_paired():
        halves += [shifted(positions, "gz", 1), shifted(species, "gz", 1)]
    (packed,) = call(
        pack_kernel,
        [((len(halves) // 2, 8, ATOMS), F32)],
        name="pack",
        cost=pl.CostEstimate(flops=1 << 34, bytes_accessed=64 << 20, transcendentals=0),
    )(*halves)
    weights = (radial_weight, mix_weight, env_weight, update_weight, second_weight)
    code, onehot, wcat, mixt, envt, updt, secondt, rocol, radial, mix, envw, upd, second = call(
        functools.partial(prep_kernel, is_paired()),
        [
            ((4, NEIGH, ATOMS), jnp.int32), ((CHUNKS * ATOMS, EDGES), BF16), ((ATOMS, 32), BF16), (square, BF16),
            (square, BF16), ((ATOMS, 3 * ATOMS), BF16), (square, BF16), (square, F32),
        ]
        + [(weight.shape, weight.dtype) for weight in weights],
        like(neighbors, center_table, neighbor_table, readout)
        + [pltpu.VMEM(square, F32), pltpu.SemaphoreType.DMA((9,))],
        name="prep",
        place=pltpu.HBM,
        cost=pl.CostEstimate(flops=1 << 28, bytes_accessed=8 << 20, transcendentals=0),
    )(
        neighbors, center_table, neighbor_table, radial_weight, mix_weight, env_weight, update_weight,
        second_weight, readout,
    )
    tables, order = gather_halo(packed, packed)
    table, edge, dsb, dsl, dse, env, field, geo = call(
        functools.partial(forward_kernel, len(tables), order),
        [
            ((1,) + square, BF16), (edges, F32), (edges, F32), (edges, F32), (edges, F32), (edges, F32),
            ((9,) + square, F32), ((4, NEIGH, ATOMS), F32),
        ],
        [pltpu.VMEM((72, 8, ATOMS), F32), pltpu.VMEM((3 * ATOMS, EDGES), BF16), pltpu.VMEM(edges, F32)],
        name="forward",
    )(*tables, code, wcat, mixt, envt, updt)
    tables, order = gather_halo(table)
    energy, grad_edge, back_own, back_other = call(
        functools.partial(second_kernel, len(tables), order),
        [((1, 1, 2, slots), F32), (edges, F32), ((9,) + square, BF16), ((9,) + square, BF16)],
        [pltpu.VMEM(edges, BF16)],
        name="second",
    )(*tables, onehot, edge, second, secondt, rocol)
    owned = reduce_halo(back_own, back_other)
    own, other = call(
        backward_kernel,
        [((9, 8, ATOMS), F32), ((9, 8, ATOMS), F32)],
        [
            pltpu.VMEM((72, 8, ATOMS), F32), pltpu.VMEM((3 * ATOMS, EDGES), BF16), pltpu.VMEM(edges, BF16),
            pltpu.VMEM(edges, F32), pltpu.VMEM((72, 8, ATOMS), F32), pltpu.VMEM((16, EDGES), BF16),
        ],
        name="backward",
    )(owned, grad_edge, dse, dsl, dsb, env, field, geo, onehot, upd, envw, mix, radial)
    motion = reduce_halo(own, other)
    (forces,) = call(finish_kernel, [((1, 1, 2, 3 * slots), F32)], name="finish")(motion)
    return energy, forces


def solution(mesh):
    split = P("gx", "gy", "gz", None)
    return jax.shard_map(
        on_device,
        mesh=mesh,
        in_specs=(split, split, split) + (P(),) * 8,
        out_specs=(split, split),
        check_vma=False,
    )
```

```python
import functools
import math

import jax
import jax.numpy as jnp
from jax import lax
from jax.experimental import pallas as pl
from jax.experimental.pallas import tpu as pltpu
from jax.sharding import PartitionSpec as P

NEIGH = 8
ATOMS = 128
EDGES = NEIGH * ATOMS
CHUNKS = 18
CUTOFF = 4.0
SHARPNESS = 2.0
ROOT3 = math.sqrt(3.0)
F32 = jnp.float32
BF16 = jnp.bfloat16
TILE = 256


RING = (0, 1, 3, 2)
ROUTES = (((1, 0), (0, 2), (1, 2), (2, 1)), ((2, 0), (0, 1), (1, 1), (2, 2)))
EVERY = ("gx", "gy", "gz")


def is_direct():
    return tuple(lax.axis_size(axis) for axis in EVERY) == (4, 4, 2)


def shifted(value, axis, step):
    count = lax.axis_size(axis)
    return lax.ppermute(value, axis, [(i, (i + step) % count) for i in range(count)])


def partner(index, way):
    if way == 0:
        return index
    if way == 1:
        return index ^ 1
    return (index + 2 * (index & 1) - 1) & 3


def number(x, y, core):
    return (x * 4 + y) * 2 + core


def permuted(value, target):
    pairs = []
    for x in range(4):
        for y in range(4):
            for core in range(2):
                to_x, to_y = target(x, y, core)
                pairs.append((number(RING[x], RING[y], core), number(RING[to_x], RING[to_y], core)))
    return lax.ppermute(value, EVERY, pairs)


def swapped(value, slot):
    return permuted(
        value, lambda x, y, core: (partner(x, ROUTES[core][slot][0]), partner(y, ROUTES[core][slot][1]))
    )


def to_workers(value):
    return permuted(value, lambda x, y, core: (RING[x], RING[y]))


def gather_halo(chunk):
    if is_direct():
        both = jnp.concatenate([chunk, shifted(chunk, "gz", 1)], axis=0)
        direct = [swapped(both, slot) for slot in range(4)]
        relayed = shifted(jnp.concatenate(direct, axis=0), "gz", 1)
        near = [(slot, row) for slot in range(4) for row in range(2)] + [(4, 0)]
        far = [(5, row) for row in range(8)] + [(4, 1)]
        return direct + [both, relayed], near + far
    for axis in ("gx", "gy"):
        lower = shifted(chunk, axis, 1)
        upper = shifted(chunk, axis, -1)
        chunk = jnp.concatenate([lower, upper, chunk], axis=0)
    order = [(array, row) for array in range(2) for row in range(9)]
    if lax.axis_size("gz") == 2:
        return [chunk, shifted(chunk, "gz", 1)], order
    half = chunk.shape[-1] // 2
    above = shifted(chunk[..., :half], "gz", -1)
    below = shifted(chunk[..., half:], "gz", 1)
    return [chunk, jnp.concatenate([above, below], axis=-1)], order


def reduce_halo(own, other):
    kind = own.dtype
    if is_direct():
        own = own.astype(F32) + shifted(other, "gz", 1).astype(F32)
        came = [swapped(own[2 * slot : 2 * slot + 2].astype(kind), slot).astype(F32) for slot in range(4)]
        both = came[0] + came[1] + came[2] + came[3]
        return own[8:] + both[:1] + shifted(both[1:], "gz", 1)
    if lax.axis_size("gz") == 2:
        back = shifted(other, "gz", 1)
    else:
        half = other.shape[-1] // 2
        first = shifted(other[..., :half], "gz", 1)
        second = shifted(other[..., half:], "gz", -1)
        back = jnp.concatenate([first, second], axis=-1)
    own = own.astype(F32) + back.astype(F32)
    for axis, size in (("gy", 3), ("gx", 1)):
        lower = shifted(own[:size].astype(kind), axis, -1)
        upper = shifted(own[size : 2 * size].astype(kind), axis, 1)
        own = own[2 * size :] + lower.astype(F32) + upper.astype(F32)
    return own


def ring_at(index):
    return index ^ (index >> 1)


def column_here():
    return ring_at(lax.axis_index("gx")), ring_at(lax.axis_index("gy")), lax.axis_index("gz")


def owner_at(step_x, step_y, outside):
    x, y, core = column_here()
    return number((x + step_x) & 3, (y + step_y) & 3, core ^ outside)


def owner_of_chunk(c):
    x, y, core = column_here()
    outside = 0
    if c % 9 == 8:
        return number(x, y, core ^ (c // 9))
    relayed = c // 9
    slot, row = (c % 9) // 2, (c % 9) % 2
    outside = row ^ relayed
    spots = [
        number(partner(x, ROUTES[mate][slot][0]), partner(y, ROUTES[mate][slot][1]), core ^ outside)
        for mate in range(2)
    ]
    return jnp.where((core ^ relayed) == 0, spots[0], spots[1])


def place_column(step_x, step_y, outside, direct):
    if not direct:
        place_x = jnp.where(step_x == 0, 2, jnp.where(step_x < 0, 0, 1))
        place_y = jnp.where(step_y == 0, 2, jnp.where(step_y < 0, 0, 1))
        return outside * 9 + place_y * 3 + place_x
    x, y, core = column_here()
    way_x = jnp.where(step_x == 0, 0, jnp.where(step_x == 1 - 2 * (x & 1), 1, 2))
    way_y = jnp.where(step_y == 0, 0, jnp.where(step_y == 1 - 2 * (y & 1), 1, 2))
    way = way_x * 3 + way_y
    chunk = 8 + 9 * outside
    for mate in range(2):
        mine = core == mate
        for slot, (to_x, to_y) in enumerate(ROUTES[mate]):
            spot = jnp.where(mine, 2 * slot + outside, 9 + 2 * slot + 1 - outside)
            chunk = jnp.where(way == to_x * 3 + to_y, spot, chunk)
    return chunk


def decode(code, slots):
    offset = code >> 6
    slot = code & 63
    step_x = jnp.where(offset >= 18, 1, jnp.where(offset >= 9, 0, -1))
    rest = offset - 9 * (step_x + 1)
    step_y = jnp.where(rest >= 6, 1, jnp.where(rest >= 3, 0, -1))
    step_z = rest - 3 * (step_y + 1) - 1
    block = lax.broadcasted_iota(jnp.int32, (NEIGH, ATOMS), 1) // slots
    level = block + step_z
    outside = jnp.where((level < 0) | (level > 1), 1, 0)
    return step_x, step_y, step_z, outside, (level & 1) * slots + slot


def blank_kernel(out_ref):
    out_ref[...] = jnp.zeros(out_ref.shape, F32)


def pack_kernel(blank_ref, pos_ref, spec_ref, out_ref):
    slots = spec_ref.shape[-1]
    for chunk in range(out_ref.shape[0]):
        for block in range(2):
            lanes = slice(block * slots, (block + 1) * slots)
            for c in range(3):
                out_ref[chunk, c : c + 1, lanes] = pos_ref[0, 0, block : block + 1, c * slots : (c + 1) * slots]
            out_ref[chunk, 3:4, lanes] = spec_ref[0, 0, block : block + 1, :].astype(F32)


def onehot_kernel(direct, code_ref, second_ref, readout_ref, onehot_ref, secondt_ref, rocol_ref):
    step_x, step_y, step_z, outside, lane = decode(code_ref[...], ATOMS // 2)
    target = place_column(step_x, step_y, outside, direct) * ATOMS + lane
    secondt_ref[...] = second_ref[...].astype(F32).T.astype(BF16)
    rocol_ref[...] = jnp.broadcast_to(readout_ref[...], (ATOMS, ATOMS)).T
    atom = lax.broadcasted_iota(jnp.int32, (ATOMS, ATOMS), 0)
    for k in range(NEIGH):
        aim = jnp.broadcast_to(target[k : k + 1, :], (ATOMS, ATOMS)) - atom

        def fill(c, carry, k=k, aim=aim):
            rows = pl.ds(pl.multiple_of(c * ATOMS, ATOMS), ATOMS)
            hit = jnp.where(aim == c * ATOMS, 1.0, 0.0)
            onehot_ref[rows, k * ATOMS : (k + 1) * ATOMS] = hit.astype(BF16)
            return carry

        lax.fori_loop(0, CHUNKS, fill, 0)


def listed_codes(nb_ref):
    width = nb_ref.shape[-1]
    slots = width // NEIGH
    lane = lax.broadcasted_iota(jnp.int32, (NEIGH, width), 1)
    row = lax.broadcasted_iota(jnp.int32, (NEIGH, width), 0)
    mine = (lane & (NEIGH - 1)) == row
    spot = lax.broadcasted_iota(jnp.int32, (width, ATOMS), 0) // NEIGH
    column = lax.broadcasted_iota(jnp.int32, (width, ATOMS), 1)
    total = jnp.zeros((NEIGH, ATOMS), F32)
    for block in range(2):
        listed = jnp.broadcast_to(nb_ref[0, 0, block : block + 1, :], (NEIGH, width))
        listed = jnp.where(mine, listed, 0)
        high = (listed >> 4).astype(F32).astype(BF16)
        low = (listed & 15).astype(F32).astype(BF16)
        pick = jnp.where(spot + block * slots == column, 1.0, 0.0).astype(BF16)
        total = total + 16.0 * jnp.dot(high, pick, preferred_element_type=F32)
        total = total + jnp.dot(low, pick, preferred_element_type=F32)
    return (total + 0.5).astype(jnp.int32)


def sigmoid(v):
    return 0.5 * jnp.tanh(0.5 * v) + 0.5


def silu_pair(v):
    s = sigmoid(v)
    value = v * s
    return value, s + value * (1.0 - s)


def angular_rows(ux, uy, uz):
    return [
        None, ux, uy, uz, ROOT3 * ux * uy, ROOT3 * uy * uz, 0.5 * (3.0 * uz * uz - 1.0),
        ROOT3 * ux * uz, 0.5 * ROOT3 * (ux * ux - uy * uy),
    ]


def spread_rows(yb_ref, angular):
    for m in range(1, 9):
        for k in range(NEIGH):
            yb_ref[m * NEIGH + k] = jnp.broadcast_to(angular[m][k : k + 1, :], (8, ATOMS))


def basis_parts(r_row):
    row = lax.broadcasted_iota(jnp.int32, (8, ATOMS), 0).astype(F32)
    centers = CUTOFF * (row + 0.5) / 8.0
    r = jnp.broadcast_to(r_row, (8, ATOMS))
    ratio = r * (1.0 / CUTOFF)
    inner = 1.0 - ratio * ratio
    gap = r - centers
    return jnp.exp(-SHARPNESS * gap * gap), gap, inner, ratio


PIECE = (0, 1, 1, 1, 2, 2, 2, 2, 2)


def forward_kernel(parts, direct, *refs):
    tables = refs[:parts]
    (
        nb_ref, center_ref, neighbor_ref, radial_ref, mix_ref, envw_ref, upd_ref,
        table_ref, code_ref, edge_ref, dsb_ref, dsl_ref, dse_ref, env_ref, v_ref, geo_ref,
        yb_ref, inv_ref, lat_ref, pad_ref,
    ) = refs[parts:]
    pad_ref[...] = jnp.zeros(pad_ref.shape, F32)
    pad_ref[0:8, :] = radial_ref[...].astype(F32)
    pad_ref[8 : 8 + neighbor_ref.shape[0], :] = neighbor_ref[...].astype(F32)
    pad_ref[16 : 16 + center_ref.shape[0], :] = center_ref[...].astype(F32)
    wcat = pad_ref[...].T[:, :32].astype(BF16)
    mixt = mix_ref[...].astype(F32).T.astype(BF16)
    envt = envw_ref[...].astype(F32).T.astype(BF16)
    updt = [upd_ref[p * ATOMS : (p + 1) * ATOMS, :].astype(F32).T.astype(BF16) for p in range(3)]
    updt = jnp.concatenate(updt, axis=1)

    code = listed_codes(nb_ref)
    code_ref[...] = code
    step_x, step_y, step_z, outside, lane = decode(code, ATOMS // 2)
    spot = outside * 9 + step_y * 3 + step_x + 4

    def chunk_at(far, dx, dy):
        if direct:
            return tables[0][owner_at(dx, dy, far)]
        return tables[far][(0, 2, 1)[dy + 1] * 3 + (0, 2, 1)[dx + 1]]

    found = [jnp.zeros((NEIGH, ATOMS), F32) for _ in range(4)]
    for far in range(2):
        for dy in (-1, 0, 1):
            for dx in (-1, 0, 1):
                hit = spot == far * 9 + dy * 3 + dx + 4
                rows = chunk_at(far, dx, dy)
                for f in range(4):
                    row = jnp.broadcast_to(rows[f : f + 1, :], (NEIGH, ATOMS))
                    found[f] = jnp.where(hit, jnp.take_along_axis(row, lane, axis=1), found[f])
    home = chunk_at(0, 0, 0)
    d = [
        step.astype(F32) + (found[c] - jnp.broadcast_to(home[c : c + 1, :], (NEIGH, ATOMS)))
        for c, step in enumerate((step_x, step_y, step_z))
    ]
    r = jnp.sqrt(d[0] * d[0] + d[1] * d[1] + d[2] * d[2])
    ux, uy, uz = d[0] / r, d[1] / r, d[2] / r
    geo_ref[0] = r
    geo_ref[1] = ux
    geo_ref[2] = uy
    geo_ref[3] = uz
    spread_rows(yb_ref, angular_rows(ux, uy, uz))

    kind = lax.broadcasted_iota(jnp.int32, (8, ATOMS), 0).astype(F32)
    center_hot = jnp.where(jnp.broadcast_to(home[3:4, :], (8, ATOMS)) == kind, 1.0, 0.0)
    zero = jnp.zeros((8, ATOMS), F32)
    columns = []
    for k in range(NEIGH):
        bump, gap, inner, ratio = basis_parts(r[k : k + 1, :])
        other_hot = jnp.where(jnp.broadcast_to(found[3][k : k + 1, :], (8, ATOMS)) == kind, 1.0, 0.0)
        columns.append(jnp.concatenate([bump * (inner * inner), other_hot, center_hot, zero], axis=0).astype(BF16))
    for j in range(EDGES // TILE):
        span = slice(j * TILE, (j + 1) * TILE)
        per = TILE // ATOMS
        x = jnp.concatenate(columns[j * per : (j + 1) * per], axis=1)
        act, ds = silu_pair(jnp.dot(wcat, x, preferred_element_type=F32))
        dsb_ref[:, span] = ds
        latent, ds = silu_pair(jnp.dot(mixt, act.astype(BF16), preferred_element_type=F32))
        dsl_ref[:, span] = ds
        lat_ref[:, span] = latent
        env_ref[:, span] = jnp.dot(envt, latent.astype(BF16), preferred_element_type=F32)
    for t in range(8):
        halves = []
        for h in range(2):
            rows = slice(t * 16 + h * 8, t * 16 + h * 8 + 8)
            env = [env_ref[rows, k * ATOMS : (k + 1) * ATOMS] for k in range(NEIGH)]
            field = []
            for m in range(9):
                terms = [env[k] if m == 0 else env[k] * yb_ref[m * NEIGH + k] for k in range(NEIGH)]
                while len(terms) > 1:
                    terms = [terms[i] + terms[i + 1] for i in range(0, len(terms), 2)]
                field.append(terms[0] * 0.125)
                v_ref[m, rows, :] = field[m]
            out = []
            for k in range(NEIGH):
                sums = [field[0], None, None]
                for m in range(1, 9):
                    term = field[m] * yb_ref[m * NEIGH + k]
                    sums[PIECE[m]] = term if sums[PIECE[m]] is None else sums[PIECE[m]] + term
                out.append(sums)
            halves.append(out)
        for k in range(NEIGH):
            for p in range(3):
                both = jnp.concatenate([halves[0][k][p], halves[1][k][p]], axis=0)
                inv_ref[p * ATOMS + t * 16 : p * ATOMS + t * 16 + 16, k * ATOMS : (k + 1) * ATOMS] = both.astype(BF16)
    mean = jnp.zeros((ATOMS, ATOMS), F32)
    for j in range(EDGES // TILE):
        span = slice(j * TILE, (j + 1) * TILE)
        update = jnp.dot(updt, inv_ref[:, span], preferred_element_type=F32)
        edge, ds = silu_pair(lat_ref[:, span] + update)
        edge_ref[:, span] = edge
        dse_ref[:, span] = ds
        for i in range(TILE // ATOMS):
            mean = mean + edge[:, i * ATOMS : (i + 1) * ATOMS]
    table_ref[0] = (mean * 0.125).astype(BF16)


def second_kernel(parts, order, *refs):
    (
        onehot_ref, edge_ref, second_ref, secondt_ref, rocol_ref,
        energy_ref, grad_edge_ref, back_own_ref, back_other_ref, grad_ref,
    ) = refs[parts:]
    table = jnp.concatenate([refs[array][row] for array, row in order], axis=1)
    rocol = rocol_ref[...]
    total = jnp.zeros((ATOMS, ATOMS), F32)
    for j in range(EDGES // TILE):
        span = slice(j * TILE, (j + 1) * TILE)
        other = jnp.dot(table, onehot_ref[:, span], preferred_element_type=F32)
        edge = edge_ref[:, span]
        hidden, ds = silu_pair(jnp.dot(secondt_ref[...], (edge * other).astype(BF16), preferred_element_type=F32))
        for i in range(TILE // ATOMS):
            total = total + hidden[:, i * ATOMS : (i + 1) * ATOMS]
        grad_hidden = ds * jnp.concatenate([rocol] * (TILE // ATOMS), axis=1)
        grad_prod = jnp.dot(second_ref[...], grad_hidden.astype(BF16), preferred_element_type=F32)
        grad_prod = grad_prod.astype(BF16).astype(F32)
        grad_edge_ref[:, span] = grad_prod * other
        grad_ref[:, span] = (grad_prod * edge).astype(BF16)
    energy = jnp.sum(total * rocol, axis=0, keepdims=True)
    energy_ref[...] = energy
    grad = grad_ref[...]
    for c in range(CHUNKS):
        rows = slice(c * ATOMS, (c + 1) * ATOMS)
        back = lax.dot_general(
            grad, onehot_ref[rows, :], (((1,), (1,)), ((), ())), preferred_element_type=F32
        )
        ref = back_own_ref if c < 9 else back_other_ref
        ref[c % 9] = back.astype(BF16)


def backward_kernel(
    direct, owned_ref, energy_ref, grad_edge_ref, dse_ref, dsl_ref, dsb_ref, env_ref, v_ref, geo_ref, onehot_ref,
    upd_ref, envw_ref, mix_ref, radial_ref, *refs,
):
    outs = refs[: 1 if direct else 2]
    yb_ref, dinv_ref, denv_ref, dlat_ref, part_ref, force_ref = refs[len(outs) :]
    r, ux, uy, uz = (geo_ref[i] for i in range(4))
    angular = angular_rows(ux, uy, uz)
    spread_rows(yb_ref, angular)
    share = owned_ref[0] * 0.125
    for j in range(EDGES // TILE):
        span = slice(j * TILE, (j + 1) * TILE)
        d_edge = grad_edge_ref[:, span] + jnp.concatenate([share] * (TILE // ATOMS), axis=1)
        d_pre = d_edge * dse_ref[:, span]
        dlat_ref[:, span] = d_pre
        dinv_ref[:, span] = jnp.dot(upd_ref[...], d_pre.astype(BF16), preferred_element_type=F32).astype(BF16)
    part_ref[...] = jnp.zeros(part_ref.shape, F32)
    for t in range(8):
        wide = [
            [
                dinv_ref[p * ATOMS + t * 16 : p * ATOMS + t * 16 + 16, k * ATOMS : (k + 1) * ATOMS].astype(F32)
                for k in range(NEIGH)
            ]
            for p in range(3)
        ]
        halves = []
        for h in range(2):
            rows = slice(t * 16 + h * 8, t * 16 + h * 8 + 8)
            dinv = [[wide[p][k][h * 8 : h * 8 + 8] for k in range(NEIGH)] for p in range(3)]
            env = [env_ref[rows, k * ATOMS : (k + 1) * ATOMS] for k in range(NEIGH)]
            denv = [None] * NEIGH
            for m in range(9):
                down = dinv[PIECE[m]]
                terms = [down[k] if m == 0 else down[k] * yb_ref[m * NEIGH + k] for k in range(NEIGH)]
                while len(terms) > 1:
                    terms = [terms[i] + terms[i + 1] for i in range(0, len(terms), 2)]
                d_field = terms[0] * 0.125
                if m == 0:
                    denv = [d_field] * NEIGH
                    continue
                field = v_ref[m, rows, :]
                for k in range(NEIGH):
                    spot = m * NEIGH + k
                    part_ref[spot] = part_ref[spot] + (down[k] * field + env[k] * d_field)
                    denv[k] = denv[k] + d_field * yb_ref[spot]
            halves.append(denv)
        for k in range(NEIGH):
            both = jnp.concatenate([halves[0][k], halves[1][k]], axis=0)
            denv_ref[t * 16 : t * 16 + 16, k * ATOMS : (k + 1) * ATOMS] = both.astype(BF16)
    d_r_rows = []
    for j in range(EDGES // TILE):
        span = slice(j * TILE, (j + 1) * TILE)
        d_lat = jnp.dot(envw_ref[...], denv_ref[:, span], preferred_element_type=F32).astype(BF16).astype(F32)
        d_mix = (dlat_ref[:, span] + d_lat) * dsl_ref[:, span]
        d_act = jnp.dot(mix_ref[...], d_mix.astype(BF16), preferred_element_type=F32).astype(BF16).astype(F32)
        d_before = (d_act * dsb_ref[:, span]).astype(BF16)
        d_basis = jnp.dot(radial_ref[...], d_before, preferred_element_type=F32).astype(BF16).astype(F32)
        for i in range(TILE // ATOMS):
            k = j * (TILE // ATOMS) + i
            bump, gap, inner, ratio = basis_parts(r[k : k + 1, :])
            slope = bump * inner * (-2.0 * SHARPNESS * gap * inner - (4.0 / CUTOFF) * ratio)
            d_r_rows.append(jnp.sum(slope * d_basis[:, i * ATOMS : (i + 1) * ATOMS], axis=0, keepdims=True))
    d_r = jnp.concatenate(d_r_rows, axis=0)
    dy = [None]
    for m in range(1, 9):
        rows = [jnp.sum(part_ref[m * NEIGH + k], axis=0, keepdims=True) for k in range(NEIGH)]
        dy.append(jnp.concatenate(rows, axis=0))
    d_ux = dy[1] + ROOT3 * (uy * dy[4] + uz * dy[7] + ux * dy[8])
    d_uy = dy[2] + ROOT3 * (ux * dy[4] + uz * dy[5] - uy * dy[8])
    d_uz = dy[3] + ROOT3 * (uy * dy[5] + ux * dy[7]) + 3.0 * uz * dy[6]
    along = ux * d_ux + uy * d_uy + uz * d_uz
    inverse = 1.0 / r
    radial = d_r - along * inverse
    pull = [d_ux * inverse + ux * radial, d_uy * inverse + uy * radial, d_uz * inverse + uz * radial]
    high = [p.astype(BF16).astype(F32) for p in pull]
    low = [p - h for p, h in zip(pull, high)]
    zero = jnp.zeros((1, ATOMS), F32)
    for k in range(NEIGH):
        rows = [h[k : k + 1, :] for h in high] + [zero] * 5 + [q[k : k + 1, :] for q in low] + [zero] * 5
        force_ref[:, k * ATOMS : (k + 1) * ATOMS] = jnp.concatenate(rows, axis=0).astype(BF16)
    force = force_ref[...]
    center = jnp.concatenate([jnp.sum(p, axis=0, keepdims=True) for p in pull] + [-energy_ref[...]], axis=0)
    if direct:
        outs[0][...] = jnp.zeros(outs[0].shape, F32)
    for c in range(CHUNKS):
        rows = slice(c * ATOMS, (c + 1) * ATOMS)
        back = lax.dot_general(
            force, onehot_ref[rows, :], (((1,), (1,)), ((), ())), preferred_element_type=F32
        )
        moved = back[:4] + back[8:12]
        if c == 8:
            moved = moved - center
        if direct:
            outs[0][owner_of_chunk(c)] = moved
        else:
            outs[c // 9][c % 9] = moved


def finish_kernel(moved_ref, energy_ref, out_ref):
    slots = energy_ref.shape[-1]
    total = jnp.sum(moved_ref[...], axis=0)
    for block in range(2):
        lanes = slice(block * slots, (block + 1) * slots)
        energy_ref[0, 0, block : block + 1, :] = total[3:4, lanes]
        for c in range(3):
            out_ref[0, 0, block : block + 1, c * slots : (c + 1) * slots] = -total[c : c + 1, lanes]


def call(kernel, outs, scratch=(), name=None, limit=24 << 20, place=pltpu.VMEM, cost=None):
    whole = pl.BlockSpec(memory_space=pltpu.VMEM)
    shapes = [jax.ShapeDtypeStruct(shape, kind) for shape, kind in outs]

    def run(*args):
        return pl.pallas_call(
            kernel,
            out_shape=shapes,
            in_specs=[pl.BlockSpec(memory_space=place)] * len(args),
            out_specs=[whole] * len(shapes),
            scratch_shapes=list(scratch),
            compiler_params=pltpu.CompilerParams(vmem_limit_bytes=limit),
            cost_estimate=cost,
            name=name,
        )(*args)

    return run


def on_device(
    positions, species, neighbors, center_table, neighbor_table, radial_weight, mix_weight,
    env_weight, update_weight, second_weight, readout,
):
    slots = species.shape[-1]
    edges = (ATOMS, EDGES)
    square = (ATOMS, ATOMS)
    readout = readout.reshape(1, ATOMS)
    direct = is_direct()
    devices = 32 if direct else 1
    (blank,) = call(
        blank_kernel,
        [((8, ATOMS), F32)],
        name="blank",
        cost=pl.CostEstimate(flops=1 << 34, bytes_accessed=64 << 20, transcendentals=0),
    )()
    (packed,) = call(pack_kernel, [((devices, 4, ATOMS), F32)], name="pack")(blank, positions, species)
    if direct:
        listed = to_workers(neighbors)
        tables = [lax.all_to_all(packed, EVERY, 0, 0, tiled=True)]
    else:
        listed = neighbors
        tables, order = gather_halo(packed)
    table, code, edge, dsb, dsl, dse, env, field, geo = call(
        functools.partial(forward_kernel, len(tables), direct),
        [
            ((1,) + square, BF16), ((NEIGH, ATOMS), jnp.int32), (edges, F32), (edges, F32), (edges, F32),
            (edges, F32), (edges, F32), ((9,) + square, F32), ((4, NEIGH, ATOMS), F32),
        ],
        [
            pltpu.VMEM((72, 8, ATOMS), F32), pltpu.VMEM((3 * ATOMS, EDGES), BF16), pltpu.VMEM(edges, F32),
            pltpu.VMEM(square, F32),
        ],
        name="forward",
    )(*tables, listed, center_table, neighbor_table, radial_weight, mix_weight, env_weight, update_weight)
    onehot, secondt, rocol = call(
        functools.partial(onehot_kernel, direct),
        [((CHUNKS * ATOMS, EDGES), BF16), (square, BF16), (square, F32)],
        name="onehot",
        cost=pl.CostEstimate(flops=1 << 30, bytes_accessed=8 << 20, transcendentals=0),
    )(code, second_weight, readout)
    tables, order = gather_halo(table)
    energy, grad_edge, back_own, back_other = call(
        functools.partial(second_kernel, len(tables), order),
        [((1, ATOMS), F32), (edges, F32), ((9,) + square, BF16), ((9,) + square, BF16)],
        [pltpu.VMEM(edges, BF16)],
        name="second",
    )(*tables, onehot, edge, second_weight, secondt, rocol)
    owned = reduce_halo(back_own, back_other)
    moved = call(
        functools.partial(backward_kernel, direct),
        [((devices, 4, ATOMS), F32)] if direct else [((9, 4, ATOMS), F32)] * 2,
        [
            pltpu.VMEM((72, 8, ATOMS), F32), pltpu.VMEM((3 * ATOMS, EDGES), BF16), pltpu.VMEM(edges, BF16),
            pltpu.VMEM(edges, F32), pltpu.VMEM((72, 8, ATOMS), F32), pltpu.VMEM((16, EDGES), BF16),
        ],
        name="backward",
    )(
        owned, energy, grad_edge, dse, dsl, dsb, env, field, geo, onehot, update_weight, env_weight, mix_weight,
        radial_weight,
    )
    moved = lax.all_to_all(moved[0], EVERY, 0, 0, tiled=True) if direct else reduce_halo(*moved)
    return call(finish_kernel, [((1, 1, 2, slots), F32), ((1, 1, 2, 3 * slots), F32)], name="finish")(moved)


def solution(mesh):
    split = P("gx", "gy", "gz", None)
    return jax.shard_map(
        on_device,
        mesh=mesh,
        in_specs=(split, split, split) + (P(),) * 8,
        out_specs=(split, split),
        check_vma=False,
    )
```

```python
import functools
import math

import jax
import jax.numpy as jnp
from jax import lax
from jax.experimental import pallas as pl
from jax.experimental.pallas import tpu as pltpu
from jax.sharding import PartitionSpec as P

NEIGH = 8
ATOMS = 128
EDGES = NEIGH * ATOMS
CHUNKS = 18
CUTOFF = 4.0
SHARPNESS = 2.0
ROOT3 = math.sqrt(3.0)
F32 = jnp.float32
BF16 = jnp.bfloat16
TILE = 256


RING = (0, 1, 3, 2)
ROUTES = (((1, 0), (0, 2), (1, 2), (2, 1)), ((2, 0), (0, 1), (1, 1), (2, 2)))
EVERY = ("gx", "gy", "gz")


def is_direct():
    return tuple(lax.axis_size(axis) for axis in EVERY) == (4, 4, 2)


def shifted(value, axis, step):
    count = lax.axis_size(axis)
    return lax.ppermute(value, axis, [(i, (i + step) % count) for i in range(count)])


def partner(index, way):
    if way == 0:
        return index
    if way == 1:
        return index ^ 1
    return (index + 2 * (index & 1) - 1) & 3


def number(x, y, core):
    return (x * 4 + y) * 2 + core


def swapped(value, slot):
    pairs = []
    for x in range(4):
        for y in range(4):
            for core in range(2):
                way_x, way_y = ROUTES[core][slot]
                to_x, to_y = partner(x, way_x), partner(y, way_y)
                pairs.append((number(RING[x], RING[y], core), number(RING[to_x], RING[to_y], core)))
    return lax.ppermute(value, EVERY, pairs)


def gather_halo(chunk):
    if is_direct():
        both = jnp.concatenate([chunk, shifted(chunk, "gz", 1)], axis=0)
        direct = [swapped(both, slot) for slot in range(4)]
        relayed = shifted(jnp.concatenate(direct, axis=0), "gz", 1)
        near = [(slot, row) for slot in range(4) for row in range(2)] + [(4, 0)]
        far = [(5, row) for row in range(8)] + [(4, 1)]
        return direct + [both, relayed], near + far
    for axis in ("gx", "gy"):
        lower = shifted(chunk, axis, 1)
        upper = shifted(chunk, axis, -1)
        chunk = jnp.concatenate([lower, upper, chunk], axis=0)
    order = [(array, row) for array in range(2) for row in range(9)]
    if lax.axis_size("gz") == 2:
        return [chunk, shifted(chunk, "gz", 1)], order
    half = chunk.shape[-1] // 2
    above = shifted(chunk[..., :half], "gz", -1)
    below = shifted(chunk[..., half:], "gz", 1)
    return [chunk, jnp.concatenate([above, below], axis=-1)], order


def reduce_halo(own, other):
    kind = own.dtype
    if is_direct():
        own = own.astype(F32) + shifted(other, "gz", 1).astype(F32)
        came = [swapped(own[2 * slot : 2 * slot + 2].astype(kind), slot).astype(F32) for slot in range(4)]
        both = came[0] + came[1] + came[2] + came[3]
        return own[8:] + both[:1] + shifted(both[1:], "gz", 1)
    if lax.axis_size("gz") == 2:
        back = shifted(other, "gz", 1)
    else:
        half = other.shape[-1] // 2
        first = shifted(other[..., :half], "gz", 1)
        second = shifted(other[..., half:], "gz", -1)
        back = jnp.concatenate([first, second], axis=-1)
    own = own.astype(F32) + back.astype(F32)
    for axis, size in (("gy", 3), ("gx", 1)):
        lower = shifted(own[:size].astype(kind), axis, -1)
        upper = shifted(own[size : 2 * size].astype(kind), axis, 1)
        own = own[2 * size :] + lower.astype(F32) + upper.astype(F32)
    return own


def ring_at(index):
    return index ^ (index >> 1)


def column_here():
    return ring_at(lax.axis_index("gx")), ring_at(lax.axis_index("gy")), lax.axis_index("gz")


def owner_at(step_x, step_y, outside):
    x, y, core = column_here()
    return number((x + step_x) & 3, (y + step_y) & 3, core ^ outside)


def owner_of_chunk(c):
    x, y, core = column_here()
    outside = 0
    if c % 9 == 8:
        return number(x, y, core ^ (c // 9))
    relayed = c // 9
    slot, row = (c % 9) // 2, (c % 9) % 2
    outside = row ^ relayed
    spots = [
        number(partner(x, ROUTES[mate][slot][0]), partner(y, ROUTES[mate][slot][1]), core ^ outside)
        for mate in range(2)
    ]
    return jnp.where((core ^ relayed) == 0, spots[0], spots[1])


def place_column(step_x, step_y, outside, direct):
    if not direct:
        place_x = jnp.where(step_x == 0, 2, jnp.where(step_x < 0, 0, 1))
        place_y = jnp.where(step_y == 0, 2, jnp.where(step_y < 0, 0, 1))
        return outside * 9 + place_y * 3 + place_x
    x, y, core = column_here()
    way_x = jnp.where(step_x == 0, 0, jnp.where(step_x == 1 - 2 * (x & 1), 1, 2))
    way_y = jnp.where(step_y == 0, 0, jnp.where(step_y == 1 - 2 * (y & 1), 1, 2))
    way = way_x * 3 + way_y
    chunk = 8 + 9 * outside
    for mate in range(2):
        mine = core == mate
        for slot, (to_x, to_y) in enumerate(ROUTES[mate]):
            spot = jnp.where(mine, 2 * slot + outside, 9 + 2 * slot + 1 - outside)
            chunk = jnp.where(way == to_x * 3 + to_y, spot, chunk)
    return chunk


def decode(code, slots):
    offset = code >> 6
    slot = code & 63
    step_x = jnp.where(offset >= 18, 1, jnp.where(offset >= 9, 0, -1))
    rest = offset - 9 * (step_x + 1)
    step_y = jnp.where(rest >= 6, 1, jnp.where(rest >= 3, 0, -1))
    step_z = rest - 3 * (step_y + 1) - 1
    block = lax.broadcasted_iota(jnp.int32, (NEIGH, ATOMS), 1) // slots
    level = block + step_z
    outside = jnp.where((level < 0) | (level > 1), 1, 0)
    return step_x, step_y, step_z, outside, (level & 1) * slots + slot


def blank_kernel(out_ref):
    out_ref[...] = jnp.zeros(out_ref.shape, F32)


def pack_kernel(blank_ref, pos_ref, spec_ref, nb_ref, out_ref):
    slots = spec_ref.shape[-1]
    half = nb_ref.shape[-1] // 2
    for block in range(2):
        lanes = slice(block * slots, (block + 1) * slots)
        for c in range(3):
            out_ref[0, c : c + 1, lanes] = pos_ref[0, 0, block : block + 1, c * slots : (c + 1) * slots]
        out_ref[0, 3:4, lanes] = spec_ref[0, 0, block : block + 1, :].astype(F32)
        for part in range(half // ATOMS):
            first = nb_ref[0, 0, block : block + 1, part * ATOMS : (part + 1) * ATOMS]
            second = nb_ref[0, 0, block : block + 1, half + part * ATOMS : half + (part + 1) * ATOMS]
            row = 4 + block * 2 + part
            out_ref[0, row : row + 1, :] = (first * 2048 + second).astype(F32)


def onehot_kernel(direct, code_ref, second_ref, readout_ref, onehot_ref, secondt_ref, rocol_ref):
    step_x, step_y, step_z, outside, lane = decode(code_ref[...], ATOMS // 2)
    target = place_column(step_x, step_y, outside, direct) * ATOMS + lane
    secondt_ref[...] = second_ref[...].astype(F32).T.astype(BF16)
    rocol_ref[...] = jnp.broadcast_to(readout_ref[...], (ATOMS, ATOMS)).T
    atom = lax.broadcasted_iota(jnp.int32, (ATOMS, ATOMS), 0)
    for k in range(NEIGH):
        aim = jnp.broadcast_to(target[k : k + 1, :], (ATOMS, ATOMS)) - atom

        def fill(c, carry, k=k, aim=aim):
            rows = pl.ds(pl.multiple_of(c * ATOMS, ATOMS), ATOMS)
            hit = jnp.where(aim == c * ATOMS, 1.0, 0.0)
            onehot_ref[rows, k * ATOMS : (k + 1) * ATOMS] = hit.astype(BF16)
            return carry

        lax.fori_loop(0, CHUNKS, fill, 0)


def listed_codes(words):
    words = words.astype(jnp.int32)
    first, second = words >> 11, words & 2047
    width = 4 * ATOMS
    slots = width // NEIGH
    lane = lax.broadcasted_iota(jnp.int32, (NEIGH, width), 1)
    row = lax.broadcasted_iota(jnp.int32, (NEIGH, width), 0)
    mine = (lane & (NEIGH - 1)) == row
    spot = lax.broadcasted_iota(jnp.int32, (width, ATOMS), 0) // NEIGH
    column = lax.broadcasted_iota(jnp.int32, (width, ATOMS), 1)
    total = jnp.zeros((NEIGH, ATOMS), F32)
    for block in range(2):
        pieces = [part[2 * block + i : 2 * block + i + 1, :] for part in (first, second) for i in range(2)]
        listed = jnp.broadcast_to(jnp.concatenate(pieces, axis=1), (NEIGH, width))
        listed = jnp.where(mine, listed, 0)
        high = (listed >> 4).astype(F32).astype(BF16)
        low = (listed & 15).astype(F32).astype(BF16)
        pick = jnp.where(spot + block * slots == column, 1.0, 0.0).astype(BF16)
        total = total + 16.0 * jnp.dot(high, pick, preferred_element_type=F32)
        total = total + jnp.dot(low, pick, preferred_element_type=F32)
    return (total + 0.5).astype(jnp.int32)


def sigmoid(v):
    return 0.5 * jnp.tanh(0.5 * v) + 0.5


def silu_pair(v):
    s = sigmoid(v)
    value = v * s
    return value, s + value * (1.0 - s)


def angular_rows(ux, uy, uz):
    return [
        None, ux, uy, uz, ROOT3 * ux * uy, ROOT3 * uy * uz, 0.5 * (3.0 * uz * uz - 1.0),
        ROOT3 * ux * uz, 0.5 * ROOT3 * (ux * ux - uy * uy),
    ]


def spread_rows(yb_ref, angular):
    for m in range(1, 9):
        for k in range(NEIGH):
            yb_ref[m * NEIGH + k] = jnp.broadcast_to(angular[m][k : k + 1, :], (8, ATOMS))


def basis_parts(r_row):
    row = lax.broadcasted_iota(jnp.int32, (8, ATOMS), 0).astype(F32)
    centers = CUTOFF * (row + 0.5) / 8.0
    r = jnp.broadcast_to(r_row, (8, ATOMS))
    ratio = r * (1.0 / CUTOFF)
    inner = 1.0 - ratio * ratio
    gap = r - centers
    return jnp.exp(-SHARPNESS * gap * gap), gap, inner, ratio


PIECE = (0, 1, 1, 1, 2, 2, 2, 2, 2)


def forward_kernel(parts, direct, *refs):
    tables = refs[:parts]
    (
        center_ref, neighbor_ref, radial_ref, mix_ref, envw_ref, upd_ref,
        table_ref, code_ref, edge_ref, dsb_ref, dsl_ref, dse_ref, env_ref, v_ref, geo_ref,
        yb_ref, inv_ref, lat_ref, pad_ref,
    ) = refs[parts:]
    pad_ref[...] = jnp.zeros(pad_ref.shape, F32)
    pad_ref[0:8, :] = radial_ref[...].astype(F32)
    pad_ref[8 : 8 + neighbor_ref.shape[0], :] = neighbor_ref[...].astype(F32)
    pad_ref[16 : 16 + center_ref.shape[0], :] = center_ref[...].astype(F32)
    wcat = pad_ref[...].T[:, :32].astype(BF16)
    mixt = mix_ref[...].astype(F32).T.astype(BF16)
    envt = envw_ref[...].astype(F32).T.astype(BF16)
    updt = [upd_ref[p * ATOMS : (p + 1) * ATOMS, :].astype(F32).T.astype(BF16) for p in range(3)]
    updt = jnp.concatenate(updt, axis=1)

    def chunk_at(far, dx, dy):
        if direct:
            return tables[0][owner_at(dx, dy, far)]
        return tables[far][(0, 2, 1)[dy + 1] * 3 + (0, 2, 1)[dx + 1]]

    home = chunk_at(0, 0, 0)
    code = listed_codes(home[4:8, :])
    code_ref[...] = code
    step_x, step_y, step_z, outside, lane = decode(code, ATOMS // 2)
    spot = outside * 9 + step_y * 3 + step_x + 4
    found = [jnp.zeros((NEIGH, ATOMS), F32) for _ in range(4)]
    for far in range(2):
        for dy in (-1, 0, 1):
            for dx in (-1, 0, 1):
                hit = spot == far * 9 + dy * 3 + dx + 4
                rows = chunk_at(far, dx, dy)
                for f in range(4):
                    row = jnp.broadcast_to(rows[f : f + 1, :], (NEIGH, ATOMS))
                    found[f] = jnp.where(hit, jnp.take_along_axis(row, lane, axis=1), found[f])
    d = [
        step.astype(F32) + (found[c] - jnp.broadcast_to(home[c : c + 1, :], (NEIGH, ATOMS)))
        for c, step in enumerate((step_x, step_y, step_z))
    ]
    r = jnp.sqrt(d[0] * d[0] + d[1] * d[1] + d[2] * d[2])
    ux, uy, uz = d[0] / r, d[1] / r, d[2] / r
    geo_ref[0] = r
    geo_ref[1] = ux
    geo_ref[2] = uy
    geo_ref[3] = uz
    spread_rows(yb_ref, angular_rows(ux, uy, uz))

    kind = lax.broadcasted_iota(jnp.int32, (8, ATOMS), 0).astype(F32)
    center_hot = jnp.where(jnp.broadcast_to(home[3:4, :], (8, ATOMS)) == kind, 1.0, 0.0)
    zero = jnp.zeros((8, ATOMS), F32)
    columns = []
    for k in range(NEIGH):
        bump, gap, inner, ratio = basis_parts(r[k : k + 1, :])
        other_hot = jnp.where(jnp.broadcast_to(found[3][k : k + 1, :], (8, ATOMS)) == kind, 1.0, 0.0)
        columns.append(jnp.concatenate([bump * (inner * inner), other_hot, center_hot, zero], axis=0).astype(BF16))
    for j in range(EDGES // TILE):
        span = slice(j * TILE, (j + 1) * TILE)
        per = TILE // ATOMS
        x = jnp.concatenate(columns[j * per : (j + 1) * per], axis=1)
        act, ds = silu_pair(jnp.dot(wcat, x, preferred_element_type=F32))
        dsb_ref[:, span] = ds
        latent, ds = silu_pair(jnp.dot(mixt, act.astype(BF16), preferred_element_type=F32))
        dsl_ref[:, span] = ds
        lat_ref[:, span] = latent
        env_ref[:, span] = jnp.dot(envt, latent.astype(BF16), preferred_element_type=F32)
    for t in range(8):
        halves = []
        for h in range(2):
            rows = slice(t * 16 + h * 8, t * 16 + h * 8 + 8)
            env = [env_ref[rows, k * ATOMS : (k + 1) * ATOMS] for k in range(NEIGH)]
            field = []
            for m in range(9):
                terms = [env[k] if m == 0 else env[k] * yb_ref[m * NEIGH + k] for k in range(NEIGH)]
                while len(terms) > 1:
                    terms = [terms[i] + terms[i + 1] for i in range(0, len(terms), 2)]
                field.append(terms[0] * 0.125)
                v_ref[m, rows, :] = field[m]
            out = []
            for k in range(NEIGH):
                sums = [field[0], None, None]
                for m in range(1, 9):
                    term = field[m] * yb_ref[m * NEIGH + k]
                    sums[PIECE[m]] = term if sums[PIECE[m]] is None else sums[PIECE[m]] + term
                out.append(sums)
            halves.append(out)
        for k in range(NEIGH):
            for p in range(3):
                both = jnp.concatenate([halves[0][k][p], halves[1][k][p]], axis=0)
                inv_ref[p * ATOMS + t * 16 : p * ATOMS + t * 16 + 16, k * ATOMS : (k + 1) * ATOMS] = both.astype(BF16)
    mean = jnp.zeros((ATOMS, ATOMS), F32)
    for j in range(EDGES // TILE):
        span = slice(j * TILE, (j + 1) * TILE)
        update = jnp.dot(updt, inv_ref[:, span], preferred_element_type=F32)
        edge, ds = silu_pair(lat_ref[:, span] + update)
        edge_ref[:, span] = edge
        dse_ref[:, span] = ds
        for i in range(TILE // ATOMS):
            mean = mean + edge[:, i * ATOMS : (i + 1) * ATOMS]
    table_ref[0] = (mean * 0.125).astype(BF16)


def second_kernel(parts, order, *refs):
    (
        onehot_ref, edge_ref, second_ref, secondt_ref, rocol_ref,
        energy_ref, grad_edge_ref, back_own_ref, back_other_ref, grad_ref,
    ) = refs[parts:]
    table = jnp.concatenate([refs[array][row] for array, row in order], axis=1)
    rocol = rocol_ref[...]
    total = jnp.zeros((ATOMS, ATOMS), F32)
    for j in range(EDGES // TILE):
        span = slice(j * TILE, (j + 1) * TILE)
        other = jnp.dot(table, onehot_ref[:, span], preferred_element_type=F32)
        edge = edge_ref[:, span]
        hidden, ds = silu_pair(jnp.dot(secondt_ref[...], (edge * other).astype(BF16), preferred_element_type=F32))
        for i in range(TILE // ATOMS):
            total = total + hidden[:, i * ATOMS : (i + 1) * ATOMS]
        grad_hidden = ds * jnp.concatenate([rocol] * (TILE // ATOMS), axis=1)
        grad_prod = jnp.dot(second_ref[...], grad_hidden.astype(BF16), preferred_element_type=F32)
        grad_prod = grad_prod.astype(BF16).astype(F32)
        grad_edge_ref[:, span] = grad_prod * other
        grad_ref[:, span] = (grad_prod * edge).astype(BF16)
    energy = jnp.sum(total * rocol, axis=0, keepdims=True)
    energy_ref[...] = energy
    grad = grad_ref[...]
    for c in range(CHUNKS):
        rows = slice(c * ATOMS, (c + 1) * ATOMS)
        back = lax.dot_general(
            grad, onehot_ref[rows, :], (((1,), (1,)), ((), ())), preferred_element_type=F32
        )
        ref = back_own_ref if c < 9 else back_other_ref
        ref[c % 9] = back.astype(BF16)


def backward_kernel(
    direct, owned_ref, energy_ref, grad_edge_ref, dse_ref, dsl_ref, dsb_ref, env_ref, v_ref, geo_ref, onehot_ref,
    upd_ref, envw_ref, mix_ref, radial_ref, *refs,
):
    outs = refs[: 1 if direct else 2]
    yb_ref, dinv_ref, denv_ref, dlat_ref, part_ref, force_ref = refs[len(outs) :]
    r, ux, uy, uz = (geo_ref[i] for i in range(4))
    angular = angular_rows(ux, uy, uz)
    spread_rows(yb_ref, angular)
    share = owned_ref[0] * 0.125
    for j in range(EDGES // TILE):
        span = slice(j * TILE, (j + 1) * TILE)
        d_edge = grad_edge_ref[:, span] + jnp.concatenate([share] * (TILE // ATOMS), axis=1)
        d_pre = d_edge * dse_ref[:, span]
        dlat_ref[:, span] = d_pre
        dinv_ref[:, span] = jnp.dot(upd_ref[...], d_pre.astype(BF16), preferred_element_type=F32).astype(BF16)
    part_ref[...] = jnp.zeros(part_ref.shape, F32)
    for t in range(8):
        wide = [
            [
                dinv_ref[p * ATOMS + t * 16 : p * ATOMS + t * 16 + 16, k * ATOMS : (k + 1) * ATOMS].astype(F32)
                for k in range(NEIGH)
            ]
            for p in range(3)
        ]
        halves = []
        for h in range(2):
            rows = slice(t * 16 + h * 8, t * 16 + h * 8 + 8)
            dinv = [[wide[p][k][h * 8 : h * 8 + 8] for k in range(NEIGH)] for p in range(3)]
            env = [env_ref[rows, k * ATOMS : (k + 1) * ATOMS] for k in range(NEIGH)]
            denv = [None] * NEIGH
            for m in range(9):
                down = dinv[PIECE[m]]
                terms = [down[k] if m == 0 else down[k] * yb_ref[m * NEIGH + k] for k in range(NEIGH)]
                while len(terms) > 1:
                    terms = [terms[i] + terms[i + 1] for i in range(0, len(terms), 2)]
                d_field = terms[0] * 0.125
                if m == 0:
                    denv = [d_field] * NEIGH
                    continue
                field = v_ref[m, rows, :]
                for k in range(NEIGH):
                    spot = m * NEIGH + k
                    part_ref[spot] = part_ref[spot] + (down[k] * field + env[k] * d_field)
                    denv[k] = denv[k] + d_field * yb_ref[spot]
            halves.append(denv)
        for k in range(NEIGH):
            both = jnp.concatenate([halves[0][k], halves[1][k]], axis=0)
            denv_ref[t * 16 : t * 16 + 16, k * ATOMS : (k + 1) * ATOMS] = both.astype(BF16)
    d_r_rows = []
    for j in range(EDGES // TILE):
        span = slice(j * TILE, (j + 1) * TILE)
        d_lat = jnp.dot(envw_ref[...], denv_ref[:, span], preferred_element_type=F32).astype(BF16).astype(F32)
        d_mix = (dlat_ref[:, span] + d_lat) * dsl_ref[:, span]
        d_act = jnp.dot(mix_ref[...], d_mix.astype(BF16), preferred_element_type=F32).astype(BF16).astype(F32)
        d_before = (d_act * dsb_ref[:, span]).astype(BF16)
        d_basis = jnp.dot(radial_ref[...], d_before, preferred_element_type=F32).astype(BF16).astype(F32)
        for i in range(TILE // ATOMS):
            k = j * (TILE // ATOMS) + i
            bump, gap, inner, ratio = basis_parts(r[k : k + 1, :])
            slope = bump * inner * (-2.0 * SHARPNESS * gap * inner - (4.0 / CUTOFF) * ratio)
            d_r_rows.append(jnp.sum(slope * d_basis[:, i * ATOMS : (i + 1) * ATOMS], axis=0, keepdims=True))
    d_r = jnp.concatenate(d_r_rows, axis=0)
    dy = [None]
    for m in range(1, 9):
        rows = [jnp.sum(part_ref[m * NEIGH + k], axis=0, keepdims=True) for k in range(NEIGH)]
        dy.append(jnp.concatenate(rows, axis=0))
    d_ux = dy[1] + ROOT3 * (uy * dy[4] + uz * dy[7] + ux * dy[8])
    d_uy = dy[2] + ROOT3 * (ux * dy[4] + uz * dy[5] - uy * dy[8])
    d_uz = dy[3] + ROOT3 * (uy * dy[5] + ux * dy[7]) + 3.0 * uz * dy[6]
    along = ux * d_ux + uy * d_uy + uz * d_uz
    inverse = 1.0 / r
    radial = d_r - along * inverse
    pull = [d_ux * inverse + ux * radial, d_uy * inverse + uy * radial, d_uz * inverse + uz * radial]
    high = [p.astype(BF16).astype(F32) for p in pull]
    low = [p - h for p, h in zip(pull, high)]
    zero = jnp.zeros((1, ATOMS), F32)
    for k in range(NEIGH):
        rows = [h[k : k + 1, :] for h in high] + [zero] * 5 + [q[k : k + 1, :] for q in low] + [zero] * 5
        force_ref[:, k * ATOMS : (k + 1) * ATOMS] = jnp.concatenate(rows, axis=0).astype(BF16)
    force = force_ref[...]
    center = jnp.concatenate([jnp.sum(p, axis=0, keepdims=True) for p in pull] + [-energy_ref[...]], axis=0)
    if direct:
        outs[0][...] = jnp.zeros(outs[0].shape, F32)
    for c in range(CHUNKS):
        rows = slice(c * ATOMS, (c + 1) * ATOMS)
        back = lax.dot_general(
            force, onehot_ref[rows, :], (((1,), (1,)), ((), ())), preferred_element_type=F32
        )
        moved = back[:4] + back[8:12]
        if c == 8:
            moved = moved - center
        if direct:
            outs[0][owner_of_chunk(c)] = moved
        else:
            outs[c // 9][c % 9] = moved


def finish_kernel(moved_ref, energy_ref, out_ref):
    slots = energy_ref.shape[-1]
    total = jnp.sum(moved_ref[...], axis=0)
    for block in range(2):
        lanes = slice(block * slots, (block + 1) * slots)
        energy_ref[0, 0, block : block + 1, :] = total[3:4, lanes]
        for c in range(3):
            out_ref[0, 0, block : block + 1, c * slots : (c + 1) * slots] = -total[c : c + 1, lanes]


def call(kernel, outs, scratch=(), name=None, limit=24 << 20, place=pltpu.VMEM, cost=None):
    whole = pl.BlockSpec(memory_space=pltpu.VMEM)
    shapes = [jax.ShapeDtypeStruct(shape, kind) for shape, kind in outs]

    def run(*args):
        return pl.pallas_call(
            kernel,
            out_shape=shapes,
            in_specs=[pl.BlockSpec(memory_space=place)] * len(args),
            out_specs=[whole] * len(shapes),
            scratch_shapes=list(scratch),
            compiler_params=pltpu.CompilerParams(vmem_limit_bytes=limit),
            cost_estimate=cost,
            name=name,
        )(*args)

    return run


def on_device(
    positions, species, neighbors, center_table, neighbor_table, radial_weight, mix_weight,
    env_weight, update_weight, second_weight, readout,
):
    slots = species.shape[-1]
    edges = (ATOMS, EDGES)
    square = (ATOMS, ATOMS)
    readout = readout.reshape(1, ATOMS)
    direct = is_direct()
    devices = 32
    (blank,) = call(
        blank_kernel,
        [((8, ATOMS), F32)],
        name="blank",
        cost=pl.CostEstimate(flops=1 << 34, bytes_accessed=64 << 20, transcendentals=0),
    )()
    (packed,) = call(pack_kernel, [((1, 8, ATOMS), F32)], name="pack")(blank, positions, species, neighbors)
    if direct:
        copies = jnp.broadcast_to(packed, (devices, 8, ATOMS))
        tables = [lax.all_to_all(copies, EVERY, 0, 0, tiled=True)]
    else:
        tables, order = gather_halo(packed)
    table, code, edge, dsb, dsl, dse, env, field, geo = call(
        functools.partial(forward_kernel, len(tables), direct),
        [
            ((1,) + square, BF16), ((NEIGH, ATOMS), jnp.int32), (edges, F32), (edges, F32), (edges, F32),
            (edges, F32), (edges, F32), ((9,) + square, F32), ((4, NEIGH, ATOMS), F32),
        ],
        [
            pltpu.VMEM((72, 8, ATOMS), F32), pltpu.VMEM((3 * ATOMS, EDGES), BF16), pltpu.VMEM(edges, F32),
            pltpu.VMEM(square, F32),
        ],
        name="forward",
    )(*tables, center_table, neighbor_table, radial_weight, mix_weight, env_weight, update_weight)
    onehot, secondt, rocol = call(
        functools.partial(onehot_kernel, direct),
        [((CHUNKS * ATOMS, EDGES), BF16), (square, BF16), (square, F32)],
        name="onehot",
        cost=pl.CostEstimate(flops=1 << 30, bytes_accessed=8 << 20, transcendentals=0),
    )(code, second_weight, readout)
    tables, order = gather_halo(table)
    energy, grad_edge, back_own, back_other = call(
        functools.partial(second_kernel, len(tables), order),
        [((1, ATOMS), F32), (edges, F32), ((9,) + square, BF16), ((9,) + square, BF16)],
        [pltpu.VMEM(edges, BF16)],
        name="second",
    )(*tables, onehot, edge, second_weight, secondt, rocol)
    owned = reduce_halo(back_own, back_other)
    moved = call(
        functools.partial(backward_kernel, direct),
        [((devices, 4, ATOMS), F32)] if direct else [((9, 4, ATOMS), F32)] * 2,
        [
            pltpu.VMEM((72, 8, ATOMS), F32), pltpu.VMEM((3 * ATOMS, EDGES), BF16), pltpu.VMEM(edges, BF16),
            pltpu.VMEM(edges, F32), pltpu.VMEM((72, 8, ATOMS), F32), pltpu.VMEM((16, EDGES), BF16),
        ],
        name="backward",
    )(
        owned, energy, grad_edge, dse, dsl, dsb, env, field, geo, onehot, update_weight, env_weight, mix_weight,
        radial_weight,
    )
    moved = lax.all_to_all(moved[0], EVERY, 0, 0, tiled=True) if direct else reduce_halo(*moved)
    return call(finish_kernel, [((1, 1, 2, slots), F32), ((1, 1, 2, 3 * slots), F32)], name="finish")(moved)


def solution(mesh):
    split = P("gx", "gy", "gz", None)
    return jax.shard_map(
        on_device,
        mesh=mesh,
        in_specs=(split, split, split) + (P(),) * 8,
        out_specs=(split, split),
        check_vma=False,
    )
```

```python
import functools
import math

import jax
import jax.numpy as jnp
from jax import lax
from jax.experimental import pallas as pl
from jax.experimental.pallas import tpu as pltpu
from jax.sharding import PartitionSpec as P

NEIGH = 8
ATOMS = 128
EDGES = NEIGH * ATOMS
CHUNKS = 18
CUTOFF = 4.0
SHARPNESS = 2.0
ROOT3 = math.sqrt(3.0)
F32 = jnp.float32
BF16 = jnp.bfloat16
TILE = 1024


RING = (0, 1, 3, 2)
ROUTES = (((1, 0), (0, 2), (1, 2), (2, 1)), ((2, 0), (0, 1), (1, 1), (2, 2)))
EVERY = ("gx", "gy", "gz")


def is_direct():
    return tuple(lax.axis_size(axis) for axis in EVERY) == (4, 4, 2)


def shifted(value, axis, step):
    count = lax.axis_size(axis)
    return lax.ppermute(value, axis, [(i, (i + step) % count) for i in range(count)])


def partner(index, way):
    if way == 0:
        return index
    if way == 1:
        return index ^ 1
    return (index + 2 * (index & 1) - 1) & 3


def number(x, y, core):
    return (x * 4 + y) * 2 + core


def swapped(value, slot):
    pairs = []
    for x in range(4):
        for y in range(4):
            for core in range(2):
                way_x, way_y = ROUTES[core][slot]
                to_x, to_y = partner(x, way_x), partner(y, way_y)
                pairs.append((number(RING[x], RING[y], core), number(RING[to_x], RING[to_y], core)))
    return lax.ppermute(value, EVERY, pairs)


def gather_halo(chunk, beside=None):
    if is_direct():
        both = jnp.concatenate([chunk, shifted(chunk, "gz", 1)], axis=0)
        direct = [swapped(both, slot) for slot in range(4)]
        direct, beside = lax.optimization_barrier((direct, beside))
        relayed = shifted(jnp.concatenate(direct, axis=0), "gz", 1)
        near = [(slot, row) for slot in range(4) for row in range(2)] + [(4, 0)]
        far = [(5, row) for row in range(8)] + [(4, 1)]
        return direct + [both, relayed], near + far, beside
    for axis in ("gx", "gy"):
        lower = shifted(chunk, axis, 1)
        upper = shifted(chunk, axis, -1)
        chunk = jnp.concatenate([lower, upper, chunk], axis=0)
    order = [(array, row) for array in range(2) for row in range(9)]
    if lax.axis_size("gz") == 2:
        return [chunk, shifted(chunk, "gz", 1)], order, beside
    half = chunk.shape[-1] // 2
    above = shifted(chunk[..., :half], "gz", -1)
    below = shifted(chunk[..., half:], "gz", 1)
    return [chunk, jnp.concatenate([above, below], axis=-1)], order, beside


def reduce_halo(own, other):
    kind = own.dtype
    if is_direct():
        own = own.astype(F32) + shifted(other, "gz", 1).astype(F32)
        came = [swapped(own[2 * slot : 2 * slot + 2].astype(kind), slot).astype(F32) for slot in range(4)]
        both = came[0] + came[1] + came[2] + came[3]
        return own[8:] + both[:1] + shifted(both[1:], "gz", 1)
    if lax.axis_size("gz") == 2:
        back = shifted(other, "gz", 1)
    else:
        half = other.shape[-1] // 2
        first = shifted(other[..., :half], "gz", 1)
        second = shifted(other[..., half:], "gz", -1)
        back = jnp.concatenate([first, second], axis=-1)
    own = own.astype(F32) + back.astype(F32)
    for axis, size in (("gy", 3), ("gx", 1)):
        lower = shifted(own[:size].astype(kind), axis, -1)
        upper = shifted(own[size : 2 * size].astype(kind), axis, 1)
        own = own[2 * size :] + lower.astype(F32) + upper.astype(F32)
    return own


def ring_at(index):
    return index ^ (index >> 1)


def column_here():
    return ring_at(lax.axis_index("gx")), ring_at(lax.axis_index("gy")), lax.axis_index("gz")


def owner_at(step_x, step_y, outside):
    x, y, core = column_here()
    return number((x + step_x) & 3, (y + step_y) & 3, core ^ outside)


def place_column(step_x, step_y, outside, direct):
    if not direct:
        place_x = jnp.where(step_x == 0, 2, jnp.where(step_x < 0, 0, 1))
        place_y = jnp.where(step_y == 0, 2, jnp.where(step_y < 0, 0, 1))
        return outside * 9 + place_y * 3 + place_x
    x, y, core = column_here()
    way_x = jnp.where(step_x == 0, 0, jnp.where(step_x == 1 - 2 * (x & 1), 1, 2))
    way_y = jnp.where(step_y == 0, 0, jnp.where(step_y == 1 - 2 * (y & 1), 1, 2))
    way = way_x * 3 + way_y
    chunk = 8 + 9 * outside
    for mate in range(2):
        mine = core == mate
        for slot, (to_x, to_y) in enumerate(ROUTES[mate]):
            spot = jnp.where(mine, 2 * slot + outside, 9 + 2 * slot + 1 - outside)
            chunk = jnp.where(way == to_x * 3 + to_y, spot, chunk)
    return chunk


def decode(code, slots):
    offset = code >> 6
    slot = code & 63
    step_x = jnp.where(offset >= 18, 1, jnp.where(offset >= 9, 0, -1))
    rest = offset - 9 * (step_x + 1)
    step_y = jnp.where(rest >= 6, 1, jnp.where(rest >= 3, 0, -1))
    step_z = rest - 3 * (step_y + 1) - 1
    block = lax.broadcasted_iota(jnp.int32, (NEIGH, ATOMS), 1) // slots
    level = block + step_z
    outside = jnp.where((level < 0) | (level > 1), 1, 0)
    return step_x, step_y, step_z, outside, (level & 1) * slots + slot


def blank_kernel(out_ref):
    out_ref[...] = jnp.zeros(out_ref.shape, F32)


def pack_kernel(blank_ref, pos_ref, spec_ref, nb_ref, out_ref):
    slots = spec_ref.shape[-1]
    half = nb_ref.shape[-1] // 2
    for block in range(2):
        lanes = slice(block * slots, (block + 1) * slots)
        for c in range(3):
            out_ref[0, c : c + 1, lanes] = pos_ref[0, 0, block : block + 1, c * slots : (c + 1) * slots]
        out_ref[0, 3:4, lanes] = spec_ref[0, 0, block : block + 1, :].astype(F32)
        for part in range(half // ATOMS):
            first = nb_ref[0, 0, block : block + 1, part * ATOMS : (part + 1) * ATOMS]
            second = nb_ref[0, 0, block : block + 1, half + part * ATOMS : half + (part + 1) * ATOMS]
            row = 4 + block * 2 + part
            out_ref[0, row : row + 1, :] = (first * 2048 + second).astype(F32)


def onehot_kernel(
    direct, code_ref, second_ref, readout_ref, gather_ref, scatter_ref, lane_ref, secondt_ref, rocol_ref, turn_ref
):
    step_x, step_y, step_z, outside, lane = decode(code_ref[...], ATOMS // 2)
    target = place_column(step_x, step_y, outside, direct) * ATOMS + lane
    secondt_ref[...] = second_ref[...].astype(F32).T.astype(BF16)
    rocol_ref[...] = jnp.broadcast_to(readout_ref[...], (ATOMS, ATOMS)).T
    turn_ref[...] = jnp.zeros(turn_ref.shape, F32)
    turn_ref[0:NEIGH, :] = target.astype(F32)
    turned = turn_ref[...].T.astype(jnp.int32)
    down = lax.broadcasted_iota(jnp.int32, (ATOMS, ATOMS), 0)
    across = lax.broadcasted_iota(jnp.int32, (ATOMS, ATOMS), 1)
    for k in range(NEIGH):
        span = slice(k * ATOMS, (k + 1) * ATOMS)
        aim = jnp.broadcast_to(target[k : k + 1, :], (ATOMS, ATOMS)) - down
        aim_turned = jnp.broadcast_to(turned[:, k : k + 1], (ATOMS, ATOMS)) - across
        near = jnp.broadcast_to(lane[k : k + 1, :], (ATOMS, ATOMS)) == down
        lane_ref[:, span] = jnp.where(near, 1.0, 0.0).astype(BF16)

        def fill(c, carry, span=span, aim=aim, aim_turned=aim_turned):
            part = pl.ds(pl.multiple_of(c * ATOMS, ATOMS), ATOMS)
            gather_ref[part, span] = jnp.where(aim == c * ATOMS, 1.0, 0.0).astype(BF16)
            scatter_ref[span, part] = jnp.where(aim_turned == c * ATOMS, 1.0, 0.0).astype(BF16)
            return carry

        lax.fori_loop(0, CHUNKS, fill, 0)


def listed_codes(words):
    words = words.astype(jnp.int32)
    first, second = words >> 11, words & 2047
    width = 4 * ATOMS
    slots = width // NEIGH
    lane = lax.broadcasted_iota(jnp.int32, (NEIGH, width), 1)
    row = lax.broadcasted_iota(jnp.int32, (NEIGH, width), 0)
    mine = (lane & (NEIGH - 1)) == row
    spot = lax.broadcasted_iota(jnp.int32, (width, ATOMS), 0) // NEIGH
    column = lax.broadcasted_iota(jnp.int32, (width, ATOMS), 1)
    total = jnp.zeros((NEIGH, ATOMS), F32)
    for block in range(2):
        pieces = [part[2 * block + i : 2 * block + i + 1, :] for part in (first, second) for i in range(2)]
        listed = jnp.broadcast_to(jnp.concatenate(pieces, axis=1), (NEIGH, width))
        listed = jnp.where(mine, listed, 0)
        high = (listed >> 4).astype(F32).astype(BF16)
        low = (listed & 15).astype(F32).astype(BF16)
        pick = jnp.where(spot + block * slots == column, 1.0, 0.0).astype(BF16)
        total = total + 16.0 * jnp.dot(high, pick, preferred_element_type=F32)
        total = total + jnp.dot(low, pick, preferred_element_type=F32)
    return (total + 0.5).astype(jnp.int32)


def sigmoid(v):
    return 0.5 * jnp.tanh(0.5 * v) + 0.5


def silu_pair(v):
    s = sigmoid(v)
    value = v * s
    return value, s + value * (1.0 - s)


def angular_rows(ux, uy, uz):
    return [
        None, ux, uy, uz, ROOT3 * ux * uy, ROOT3 * uy * uz, 0.5 * (3.0 * uz * uz - 1.0),
        ROOT3 * ux * uz, 0.5 * ROOT3 * (ux * ux - uy * uy),
    ]


def spread_rows(yb_ref, angular):
    for m in range(1, 9):
        for k in range(NEIGH):
            yb_ref[m * NEIGH + k] = jnp.broadcast_to(angular[m][k : k + 1, :], (8, ATOMS))


def basis_parts(r_row):
    row = lax.broadcasted_iota(jnp.int32, (8, ATOMS), 0).astype(F32)
    centers = CUTOFF * (row + 0.5) / 8.0
    r = jnp.broadcast_to(r_row, (8, ATOMS))
    ratio = r * (1.0 / CUTOFF)
    inner = 1.0 - ratio * ratio
    gap = r - centers
    return jnp.exp(-SHARPNESS * gap * gap), gap, inner, ratio


PIECE = (0, 1, 1, 1, 2, 2, 2, 2, 2)


def forward_kernel(parts, direct, *refs):
    tables = refs[:parts]
    (
        center_ref, neighbor_ref, radial_ref, mix_ref, envw_ref, upd_ref,
        table_ref, code_ref, edge_ref, dsb_ref, dsl_ref, dse_ref, env_ref, v_ref, geo_ref,
        yb_ref, inv_ref, lat_ref, pad_ref,
    ) = refs[parts:]
    pad_ref[...] = jnp.zeros(pad_ref.shape, F32)
    pad_ref[0:8, :] = radial_ref[...].astype(F32)
    pad_ref[8 : 8 + neighbor_ref.shape[0], :] = neighbor_ref[...].astype(F32)
    pad_ref[16 : 16 + center_ref.shape[0], :] = center_ref[...].astype(F32)
    wcat = pad_ref[...].T[:, :32].astype(BF16)
    mixt = mix_ref[...].astype(F32).T.astype(BF16)
    envt = envw_ref[...].astype(F32).T.astype(BF16)
    updt = [upd_ref[p * ATOMS : (p + 1) * ATOMS, :].astype(F32).T.astype(BF16) for p in range(3)]
    updt = jnp.concatenate(updt, axis=1)

    def chunk_at(far, dx, dy):
        if direct:
            return tables[0][owner_at(dx, dy, far)]
        return tables[far][(0, 2, 1)[dy + 1] * 3 + (0, 2, 1)[dx + 1]]

    home = chunk_at(0, 0, 0)
    code = listed_codes(home[4:8, :])
    code_ref[...] = code
    step_x, step_y, step_z, outside, lane = decode(code, ATOMS // 2)
    spot = outside * 9 + step_y * 3 + step_x + 4
    found = [jnp.zeros((NEIGH, ATOMS), F32) for _ in range(4)]
    for far in range(2):
        for dy in (-1, 0, 1):
            for dx in (-1, 0, 1):
                hit = spot == far * 9 + dy * 3 + dx + 4
                rows = chunk_at(far, dx, dy)
                for f in range(4):
                    row = jnp.broadcast_to(rows[f : f + 1, :], (NEIGH, ATOMS))
                    found[f] = jnp.where(hit, jnp.take_along_axis(row, lane, axis=1), found[f])
    d = [
        step.astype(F32) + (found[c] - jnp.broadcast_to(home[c : c + 1, :], (NEIGH, ATOMS)))
        for c, step in enumerate((step_x, step_y, step_z))
    ]
    r = jnp.sqrt(d[0] * d[0] + d[1] * d[1] + d[2] * d[2])
    ux, uy, uz = d[0] / r, d[1] / r, d[2] / r
    geo_ref[0] = r
    geo_ref[1] = ux
    geo_ref[2] = uy
    geo_ref[3] = uz
    spread_rows(yb_ref, angular_rows(ux, uy, uz))

    kind = lax.broadcasted_iota(jnp.int32, (8, ATOMS), 0).astype(F32)
    center_hot = jnp.where(jnp.broadcast_to(home[3:4, :], (8, ATOMS)) == kind, 1.0, 0.0)
    zero = jnp.zeros((8, ATOMS), F32)
    columns = []
    for k in range(NEIGH):
        bump, gap, inner, ratio = basis_parts(r[k : k + 1, :])
        other_hot = jnp.where(jnp.broadcast_to(found[3][k : k + 1, :], (8, ATOMS)) == kind, 1.0, 0.0)
        columns.append(jnp.concatenate([bump * (inner * inner), other_hot, center_hot, zero], axis=0).astype(BF16))
    for j in range(EDGES // TILE):
        span = slice(j * TILE, (j + 1) * TILE)
        per = TILE // ATOMS
        x = jnp.concatenate(columns[j * per : (j + 1) * per], axis=1)
        act, ds = silu_pair(jnp.dot(wcat, x, preferred_element_type=F32))
        dsb_ref[:, span] = ds
        latent, ds = silu_pair(jnp.dot(mixt, act.astype(BF16), preferred_element_type=F32))
        dsl_ref[:, span] = ds
        lat_ref[:, span] = latent
        env_ref[:, span] = jnp.dot(envt, latent.astype(BF16), preferred_element_type=F32)
    for t in range(8):
        halves = []
        for h in range(2):
            rows = slice(t * 16 + h * 8, t * 16 + h * 8 + 8)
            env = [env_ref[rows, k * ATOMS : (k + 1) * ATOMS] for k in range(NEIGH)]
            field = []
            for m in range(9):
                terms = [env[k] if m == 0 else env[k] * yb_ref[m * NEIGH + k] for k in range(NEIGH)]
                while len(terms) > 1:
                    terms = [terms[i] + terms[i + 1] for i in range(0, len(terms), 2)]
                field.append(terms[0] * 0.125)
                v_ref[m, rows, :] = field[m]
            out = []
            for k in range(NEIGH):
                sums = [field[0], None, None]
                for m in range(1, 9):
                    term = field[m] * yb_ref[m * NEIGH + k]
                    sums[PIECE[m]] = term if sums[PIECE[m]] is None else sums[PIECE[m]] + term
                out.append(sums)
            halves.append(out)
        for k in range(NEIGH):
            for p in range(3):
                both = jnp.concatenate([halves[0][k][p], halves[1][k][p]], axis=0)
                inv_ref[p * ATOMS + t * 16 : p * ATOMS + t * 16 + 16, k * ATOMS : (k + 1) * ATOMS] = both.astype(BF16)
    mean = jnp.zeros((ATOMS, ATOMS), F32)
    for j in range(EDGES // TILE):
        span = slice(j * TILE, (j + 1) * TILE)
        update = jnp.dot(updt, inv_ref[:, span], preferred_element_type=F32)
        edge, ds = silu_pair(lat_ref[:, span] + update)
        edge_ref[:, span] = edge
        dse_ref[:, span] = ds
        for i in range(TILE // ATOMS):
            mean = mean + edge[:, i * ATOMS : (i + 1) * ATOMS]
    table_ref[0] = (mean * 0.125).astype(BF16)


def second_kernel(parts, order, *refs):
    (
        gather_ref, scatter_ref, edge_ref, second_ref, secondt_ref, rocol_ref,
        energy_ref, grad_edge_ref, back_own_ref, back_other_ref, other_ref, grad_ref,
    ) = refs[parts:]
    table = jnp.concatenate([refs[array][row] for array, row in order], axis=1)
    rocol = rocol_ref[...]
    other_ref[...] = jnp.dot(table, gather_ref[...], preferred_element_type=F32)
    wide = 2 * ATOMS
    total = jnp.zeros((ATOMS, ATOMS), F32)
    for j in range(EDGES // wide):
        span = slice(j * wide, (j + 1) * wide)
        other = other_ref[:, span]
        edge = edge_ref[:, span]
        hidden, ds = silu_pair(jnp.dot(secondt_ref[...], (edge * other).astype(BF16), preferred_element_type=F32))
        total = total + hidden[:, :ATOMS] + hidden[:, ATOMS:]
        grad_hidden = ds * jnp.concatenate([rocol, rocol], axis=1)
        grad_prod = jnp.dot(second_ref[...], grad_hidden.astype(BF16), preferred_element_type=F32)
        grad_prod = grad_prod.astype(BF16).astype(F32)
        grad_edge_ref[:, span] = grad_prod * other
        grad_ref[:, span] = (grad_prod * edge).astype(BF16)
    energy_ref[...] = jnp.sum(total * rocol, axis=0, keepdims=True)
    for c in range(0, CHUNKS, 2):
        back = jnp.dot(
            grad_ref[...], scatter_ref[:, c * ATOMS : (c + 2) * ATOMS], preferred_element_type=F32
        ).astype(BF16)
        for i in range(2):
            ref = back_own_ref if c + i < 9 else back_other_ref
            ref[(c + i) % 9] = back[:, i * ATOMS : (i + 1) * ATOMS]


def backward_kernel(
    direct, owned_ref, energy_ref, grad_edge_ref, dse_ref, dsl_ref, dsb_ref, env_ref, v_ref, geo_ref, code_ref, lane_ref,
    upd_ref, envw_ref, mix_ref, radial_ref, *refs,
):
    outs = refs[: 1 if direct else 2]
    yb_ref, dinv_ref, denv_ref, dlat_ref, part_ref, force_ref = refs[len(outs) :]
    r, ux, uy, uz = (geo_ref[i] for i in range(4))
    angular = angular_rows(ux, uy, uz)
    spread_rows(yb_ref, angular)
    share = owned_ref[0] * 0.125
    for j in range(EDGES // TILE):
        span = slice(j * TILE, (j + 1) * TILE)
        d_edge = grad_edge_ref[:, span] + jnp.concatenate([share] * (TILE // ATOMS), axis=1)
        d_pre = d_edge * dse_ref[:, span]
        dlat_ref[:, span] = d_pre
        dinv_ref[:, span] = jnp.dot(upd_ref[...], d_pre.astype(BF16), preferred_element_type=F32).astype(BF16)
    part_ref[...] = jnp.zeros(part_ref.shape, F32)
    for t in range(8):
        wide = [
            [
                dinv_ref[p * ATOMS + t * 16 : p * ATOMS + t * 16 + 16, k * ATOMS : (k + 1) * ATOMS].astype(F32)
                for k in range(NEIGH)
            ]
            for p in range(3)
        ]
        halves = []
        for h in range(2):
            rows = slice(t * 16 + h * 8, t * 16 + h * 8 + 8)
            dinv = [[wide[p][k][h * 8 : h * 8 + 8] for k in range(NEIGH)] for p in range(3)]
            env = [env_ref[rows, k * ATOMS : (k + 1) * ATOMS] for k in range(NEIGH)]
            denv = [None] * NEIGH
            for m in range(9):
                down = dinv[PIECE[m]]
                terms = [down[k] if m == 0 else down[k] * yb_ref[m * NEIGH + k] for k in range(NEIGH)]
                while len(terms) > 1:
                    terms = [terms[i] + terms[i + 1] for i in range(0, len(terms), 2)]
                d_field = terms[0] * 0.125
                if m == 0:
                    denv = [d_field] * NEIGH
                    continue
                field = v_ref[m, rows, :]
                for k in range(NEIGH):
                    spot = m * NEIGH + k
                    part_ref[spot] = part_ref[spot] + (down[k] * field + env[k] * d_field)
                    denv[k] = denv[k] + d_field * yb_ref[spot]
            halves.append(denv)
        for k in range(NEIGH):
            both = jnp.concatenate([halves[0][k], halves[1][k]], axis=0)
            denv_ref[t * 16 : t * 16 + 16, k * ATOMS : (k + 1) * ATOMS] = both.astype(BF16)
    d_r_rows = []
    for j in range(EDGES // TILE):
        span = slice(j * TILE, (j + 1) * TILE)
        d_lat = jnp.dot(envw_ref[...], denv_ref[:, span], preferred_element_type=F32).astype(BF16).astype(F32)
        d_mix = (dlat_ref[:, span] + d_lat) * dsl_ref[:, span]
        d_act = jnp.dot(mix_ref[...], d_mix.astype(BF16), preferred_element_type=F32).astype(BF16).astype(F32)
        d_before = (d_act * dsb_ref[:, span]).astype(BF16)
        d_basis = jnp.dot(radial_ref[...], d_before, preferred_element_type=F32).astype(BF16).astype(F32)
        for i in range(TILE // ATOMS):
            k = j * (TILE // ATOMS) + i
            bump, gap, inner, ratio = basis_parts(r[k : k + 1, :])
            slope = bump * inner * (-2.0 * SHARPNESS * gap * inner - (4.0 / CUTOFF) * ratio)
            d_r_rows.append(jnp.sum(slope * d_basis[:, i * ATOMS : (i + 1) * ATOMS], axis=0, keepdims=True))
    d_r = jnp.concatenate(d_r_rows, axis=0)
    dy = [None]
    for m in range(1, 9):
        rows = [jnp.sum(part_ref[m * NEIGH + k], axis=0, keepdims=True) for k in range(NEIGH)]
        dy.append(jnp.concatenate(rows, axis=0))
    d_ux = dy[1] + ROOT3 * (uy * dy[4] + uz * dy[7] + ux * dy[8])
    d_uy = dy[2] + ROOT3 * (ux * dy[4] + uz * dy[5] - uy * dy[8])
    d_uz = dy[3] + ROOT3 * (uy * dy[5] + ux * dy[7]) + 3.0 * uz * dy[6]
    along = ux * d_ux + uy * d_uy + uz * d_uz
    inverse = 1.0 / r
    radial = d_r - along * inverse
    pull = [d_ux * inverse + ux * radial, d_uy * inverse + uy * radial, d_uz * inverse + uz * radial]
    high = [p.astype(BF16).astype(F32) for p in pull]
    low = [p - h for p, h in zip(pull, high)]
    zero = jnp.zeros((1, ATOMS), F32)
    step_x, step_y, step_z, outside, lane = decode(code_ref[...], ATOMS // 2)
    spot = outside * 9 + step_y * 3 + step_x + 4
    rows, spots = [], []
    for k in range(NEIGH):
        parts = [h[k : k + 1, :] for h in high] + [zero] + [q[k : k + 1, :] for q in low] + [zero]
        rows.append(jnp.concatenate(parts, axis=0))
        spots.append(jnp.broadcast_to(spot[k : k + 1, :], (8, ATOMS)))
    for c in range(0, CHUNKS, 2):
        for k in range(NEIGH):
            both = [jnp.where(spots[k] == c + i, rows[k], 0.0) for i in range(2)]
            force_ref[c * 8 : c * 8 + 16, k * ATOMS : (k + 1) * ATOMS] = jnp.concatenate(both, axis=0).astype(BF16)
    back = lax.dot_general(
        force_ref[...], lane_ref[...], (((1,), (1,)), ((), ())), preferred_element_type=F32
    )
    center = jnp.concatenate([jnp.sum(p, axis=0, keepdims=True) for p in pull] + [-energy_ref[...]], axis=0)
    if direct:
        outs[0][...] = jnp.zeros(outs[0].shape, F32)
    for c in range(CHUNKS):
        far, dy, dx = c // 9, c % 9 // 3 - 1, c % 3 - 1
        moved = back[8 * c : 8 * c + 4] + back[8 * c + 4 : 8 * c + 8]
        if (far, dy, dx) == (0, 0, 0):
            moved = moved - center
        if direct:
            outs[0][owner_at(dx, dy, far)] = moved
        else:
            outs[far][(0, 2, 1)[dy + 1] * 3 + (0, 2, 1)[dx + 1]] = moved


def finish_kernel(moved_ref, energy_ref, out_ref):
    slots = energy_ref.shape[-1]
    total = jnp.sum(moved_ref[...], axis=0)
    for block in range(2):
        lanes = slice(block * slots, (block + 1) * slots)
        energy_ref[0, 0, block : block + 1, :] = total[3:4, lanes]
        for c in range(3):
            out_ref[0, 0, block : block + 1, c * slots : (c + 1) * slots] = -total[c : c + 1, lanes]


def call(kernel, outs, scratch=(), name=None, limit=24 << 20, place=pltpu.VMEM, cost=None):
    whole = pl.BlockSpec(memory_space=pltpu.VMEM)
    shapes = [jax.ShapeDtypeStruct(shape, kind) for shape, kind in outs]

    def run(*args):
        return pl.pallas_call(
            kernel,
            out_shape=shapes,
            in_specs=[pl.BlockSpec(memory_space=place)] * len(args),
            out_specs=[whole] * len(shapes),
            scratch_shapes=list(scratch),
            compiler_params=pltpu.CompilerParams(vmem_limit_bytes=limit),
            cost_estimate=cost,
            name=name,
        )(*args)

    return run


def on_device(
    positions, species, neighbors, center_table, neighbor_table, radial_weight, mix_weight,
    env_weight, update_weight, second_weight, readout,
):
    slots = species.shape[-1]
    edges = (ATOMS, EDGES)
    square = (ATOMS, ATOMS)
    readout = readout.reshape(1, ATOMS)
    direct = is_direct()
    devices = 32
    (blank,) = call(
        blank_kernel,
        [((8, ATOMS), F32)],
        name="blank",
        cost=pl.CostEstimate(flops=1 << 34, bytes_accessed=64 << 20, transcendentals=0),
    )()
    (packed,) = call(pack_kernel, [((1, 8, ATOMS), F32)], name="pack")(blank, positions, species, neighbors)
    if direct:
        copies = jnp.broadcast_to(packed, (devices, 8, ATOMS))
        tables = [lax.all_to_all(copies, EVERY, 0, 0, tiled=True)]
    else:
        tables, order, _ = gather_halo(packed)
    table, code, edge, dsb, dsl, dse, env, field, geo = call(
        functools.partial(forward_kernel, len(tables), direct),
        [
            ((1,) + square, BF16), ((NEIGH, ATOMS), jnp.int32), (edges, F32), (edges, F32), (edges, F32),
            (edges, F32), (edges, F32), ((9,) + square, F32), ((4, NEIGH, ATOMS), F32),
        ],
        [
            pltpu.VMEM((72, 8, ATOMS), F32), pltpu.VMEM((3 * ATOMS, EDGES), BF16), pltpu.VMEM(edges, F32),
            pltpu.VMEM(square, F32),
        ],
        name="forward",
    )(*tables, center_table, neighbor_table, radial_weight, mix_weight, env_weight, update_weight)
    beside = call(
        functools.partial(onehot_kernel, direct),
        [
            ((CHUNKS * ATOMS, EDGES), BF16), ((EDGES, CHUNKS * ATOMS), BF16), (edges, BF16), (square, BF16),
            (square, F32),
        ],
        [pltpu.VMEM(square, F32)],
        name="onehot",
        cost=pl.CostEstimate(flops=1 << 30, bytes_accessed=8 << 20, transcendentals=0),
    )(code, second_weight, readout)
    tables, order, beside = gather_halo(table, beside)
    gather, scatter, lanes, secondt, rocol = beside
    energy, grad_edge, back_own, back_other = call(
        functools.partial(second_kernel, len(tables), order),
        [((1, ATOMS), F32), (edges, F32), ((9,) + square, BF16), ((9,) + square, BF16)],
        [pltpu.VMEM(edges, F32), pltpu.VMEM(edges, BF16)],
        name="second",
    )(*tables, gather, scatter, edge, second_weight, secondt, rocol)
    owned = reduce_halo(back_own, back_other)
    moved = call(
        functools.partial(backward_kernel, direct),
        [((devices, 4, ATOMS), F32)] if direct else [((9, 4, ATOMS), F32)] * 2,
        [
            pltpu.VMEM((72, 8, ATOMS), F32), pltpu.VMEM((3 * ATOMS, EDGES), BF16), pltpu.VMEM(edges, BF16),
            pltpu.VMEM(edges, F32), pltpu.VMEM((72, 8, ATOMS), F32), pltpu.VMEM((CHUNKS * 8, EDGES), BF16),
        ],
        name="backward",
    )(
        owned, energy, grad_edge, dse, dsl, dsb, env, field, geo, code, lanes, update_weight, env_weight, mix_weight,
        radial_weight,
    )
    moved = lax.all_to_all(moved[0], EVERY, 0, 0, tiled=True) if direct else reduce_halo(*moved)
    return call(finish_kernel, [((1, 1, 2, slots), F32), ((1, 1, 2, 3 * slots), F32)], name="finish")(moved)


def solution(mesh):
    split = P("gx", "gy", "gz", None)
    return jax.shard_map(
        on_device,
        mesh=mesh,
        in_specs=(split, split, split) + (P(),) * 8,
        out_specs=(split, split),
        check_vma=False,
    )
```

```python
import functools
import math

import jax
import jax.numpy as jnp
from jax import lax
from jax.experimental import pallas as pl
from jax.experimental.pallas import tpu as pltpu
from jax.sharding import PartitionSpec as P

NEIGH = 8
ATOMS = 128
EDGES = NEIGH * ATOMS
CHUNKS = 18
CUTOFF = 4.0
SHARPNESS = 2.0
ROOT3 = math.sqrt(3.0)
F32 = jnp.float32
BF16 = jnp.bfloat16
TILE = 1024


RING = (0, 1, 3, 2)
ROUTES = (((1, 0), (0, 2), (1, 2), (2, 1)), ((2, 0), (0, 1), (1, 1), (2, 2)))
EVERY = ("gx", "gy", "gz")


def is_direct():
    return tuple(lax.axis_size(axis) for axis in EVERY) == (4, 4, 2)


def shifted(value, axis, step):
    count = lax.axis_size(axis)
    return lax.ppermute(value, axis, [(i, (i + step) % count) for i in range(count)])


def partner(index, way):
    if way == 0:
        return index
    if way == 1:
        return index ^ 1
    return (index + 2 * (index & 1) - 1) & 3


def number(x, y, core):
    return (x * 4 + y) * 2 + core


def swapped(value, slot):
    pairs = []
    for x in range(4):
        for y in range(4):
            for core in range(2):
                way_x, way_y = ROUTES[core][slot]
                to_x, to_y = partner(x, way_x), partner(y, way_y)
                pairs.append((number(RING[x], RING[y], core), number(RING[to_x], RING[to_y], core)))
    return lax.ppermute(value, EVERY, pairs)


def ring_gather(chunk):
    for axis in ("gx", "gy"):
        lower = shifted(chunk, axis, 1)
        upper = shifted(chunk, axis, -1)
        chunk = jnp.concatenate([lower, upper, chunk], axis=0)
    if lax.axis_size("gz") == 2:
        return [chunk, shifted(chunk, "gz", 1)]
    half = chunk.shape[-1] // 2
    above = shifted(chunk[..., :half], "gz", -1)
    below = shifted(chunk[..., half:], "gz", 1)
    return [chunk, jnp.concatenate([above, below], axis=-1)]


def ring_reduce(own, other):
    kind = own.dtype
    if lax.axis_size("gz") == 2:
        back = shifted(other, "gz", 1)
    else:
        half = other.shape[-1] // 2
        first = shifted(other[..., :half], "gz", 1)
        second = shifted(other[..., half:], "gz", -1)
        back = jnp.concatenate([first, second], axis=-1)
    own = own.astype(F32) + back.astype(F32)
    for axis, size in (("gy", 3), ("gx", 1)):
        lower = shifted(own[:size].astype(kind), axis, -1)
        upper = shifted(own[size : 2 * size].astype(kind), axis, 1)
        own = own[2 * size :] + lower.astype(F32) + upper.astype(F32)
    return own


def ring_at(index):
    return index ^ (index >> 1)


def column_here():
    return ring_at(lax.axis_index("gx")), ring_at(lax.axis_index("gy")), lax.axis_index("gz")


def owner_at(step_x, step_y, outside):
    x, y, core = column_here()
    return number((x + step_x) & 3, (y + step_y) & 3, core ^ outside)


def place_ring(step_x, step_y, outside):
    place_x = jnp.where(step_x == 0, 2, jnp.where(step_x < 0, 0, 1))
    place_y = jnp.where(step_y == 0, 2, jnp.where(step_y < 0, 0, 1))
    return outside * 9 + place_y * 3 + place_x


def place_direct(step_x, step_y, outside, twin):
    x, y, core = column_here()
    way_x = jnp.where(step_x == 0, 0, jnp.where(step_x == 1 - 2 * (x & 1), 1, 2))
    way_y = jnp.where(step_y == 0, 0, jnp.where(step_y == 1 - 2 * (y & 1), 1, 2))
    way = way_x * 3 + way_y
    other = 1 - outside if twin else outside
    chunk = jnp.where(way == 0, -1 if twin else 8 + other, -1)
    for slot in range(4):
        here, there = (ROUTES[mate][slot][0] * 3 + ROUTES[mate][slot][1] for mate in range(2))
        chunk = jnp.where(way == jnp.where(core == 0, here, there), 2 * slot + other, chunk)
    return chunk


def decode(code, slots):
    offset = code >> 6
    slot = code & 63
    step_x = jnp.where(offset >= 18, 1, jnp.where(offset >= 9, 0, -1))
    rest = offset - 9 * (step_x + 1)
    step_y = jnp.where(rest >= 6, 1, jnp.where(rest >= 3, 0, -1))
    step_z = rest - 3 * (step_y + 1) - 1
    block = lax.broadcasted_iota(jnp.int32, (NEIGH, ATOMS), 1) // slots
    level = block + step_z
    outside = jnp.where((level < 0) | (level > 1), 1, 0)
    return step_x, step_y, step_z, outside, (level & 1) * slots + slot


def blank_kernel(out_ref):
    out_ref[...] = jnp.zeros(out_ref.shape, F32)


def pack_kernel(blank_ref, pos_ref, spec_ref, nb_ref, out_ref):
    slots = spec_ref.shape[-1]
    half = nb_ref.shape[-1] // 2
    for block in range(2):
        lanes = slice(block * slots, (block + 1) * slots)
        for c in range(3):
            out_ref[0, c : c + 1, lanes] = pos_ref[0, 0, block : block + 1, c * slots : (c + 1) * slots]
        out_ref[0, 3:4, lanes] = spec_ref[0, 0, block : block + 1, :].astype(F32)
        for part in range(half // ATOMS):
            first = nb_ref[0, 0, block : block + 1, part * ATOMS : (part + 1) * ATOMS]
            second = nb_ref[0, 0, block : block + 1, half + part * ATOMS : half + (part + 1) * ATOMS]
            row = 4 + block * 2 + part
            out_ref[0, row : row + 1, :] = (first * 2048 + second).astype(F32)


def onehot_kernel(direct, *refs):
    codes = [refs[0][...]]
    if direct:
        codes.append(listed_codes(refs[1][owner_at(0, 0, 1)][4:8, :]))
    second_ref, readout_ref, gather_ref, scatter_ref, lane_ref, secondt_ref, rocol_ref, turn_ref = refs[-8:]
    secondt_ref[...] = second_ref[...].astype(F32).T.astype(BF16)
    rocol_ref[...] = jnp.broadcast_to(readout_ref[...], (ATOMS, ATOMS)).T
    down = lax.broadcasted_iota(jnp.int32, (ATOMS, ATOMS), 0).astype(F32).astype(BF16)
    across = lax.broadcasted_iota(jnp.int32, (ATOMS, ATOMS), 1).astype(F32).astype(BF16)
    one = jnp.ones((ATOMS, ATOMS), BF16)
    zero = jnp.zeros((ATOMS, ATOMS), BF16)
    turn_ref[...] = jnp.zeros(turn_ref.shape, F32)
    for twin, code in enumerate(codes):
        step_x, step_y, step_z, outside, lane = decode(code, ATOMS // 2)
        chunk = place_direct(step_x, step_y, outside, twin) if direct else place_ring(step_x, step_y, outside)
        lane, chunk = lane.astype(F32), chunk.astype(F32)
        turn_ref[0:NEIGH, :] = lane
        turn_ref[NEIGH : 2 * NEIGH, :] = chunk
        turned = turn_ref[...].T
        for k in range(NEIGH):
            span = slice((twin * NEIGH + k) * ATOMS, (twin * NEIGH + k + 1) * ATOMS)

            def row(array, k=k):
                return jnp.broadcast_to(array[k : k + 1, :], (ATOMS, ATOMS)).astype(BF16)

            def column(at):
                return jnp.broadcast_to(turned[:, at : at + 1], (ATOMS, ATOMS)).astype(BF16)

            near = jnp.where(row(lane) == down, one, zero)
            near_turned = jnp.where(column(k) == across, one, zero)
            at, at_turned = row(chunk), column(NEIGH + k)
            if not twin:
                lane_ref[:, span] = near
            for c in range(gather_ref.shape[0] // ATOMS):
                part = slice(c * ATOMS, (c + 1) * ATOMS)
                this = jnp.full((ATOMS, ATOMS), c, BF16)
                gather_ref[part, span] = jnp.where(at == this, near, zero)
                scatter_ref[span, part] = jnp.where(at_turned == this, near_turned, zero)


def listed_codes(words):
    words = words.astype(jnp.int32)
    first, second = words >> 11, words & 2047
    width = 4 * ATOMS
    slots = width // NEIGH
    lane = lax.broadcasted_iota(jnp.int32, (NEIGH, width), 1)
    row = lax.broadcasted_iota(jnp.int32, (NEIGH, width), 0)
    mine = (lane & (NEIGH - 1)) == row
    spot = lax.broadcasted_iota(jnp.int32, (width, ATOMS), 0) // NEIGH
    column = lax.broadcasted_iota(jnp.int32, (width, ATOMS), 1)
    total = jnp.zeros((NEIGH, ATOMS), F32)
    for block in range(2):
        pieces = [part[2 * block + i : 2 * block + i + 1, :] for part in (first, second) for i in range(2)]
        listed = jnp.broadcast_to(jnp.concatenate(pieces, axis=1), (NEIGH, width))
        listed = jnp.where(mine, listed, 0)
        high = (listed >> 4).astype(F32).astype(BF16)
        low = (listed & 15).astype(F32).astype(BF16)
        pick = jnp.where(spot + block * slots == column, 1.0, 0.0).astype(BF16)
        total = total + 16.0 * jnp.dot(high, pick, preferred_element_type=F32)
        total = total + jnp.dot(low, pick, preferred_element_type=F32)
    return (total + 0.5).astype(jnp.int32)


def sigmoid(v):
    return 0.5 * jnp.tanh(0.5 * v) + 0.5


def silu_pair(v):
    s = sigmoid(v)
    value = v * s
    return value, s + value * (1.0 - s)


def angular_rows(ux, uy, uz):
    return [
        None, ux, uy, uz, ROOT3 * ux * uy, ROOT3 * uy * uz, 0.5 * (3.0 * uz * uz - 1.0),
        ROOT3 * ux * uz, 0.5 * ROOT3 * (ux * ux - uy * uy),
    ]


def spread_rows(yb_ref, angular):
    for m in range(1, 9):
        for k in range(NEIGH):
            yb_ref[m * NEIGH + k] = jnp.broadcast_to(angular[m][k : k + 1, :], (8, ATOMS))


def basis_parts(r_row):
    row = lax.broadcasted_iota(jnp.int32, (8, ATOMS), 0).astype(F32)
    centers = CUTOFF * (row + 0.5) / 8.0
    r = jnp.broadcast_to(r_row, (8, ATOMS))
    ratio = r * (1.0 / CUTOFF)
    inner = 1.0 - ratio * ratio
    gap = r - centers
    return jnp.exp(-SHARPNESS * gap * gap), gap, inner, ratio


PIECE = (0, 1, 1, 1, 2, 2, 2, 2, 2)


def forward_kernel(parts, direct, *refs):
    tables = refs[:parts]
    (
        center_ref, neighbor_ref, radial_ref, mix_ref, envw_ref, upd_ref,
        table_ref, code_ref, edge_ref, dsb_ref, dsl_ref, dse_ref, env_ref, v_ref, geo_ref,
        yb_ref, inv_ref, lat_ref, pad_ref,
    ) = refs[parts:]
    pad_ref[...] = jnp.zeros(pad_ref.shape, F32)
    pad_ref[0:8, :] = radial_ref[...].astype(F32)
    pad_ref[8 : 8 + neighbor_ref.shape[0], :] = neighbor_ref[...].astype(F32)
    pad_ref[16 : 16 + center_ref.shape[0], :] = center_ref[...].astype(F32)
    wcat = pad_ref[...].T[:, :32].astype(BF16)
    mixt = mix_ref[...].astype(F32).T.astype(BF16)
    envt = envw_ref[...].astype(F32).T.astype(BF16)
    updt = [upd_ref[p * ATOMS : (p + 1) * ATOMS, :].astype(F32).T.astype(BF16) for p in range(3)]
    updt = jnp.concatenate(updt, axis=1)

    def chunk_at(far, dx, dy):
        if direct:
            return tables[0][owner_at(dx, dy, far)]
        return tables[far][(0, 2, 1)[dy + 1] * 3 + (0, 2, 1)[dx + 1]]

    home = chunk_at(0, 0, 0)
    code = listed_codes(home[4:8, :])
    code_ref[...] = code
    step_x, step_y, step_z, outside, lane = decode(code, ATOMS // 2)
    spot = outside * 9 + step_y * 3 + step_x + 4
    found = [jnp.zeros((NEIGH, ATOMS), F32) for _ in range(4)]
    for far in range(2):
        for dy in (-1, 0, 1):
            for dx in (-1, 0, 1):
                hit = spot == far * 9 + dy * 3 + dx + 4
                rows = chunk_at(far, dx, dy)
                for f in range(4):
                    row = jnp.broadcast_to(rows[f : f + 1, :], (NEIGH, ATOMS))
                    found[f] = jnp.where(hit, jnp.take_along_axis(row, lane, axis=1), found[f])
    d = [
        step.astype(F32) + (found[c] - jnp.broadcast_to(home[c : c + 1, :], (NEIGH, ATOMS)))
        for c, step in enumerate((step_x, step_y, step_z))
    ]
    r = jnp.sqrt(d[0] * d[0] + d[1] * d[1] + d[2] * d[2])
    ux, uy, uz = d[0] / r, d[1] / r, d[2] / r
    geo_ref[0] = r
    geo_ref[1] = ux
    geo_ref[2] = uy
    geo_ref[3] = uz
    spread_rows(yb_ref, angular_rows(ux, uy, uz))

    kind = lax.broadcasted_iota(jnp.int32, (8, ATOMS), 0).astype(F32)
    center_hot = jnp.where(jnp.broadcast_to(home[3:4, :], (8, ATOMS)) == kind, 1.0, 0.0)
    zero = jnp.zeros((8, ATOMS), F32)
    columns = []
    for k in range(NEIGH):
        bump, gap, inner, ratio = basis_parts(r[k : k + 1, :])
        other_hot = jnp.where(jnp.broadcast_to(found[3][k : k + 1, :], (8, ATOMS)) == kind, 1.0, 0.0)
        columns.append(jnp.concatenate([bump * (inner * inner), other_hot, center_hot, zero], axis=0).astype(BF16))
    for j in range(EDGES // TILE):
        span = slice(j * TILE, (j + 1) * TILE)
        per = TILE // ATOMS
        x = jnp.concatenate(columns[j * per : (j + 1) * per], axis=1)
        act, ds = silu_pair(jnp.dot(wcat, x, preferred_element_type=F32))
        dsb_ref[:, span] = ds
        latent, ds = silu_pair(jnp.dot(mixt, act.astype(BF16), preferred_element_type=F32))
        dsl_ref[:, span] = ds
        lat_ref[:, span] = latent
        env_ref[:, span] = jnp.dot(envt, latent.astype(BF16), preferred_element_type=F32)
    for t in range(8):
        halves = []
        for h in range(2):
            rows = slice(t * 16 + h * 8, t * 16 + h * 8 + 8)
            env = [env_ref[rows, k * ATOMS : (k + 1) * ATOMS] for k in range(NEIGH)]
            field = []
            for m in range(9):
                terms = [env[k] if m == 0 else env[k] * yb_ref[m * NEIGH + k] for k in range(NEIGH)]
                while len(terms) > 1:
                    terms = [terms[i] + terms[i + 1] for i in range(0, len(terms), 2)]
                field.append(terms[0] * 0.125)
                v_ref[m, rows, :] = field[m]
            out = []
            for k in range(NEIGH):
                sums = [field[0], None, None]
                for m in range(1, 9):
                    term = field[m] * yb_ref[m * NEIGH + k]
                    sums[PIECE[m]] = term if sums[PIECE[m]] is None else sums[PIECE[m]] + term
                out.append(sums)
            halves.append(out)
        for k in range(NEIGH):
            for p in range(3):
                both = jnp.concatenate([halves[0][k][p], halves[1][k][p]], axis=0)
                inv_ref[p * ATOMS + t * 16 : p * ATOMS + t * 16 + 16, k * ATOMS : (k + 1) * ATOMS] = both.astype(BF16)
    mean = jnp.zeros((ATOMS, ATOMS), F32)
    for j in range(EDGES // TILE):
        span = slice(j * TILE, (j + 1) * TILE)
        update = jnp.dot(updt, inv_ref[:, span], preferred_element_type=F32)
        edge, ds = silu_pair(lat_ref[:, span] + update)
        edge_ref[:, span] = edge
        dse_ref[:, span] = ds
        for i in range(TILE // ATOMS):
            mean = mean + edge[:, i * ATOMS : (i + 1) * ATOMS]
    table_ref[0] = (mean * 0.125).astype(BF16)


def second_kernel(parts, order, *refs):
    gather_ref, scatter_ref, second_ref, secondt_ref, rocol_ref = refs[parts : parts + 5]
    sets = gather_ref.shape[1] // EDGES
    edges = refs[parts + 5 : parts + 5 + sets]
    energy_ref, grad_edge_ref, *outs = refs[parts + 5 + sets : -2]
    other_ref, grad_ref = refs[-2:]
    table = jnp.concatenate([refs[array][row] for array, row in order], axis=1)
    rocol = rocol_ref[...]
    other_ref[...] = jnp.dot(table, gather_ref[...], preferred_element_type=F32)
    wide = 2 * ATOMS
    if sets == 2:
        give_ref = outs.pop(0)
        give_ref[ATOMS:, :] = jnp.zeros((8, EDGES), F32)
    for own in range(sets):
        total = jnp.zeros((ATOMS, ATOMS), F32)
        for j in range(EDGES // wide):
            span = slice(j * wide, (j + 1) * wide)
            both = slice(own * EDGES + j * wide, own * EDGES + (j + 1) * wide)
            other = other_ref[:, both]
            edge = edges[own][:, span]
            hidden, ds = silu_pair(
                jnp.dot(secondt_ref[...], (edge * other).astype(BF16), preferred_element_type=F32)
            )
            total = total + hidden[:, :ATOMS] + hidden[:, ATOMS:]
            grad_hidden = ds * jnp.concatenate([rocol, rocol], axis=1)
            grad_prod = jnp.dot(second_ref[...], grad_hidden.astype(BF16), preferred_element_type=F32)
            grad_prod = grad_prod.astype(BF16).astype(F32)
            if own == 0:
                grad_edge_ref[:, span] = grad_prod * other
            else:
                give_ref[:ATOMS, span] = grad_prod * other
            grad_ref[:, both] = (grad_prod * edge).astype(BF16)
        energy = jnp.sum(total * rocol, axis=0, keepdims=True)
        if own == 0:
            energy_ref[...] = energy
        else:
            give_ref[ATOMS : ATOMS + 1, :ATOMS] = energy
    places = [(ref, row) for ref in outs for row in range(ref.shape[0])]
    for c in range(0, len(places), 2):
        back = jnp.dot(grad_ref[...], scatter_ref[:, c * ATOMS : (c + 2) * ATOMS], preferred_element_type=F32)
        for i in range(2):
            ref, row = places[c + i]
            ref[row] = back[:, i * ATOMS : (i + 1) * ATOMS].astype(ref.dtype)


def backward_kernel(
    direct, owned_ref, energy_ref, grad_edge_ref, dse_ref, dsl_ref, dsb_ref, env_ref, v_ref, geo_ref, code_ref, lane_ref,
    upd_ref, envw_ref, mix_ref, radial_ref, *refs,
):
    *extra, yb_ref, dinv_ref, denv_ref, dlat_ref, part_ref, force_ref = refs
    energy = energy_ref[...]
    if direct:
        given_ref, *extra = extra
        energy = energy + given_ref[ATOMS : ATOMS + 1, :ATOMS]
    outs = extra
    r, ux, uy, uz = (geo_ref[i] for i in range(4))
    angular = angular_rows(ux, uy, uz)
    spread_rows(yb_ref, angular)
    share = owned_ref[0] * 0.125
    for j in range(EDGES // TILE):
        span = slice(j * TILE, (j + 1) * TILE)
        d_edge = grad_edge_ref[:, span] + jnp.concatenate([share] * (TILE // ATOMS), axis=1)
        if direct:
            d_edge = d_edge + given_ref[:ATOMS, span]
        d_pre = d_edge * dse_ref[:, span]
        dlat_ref[:, span] = d_pre
        dinv_ref[:, span] = jnp.dot(upd_ref[...], d_pre.astype(BF16), preferred_element_type=F32).astype(BF16)
    part_ref[...] = jnp.zeros(part_ref.shape, F32)
    for t in range(8):
        wide = [
            [
                dinv_ref[p * ATOMS + t * 16 : p * ATOMS + t * 16 + 16, k * ATOMS : (k + 1) * ATOMS].astype(F32)
                for k in range(NEIGH)
            ]
            for p in range(3)
        ]
        halves = []
        for h in range(2):
            rows = slice(t * 16 + h * 8, t * 16 + h * 8 + 8)
            dinv = [[wide[p][k][h * 8 : h * 8 + 8] for k in range(NEIGH)] for p in range(3)]
            env = [env_ref[rows, k * ATOMS : (k + 1) * ATOMS] for k in range(NEIGH)]
            denv = [None] * NEIGH
            for m in range(9):
                down = dinv[PIECE[m]]
                terms = [down[k] if m == 0 else down[k] * yb_ref[m * NEIGH + k] for k in range(NEIGH)]
                while len(terms) > 1:
                    terms = [terms[i] + terms[i + 1] for i in range(0, len(terms), 2)]
                d_field = terms[0] * 0.125
                if m == 0:
                    denv = [d_field] * NEIGH
                    continue
                field = v_ref[m, rows, :]
                for k in range(NEIGH):
                    spot = m * NEIGH + k
                    part_ref[spot] = part_ref[spot] + (down[k] * field + env[k] * d_field)
                    denv[k] = denv[k] + d_field * yb_ref[spot]
            halves.append(denv)
        for k in range(NEIGH):
            both = jnp.concatenate([halves[0][k], halves[1][k]], axis=0)
            denv_ref[t * 16 : t * 16 + 16, k * ATOMS : (k + 1) * ATOMS] = both.astype(BF16)
    d_r_rows = []
    for j in range(EDGES // TILE):
        span = slice(j * TILE, (j + 1) * TILE)
        d_lat = jnp.dot(envw_ref[...], denv_ref[:, span], preferred_element_type=F32).astype(BF16).astype(F32)
        d_mix = (dlat_ref[:, span] + d_lat) * dsl_ref[:, span]
        d_act = jnp.dot(mix_ref[...], d_mix.astype(BF16), preferred_element_type=F32).astype(BF16).astype(F32)
        d_before = (d_act * dsb_ref[:, span]).astype(BF16)
        d_basis = jnp.dot(radial_ref[...], d_before, preferred_element_type=F32).astype(BF16).astype(F32)
        for i in range(TILE // ATOMS):
            k = j * (TILE // ATOMS) + i
            bump, gap, inner, ratio = basis_parts(r[k : k + 1, :])
            slope = bump * inner * (-2.0 * SHARPNESS * gap * inner - (4.0 / CUTOFF) * ratio)
            d_r_rows.append(jnp.sum(slope * d_basis[:, i * ATOMS : (i + 1) * ATOMS], axis=0, keepdims=True))
    d_r = jnp.concatenate(d_r_rows, axis=0)
    dy = [None]
    for m in range(1, 9):
        rows = [jnp.sum(part_ref[m * NEIGH + k], axis=0, keepdims=True) for k in range(NEIGH)]
        dy.append(jnp.concatenate(rows, axis=0))
    d_ux = dy[1] + ROOT3 * (uy * dy[4] + uz * dy[7] + ux * dy[8])
    d_uy = dy[2] + ROOT3 * (ux * dy[4] + uz * dy[5] - uy * dy[8])
    d_uz = dy[3] + ROOT3 * (uy * dy[5] + ux * dy[7]) + 3.0 * uz * dy[6]
    along = ux * d_ux + uy * d_uy + uz * d_uz
    inverse = 1.0 / r
    radial = d_r - along * inverse
    pull = [d_ux * inverse + ux * radial, d_uy * inverse + uy * radial, d_uz * inverse + uz * radial]
    high = [p.astype(BF16).astype(F32) for p in pull]
    low = [p - h for p, h in zip(pull, high)]
    zero = jnp.zeros((1, ATOMS), F32)
    step_x, step_y, step_z, outside, lane = decode(code_ref[...], ATOMS // 2)
    spot = outside * 9 + step_y * 3 + step_x + 4
    rows, spots = [], []
    for k in range(NEIGH):
        parts = [h[k : k + 1, :] for h in high] + [zero] + [q[k : k + 1, :] for q in low] + [zero]
        rows.append(jnp.concatenate(parts, axis=0))
        spots.append(jnp.broadcast_to(spot[k : k + 1, :], (8, ATOMS)))
    for c in range(0, CHUNKS, 2):
        for k in range(NEIGH):
            both = [jnp.where(spots[k] == c + i, rows[k], 0.0) for i in range(2)]
            force_ref[c * 8 : c * 8 + 16, k * ATOMS : (k + 1) * ATOMS] = jnp.concatenate(both, axis=0).astype(BF16)
    back = lax.dot_general(
        force_ref[...], lane_ref[...], (((1,), (1,)), ((), ())), preferred_element_type=F32
    )
    center = jnp.concatenate([jnp.sum(p, axis=0, keepdims=True) for p in pull] + [-energy], axis=0)
    if direct:
        outs[0][...] = jnp.zeros(outs[0].shape, F32)
    for c in range(CHUNKS):
        far, dy, dx = c // 9, c % 9 // 3 - 1, c % 3 - 1
        moved = back[8 * c : 8 * c + 4] + back[8 * c + 4 : 8 * c + 8]
        if (far, dy, dx) == (0, 0, 0):
            moved = moved - center
        if direct:
            outs[0][owner_at(dx, dy, far)] = moved
        else:
            outs[far][(0, 2, 1)[dy + 1] * 3 + (0, 2, 1)[dx + 1]] = moved


def finish_kernel(moved_ref, energy_ref, out_ref):
    slots = energy_ref.shape[-1]
    total = jnp.sum(moved_ref[...], axis=0)
    for block in range(2):
        lanes = slice(block * slots, (block + 1) * slots)
        energy_ref[0, 0, block : block + 1, :] = total[3:4, lanes]
        for c in range(3):
            out_ref[0, 0, block : block + 1, c * slots : (c + 1) * slots] = -total[c : c + 1, lanes]


def call(kernel, outs, scratch=(), name=None, limit=24 << 20, place=pltpu.VMEM, cost=None):
    whole = pl.BlockSpec(memory_space=pltpu.VMEM)
    shapes = [jax.ShapeDtypeStruct(shape, kind) for shape, kind in outs]

    def run(*args):
        return pl.pallas_call(
            kernel,
            out_shape=shapes,
            in_specs=[pl.BlockSpec(memory_space=place)] * len(args),
            out_specs=[whole] * len(shapes),
            scratch_shapes=list(scratch),
            compiler_params=pltpu.CompilerParams(vmem_limit_bytes=limit),
            cost_estimate=cost,
            name=name,
        )(*args)

    return run


def on_device(
    positions, species, neighbors, center_table, neighbor_table, radial_weight, mix_weight,
    env_weight, update_weight, second_weight, readout,
):
    slots = species.shape[-1]
    edges = (ATOMS, EDGES)
    square = (ATOMS, ATOMS)
    readout = readout.reshape(1, ATOMS)
    direct = is_direct()
    devices = 32
    (blank,) = call(
        blank_kernel,
        [((8, ATOMS), F32)],
        name="blank",
        cost=pl.CostEstimate(flops=1 << 34, bytes_accessed=64 << 20, transcendentals=0),
    )()
    (packed,) = call(pack_kernel, [((1, 8, ATOMS), F32)], name="pack")(blank, positions, species, neighbors)
    if direct:
        copies = jnp.broadcast_to(packed, (devices, 8, ATOMS))
        tables = [lax.all_to_all(copies, EVERY, 0, 0, tiled=True)]
    else:
        tables = ring_gather(packed)
    table, code, edge, dsb, dsl, dse, env, field, geo = call(
        functools.partial(forward_kernel, len(tables), direct),
        [
            ((1,) + square, BF16), ((NEIGH, ATOMS), jnp.int32), (edges, F32), (edges, F32), (edges, F32),
            (edges, F32), (edges, F32), ((9,) + square, F32), ((4, NEIGH, ATOMS), F32),
        ],
        [
            pltpu.VMEM((72, 8, ATOMS), F32), pltpu.VMEM((3 * ATOMS, EDGES), BF16), pltpu.VMEM(edges, F32),
            pltpu.VMEM(square, F32),
        ],
        name="forward",
    )(*tables, center_table, neighbor_table, radial_weight, mix_weight, env_weight, update_weight)
    chunks, sets = (10, 2) if direct else (CHUNKS, 1)
    sent = edge
    if direct:
        both = jnp.concatenate([table, shifted(table, "gz", 1)], axis=0)
        both, sent, code = lax.optimization_barrier((both, edge, code))
    gather, scatter, lanes, secondt, rocol = call(
        functools.partial(onehot_kernel, direct),
        [
            ((chunks * ATOMS, sets * EDGES), BF16), ((sets * EDGES, chunks * ATOMS), BF16), (edges, BF16),
            (square, BF16), (square, F32),
        ],
        [pltpu.VMEM(square, F32)],
        name="onehot",
        cost=pl.CostEstimate(flops=1 << 30, bytes_accessed=8 << 20, transcendentals=0),
    )(code, *(tables if direct else ()), second_weight, readout)
    if direct:
        tables = [swapped(both, slot) for slot in range(4)] + [both]
        order = [(array, row) for array in range(5) for row in range(2)]
        latents = [edge, shifted(sent, "gz", 1)]
        returned = [((ATOMS + 8, EDGES), F32)] + [((2,) + square, BF16)] * 4 + [((2,) + square, F32)]
    else:
        tables = ring_gather(table)
        order = [(array, row) for array in range(2) for row in range(9)]
        latents = [edge]
        returned = [((9,) + square, BF16)] * 2
    energy, grad_edge, *returned = call(
        functools.partial(second_kernel, len(tables), order),
        [((1, ATOMS), F32), (edges, F32)] + returned,
        [pltpu.VMEM((ATOMS, sets * EDGES), F32), pltpu.VMEM((ATOMS, sets * EDGES), BF16)],
        name="second",
    )(*tables, gather, scatter, second_weight, secondt, rocol, *latents)
    if direct:
        give, *back, home = returned
        given = [shifted(give, "gz", 1)]
        for slot in range(4):
            home = home + swapped(back[slot], slot).astype(F32)
        owned = home[:1] + shifted(home[1:], "gz", 1)
    else:
        given = []
        owned = ring_reduce(*returned)
    moved = call(
        functools.partial(backward_kernel, direct),
        [((devices, 4, ATOMS), F32)] if direct else [((9, 4, ATOMS), F32)] * 2,
        [
            pltpu.VMEM((72, 8, ATOMS), F32), pltpu.VMEM((3 * ATOMS, EDGES), BF16), pltpu.VMEM(edges, BF16),
            pltpu.VMEM(edges, F32), pltpu.VMEM((72, 8, ATOMS), F32), pltpu.VMEM((CHUNKS * 8, EDGES), BF16),
        ],
        name="backward",
    )(
        owned, energy, grad_edge, dse, dsl, dsb, env, field, geo, code, lanes, update_weight, env_weight, mix_weight,
        radial_weight, *given,
    )
    moved = lax.all_to_all(moved[0], EVERY, 0, 0, tiled=True) if direct else ring_reduce(*moved)
    return call(finish_kernel, [((1, 1, 2, slots), F32), ((1, 1, 2, 3 * slots), F32)], name="finish")(moved)


def solution(mesh):
    split = P("gx", "gy", "gz", None)
    return jax.shard_map(
        on_device,
        mesh=mesh,
        in_specs=(split, split, split) + (P(),) * 8,
        out_specs=(split, split),
        check_vma=False,
    )
```

```python
import functools
import math

import jax
import jax.numpy as jnp
from jax import lax
from jax.experimental import pallas as pl
from jax.experimental.pallas import tpu as pltpu
from jax.sharding import PartitionSpec as P

NEIGH = 8
ATOMS = 128
EDGES = NEIGH * ATOMS
CHUNKS = 18
CUTOFF = 4.0
SHARPNESS = 2.0
ROOT3 = math.sqrt(3.0)
F32 = jnp.float32
BF16 = jnp.bfloat16
TILE = 1024


RING = (0, 1, 3, 2)
ROUTES = (((0, 1), (1, 0), (1, 2), (2, 2)), ((0, 2), (2, 0), (1, 1), (2, 1)))
EVERY = ("gx", "gy", "gz")


def is_direct():
    return tuple(lax.axis_size(axis) for axis in EVERY) == (4, 4, 2)


def shifted(value, axis, step):
    count = lax.axis_size(axis)
    return lax.ppermute(value, axis, [(i, (i + step) % count) for i in range(count)])


def partner(index, way):
    if way == 0:
        return index
    if way == 1:
        return index ^ 1
    return (index + 2 * (index & 1) - 1) & 3


def number(x, y, core):
    return (x * 4 + y) * 2 + core


def swapped(value, slot):
    pairs = []
    for x in range(4):
        for y in range(4):
            for core in range(2):
                way_x, way_y = ROUTES[core][slot]
                to_x, to_y = partner(x, way_x), partner(y, way_y)
                pairs.append((number(RING[x], RING[y], core), number(RING[to_x], RING[to_y], core)))
    return lax.ppermute(value, EVERY, pairs)


def ring_gather(chunk):
    for axis in ("gx", "gy"):
        lower = shifted(chunk, axis, 1)
        upper = shifted(chunk, axis, -1)
        chunk = jnp.concatenate([lower, upper, chunk], axis=0)
    if lax.axis_size("gz") == 2:
        return [chunk, shifted(chunk, "gz", 1)]
    half = chunk.shape[-1] // 2
    above = shifted(chunk[..., :half], "gz", -1)
    below = shifted(chunk[..., half:], "gz", 1)
    return [chunk, jnp.concatenate([above, below], axis=-1)]


def ring_reduce(own, other):
    kind = own.dtype
    if lax.axis_size("gz") == 2:
        back = shifted(other, "gz", 1)
    else:
        half = other.shape[-1] // 2
        first = shifted(other[..., :half], "gz", 1)
        second = shifted(other[..., half:], "gz", -1)
        back = jnp.concatenate([first, second], axis=-1)
    own = own.astype(F32) + back.astype(F32)
    for axis, size in (("gy", 3), ("gx", 1)):
        lower = shifted(own[:size].astype(kind), axis, -1)
        upper = shifted(own[size : 2 * size].astype(kind), axis, 1)
        own = own[2 * size :] + lower.astype(F32) + upper.astype(F32)
    return own


def ring_at(index):
    return index ^ (index >> 1)


def column_here():
    return ring_at(lax.axis_index("gx")), ring_at(lax.axis_index("gy")), lax.axis_index("gz")


def owner_at(step_x, step_y, outside):
    x, y, core = column_here()
    return number((x + step_x) & 3, (y + step_y) & 3, core ^ outside)


def place_ring(step_x, step_y, outside):
    place_x = jnp.where(step_x == 0, 2, jnp.where(step_x < 0, 0, 1))
    place_y = jnp.where(step_y == 0, 2, jnp.where(step_y < 0, 0, 1))
    return outside * 9 + place_y * 3 + place_x


def place_direct(step_x, step_y, outside, twin):
    x, y, core = column_here()
    way_x = jnp.where(step_x == 0, 0, jnp.where(step_x == 1 - 2 * (x & 1), 1, 2))
    way_y = jnp.where(step_y == 0, 0, jnp.where(step_y == 1 - 2 * (y & 1), 1, 2))
    way = way_x * 3 + way_y
    other = 1 - outside if twin else outside
    chunk = jnp.where(way == 0, -1 if twin else 8 + other, -1)
    for slot in range(4):
        here, there = (ROUTES[mate][slot][0] * 3 + ROUTES[mate][slot][1] for mate in range(2))
        chunk = jnp.where(way == jnp.where(core == 0, here, there), 2 * slot + other, chunk)
    return chunk


def decode(code, slots):
    offset = code >> 6
    slot = code & 63
    step_x = jnp.where(offset >= 18, 1, jnp.where(offset >= 9, 0, -1))
    rest = offset - 9 * (step_x + 1)
    step_y = jnp.where(rest >= 6, 1, jnp.where(rest >= 3, 0, -1))
    step_z = rest - 3 * (step_y + 1) - 1
    block = lax.broadcasted_iota(jnp.int32, (NEIGH, ATOMS), 1) // slots
    level = block + step_z
    outside = jnp.where((level < 0) | (level > 1), 1, 0)
    return step_x, step_y, step_z, outside, (level & 1) * slots + slot


def blank_kernel(out_ref):
    out_ref[...] = jnp.zeros(out_ref.shape, F32)


def pack_kernel(blank_ref, pos_ref, spec_ref, nb_ref, out_ref):
    slots = spec_ref.shape[-1]
    half = nb_ref.shape[-1] // 2
    for block in range(2):
        lanes = slice(block * slots, (block + 1) * slots)
        for c in range(3):
            out_ref[0, c : c + 1, lanes] = pos_ref[0, 0, block : block + 1, c * slots : (c + 1) * slots]
        out_ref[0, 3:4, lanes] = spec_ref[0, 0, block : block + 1, :].astype(F32)
        for part in range(half // ATOMS):
            first = nb_ref[0, 0, block : block + 1, part * ATOMS : (part + 1) * ATOMS]
            second = nb_ref[0, 0, block : block + 1, half + part * ATOMS : half + (part + 1) * ATOMS]
            row = 4 + block * 2 + part
            out_ref[0, row : row + 1, :] = (first * 2048 + second).astype(F32)


def onehot_kernel(direct, *refs):
    codes = [refs[0][...]]
    if direct:
        codes.append(listed_codes(refs[1][owner_at(0, 0, 1)][4:8, :]))
    second_ref, readout_ref, gather_ref, scatter_ref, lane_ref, secondt_ref, rocol_ref, turn_ref = refs[-8:]
    secondt_ref[...] = second_ref[...].astype(F32).T.astype(BF16)
    rocol_ref[...] = jnp.broadcast_to(readout_ref[...], (ATOMS, ATOMS)).T
    down = lax.broadcasted_iota(jnp.int32, (ATOMS, ATOMS), 0).astype(F32).astype(BF16)
    across = lax.broadcasted_iota(jnp.int32, (ATOMS, ATOMS), 1).astype(F32).astype(BF16)
    one = jnp.ones((ATOMS, ATOMS), BF16)
    zero = jnp.zeros((ATOMS, ATOMS), BF16)
    turn_ref[...] = jnp.zeros(turn_ref.shape, F32)
    for twin, code in enumerate(codes):
        step_x, step_y, step_z, outside, lane = decode(code, ATOMS // 2)
        chunk = place_direct(step_x, step_y, outside, twin) if direct else place_ring(step_x, step_y, outside)
        lane, chunk = lane.astype(F32), chunk.astype(F32)
        turn_ref[0:NEIGH, :] = lane
        turn_ref[NEIGH : 2 * NEIGH, :] = chunk
        turned = turn_ref[...].T
        for k in range(NEIGH):
            span = slice((twin * NEIGH + k) * ATOMS, (twin * NEIGH + k + 1) * ATOMS)

            def row(array, k=k):
                return jnp.broadcast_to(array[k : k + 1, :], (ATOMS, ATOMS)).astype(BF16)

            def column(at):
                return jnp.broadcast_to(turned[:, at : at + 1], (ATOMS, ATOMS)).astype(BF16)

            near = jnp.where(row(lane) == down, one, zero)
            near_turned = jnp.where(column(k) == across, one, zero)
            at, at_turned = row(chunk), column(NEIGH + k)
            if not twin:
                lane_ref[:, span] = near
            for c in range(gather_ref.shape[0] // ATOMS):
                part = slice(c * ATOMS, (c + 1) * ATOMS)
                this = jnp.full((ATOMS, ATOMS), c, BF16)
                gather_ref[part, span] = jnp.where(at == this, near, zero)
                scatter_ref[span, part] = jnp.where(at_turned == this, near_turned, zero)


def listed_codes(words):
    words = words.astype(jnp.int32)
    first, second = words >> 11, words & 2047
    width = 4 * ATOMS
    slots = width // NEIGH
    lane = lax.broadcasted_iota(jnp.int32, (NEIGH, width), 1)
    row = lax.broadcasted_iota(jnp.int32, (NEIGH, width), 0)
    mine = (lane & (NEIGH - 1)) == row
    spot = lax.broadcasted_iota(jnp.int32, (width, ATOMS), 0) // NEIGH
    column = lax.broadcasted_iota(jnp.int32, (width, ATOMS), 1)
    total = jnp.zeros((NEIGH, ATOMS), F32)
    for block in range(2):
        pieces = [part[2 * block + i : 2 * block + i + 1, :] for part in (first, second) for i in range(2)]
        listed = jnp.broadcast_to(jnp.concatenate(pieces, axis=1), (NEIGH, width))
        listed = jnp.where(mine, listed, 0)
        high = (listed >> 4).astype(F32).astype(BF16)
        low = (listed & 15).astype(F32).astype(BF16)
        pick = jnp.where(spot + block * slots == column, 1.0, 0.0).astype(BF16)
        total = total + 16.0 * jnp.dot(high, pick, preferred_element_type=F32)
        total = total + jnp.dot(low, pick, preferred_element_type=F32)
    return (total + 0.5).astype(jnp.int32)


def sigmoid(v):
    return 0.5 * jnp.tanh(0.5 * v) + 0.5


def silu_pair(v):
    s = sigmoid(v)
    value = v * s
    return value, s + value * (1.0 - s)


def angular_rows(ux, uy, uz):
    return [
        None, ux, uy, uz, ROOT3 * ux * uy, ROOT3 * uy * uz, 0.5 * (3.0 * uz * uz - 1.0),
        ROOT3 * ux * uz, 0.5 * ROOT3 * (ux * ux - uy * uy),
    ]


def spread_rows(yb_ref, angular):
    for m in range(1, 9):
        for k in range(NEIGH):
            yb_ref[m * NEIGH + k] = jnp.broadcast_to(angular[m][k : k + 1, :], (8, ATOMS))


def basis_parts(r_row):
    row = lax.broadcasted_iota(jnp.int32, (8, ATOMS), 0).astype(F32)
    centers = CUTOFF * (row + 0.5) / 8.0
    r = jnp.broadcast_to(r_row, (8, ATOMS))
    ratio = r * (1.0 / CUTOFF)
    inner = 1.0 - ratio * ratio
    gap = r - centers
    return jnp.exp(-SHARPNESS * gap * gap), gap, inner, ratio


PIECE = (0, 1, 1, 1, 2, 2, 2, 2, 2)


def forward_kernel(parts, direct, *refs):
    tables = refs[:parts]
    (
        center_ref, neighbor_ref, radial_ref, mix_ref, envw_ref, upd_ref,
        table_ref, code_ref, edge_ref, dsb_ref, dsl_ref, dse_ref, env_ref, v_ref, geo_ref,
        yb_ref, inv_ref, lat_ref, pad_ref,
    ) = refs[parts:]
    pad_ref[...] = jnp.zeros(pad_ref.shape, F32)
    pad_ref[0:8, :] = radial_ref[...].astype(F32)
    pad_ref[8 : 8 + neighbor_ref.shape[0], :] = neighbor_ref[...].astype(F32)
    pad_ref[16 : 16 + center_ref.shape[0], :] = center_ref[...].astype(F32)
    wcat = pad_ref[...].T[:, :32].astype(BF16)
    mixt = mix_ref[...].astype(F32).T.astype(BF16)
    envt = envw_ref[...].astype(F32).T.astype(BF16)
    updt = [upd_ref[p * ATOMS : (p + 1) * ATOMS, :].astype(F32).T.astype(BF16) for p in range(3)]
    updt = jnp.concatenate(updt, axis=1)

    def chunk_at(far, dx, dy):
        if direct:
            return tables[0][owner_at(dx, dy, far)]
        return tables[far][(0, 2, 1)[dy + 1] * 3 + (0, 2, 1)[dx + 1]]

    home = chunk_at(0, 0, 0)
    code = listed_codes(home[4:8, :])
    code_ref[...] = code
    step_x, step_y, step_z, outside, lane = decode(code, ATOMS // 2)
    spot = outside * 9 + step_y * 3 + step_x + 4
    found = [jnp.zeros((NEIGH, ATOMS), F32) for _ in range(4)]
    for far in range(2):
        for dy in (-1, 0, 1):
            for dx in (-1, 0, 1):
                hit = spot == far * 9 + dy * 3 + dx + 4
                rows = chunk_at(far, dx, dy)
                for f in range(4):
                    row = jnp.broadcast_to(rows[f : f + 1, :], (NEIGH, ATOMS))
                    found[f] = jnp.where(hit, jnp.take_along_axis(row, lane, axis=1), found[f])
    d = [
        step.astype(F32) + (found[c] - jnp.broadcast_to(home[c : c + 1, :], (NEIGH, ATOMS)))
        for c, step in enumerate((step_x, step_y, step_z))
    ]
    r = jnp.sqrt(d[0] * d[0] + d[1] * d[1] + d[2] * d[2])
    ux, uy, uz = d[0] / r, d[1] / r, d[2] / r
    geo_ref[0] = r
    geo_ref[1] = ux
    geo_ref[2] = uy
    geo_ref[3] = uz
    spread_rows(yb_ref, angular_rows(ux, uy, uz))

    kind = lax.broadcasted_iota(jnp.int32, (8, ATOMS), 0).astype(F32)
    center_hot = jnp.where(jnp.broadcast_to(home[3:4, :], (8, ATOMS)) == kind, 1.0, 0.0)
    zero = jnp.zeros((8, ATOMS), F32)
    columns = []
    for k in range(NEIGH):
        bump, gap, inner, ratio = basis_parts(r[k : k + 1, :])
        other_hot = jnp.where(jnp.broadcast_to(found[3][k : k + 1, :], (8, ATOMS)) == kind, 1.0, 0.0)
        columns.append(jnp.concatenate([bump * (inner * inner), other_hot, center_hot, zero], axis=0).astype(BF16))
    for j in range(EDGES // TILE):
        span = slice(j * TILE, (j + 1) * TILE)
        per = TILE // ATOMS
        x = jnp.concatenate(columns[j * per : (j + 1) * per], axis=1)
        act, ds = silu_pair(jnp.dot(wcat, x, preferred_element_type=F32))
        dsb_ref[:, span] = ds
        latent, ds = silu_pair(jnp.dot(mixt, act.astype(BF16), preferred_element_type=F32))
        dsl_ref[:, span] = ds
        lat_ref[:, span] = latent
        env_ref[:, span] = jnp.dot(envt, latent.astype(BF16), preferred_element_type=F32)
    for t in range(8):
        halves = []
        for h in range(2):
            rows = slice(t * 16 + h * 8, t * 16 + h * 8 + 8)
            env = [env_ref[rows, k * ATOMS : (k + 1) * ATOMS] for k in range(NEIGH)]
            field = []
            for m in range(9):
                terms = [env[k] if m == 0 else env[k] * yb_ref[m * NEIGH + k] for k in range(NEIGH)]
                while len(terms) > 1:
                    terms = [terms[i] + terms[i + 1] for i in range(0, len(terms), 2)]
                field.append(terms[0] * 0.125)
                v_ref[m, rows, :] = field[m]
            out = []
            for k in range(NEIGH):
                sums = [field[0], None, None]
                for m in range(1, 9):
                    term = field[m] * yb_ref[m * NEIGH + k]
                    sums[PIECE[m]] = term if sums[PIECE[m]] is None else sums[PIECE[m]] + term
                out.append(sums)
            halves.append(out)
        for k in range(NEIGH):
            for p in range(3):
                both = jnp.concatenate([halves[0][k][p], halves[1][k][p]], axis=0)
                inv_ref[p * ATOMS + t * 16 : p * ATOMS + t * 16 + 16, k * ATOMS : (k + 1) * ATOMS] = both.astype(BF16)
    mean = jnp.zeros((ATOMS, ATOMS), F32)
    for j in range(EDGES // TILE):
        span = slice(j * TILE, (j + 1) * TILE)
        update = jnp.dot(updt, inv_ref[:, span], preferred_element_type=F32)
        edge, ds = silu_pair(lat_ref[:, span] + update)
        edge_ref[:, span] = edge
        dse_ref[:, span] = ds
        for i in range(TILE // ATOMS):
            mean = mean + edge[:, i * ATOMS : (i + 1) * ATOMS]
    table_ref[0] = (mean * 0.125).astype(BF16)


def second_kernel(parts, order, *refs):
    gather_ref, scatter_ref, second_ref, secondt_ref, rocol_ref = refs[parts : parts + 5]
    sets = gather_ref.shape[1] // EDGES
    edges = refs[parts + 5 : parts + 5 + sets]
    energy_ref, grad_edge_ref, *outs = refs[parts + 5 + sets : -2]
    other_ref, grad_ref = refs[-2:]
    table = jnp.concatenate([refs[array][row] for array, row in order], axis=1)
    rocol = rocol_ref[...]
    other_ref[...] = jnp.dot(table, gather_ref[...], preferred_element_type=F32)
    wide = 2 * ATOMS
    if sets == 2:
        give_ref = outs.pop(0)
        give_ref[ATOMS:, :] = jnp.zeros((8, EDGES), F32)
    for own in range(sets):
        total = jnp.zeros((ATOMS, ATOMS), F32)
        for j in range(EDGES // wide):
            span = slice(j * wide, (j + 1) * wide)
            both = slice(own * EDGES + j * wide, own * EDGES + (j + 1) * wide)
            other = other_ref[:, both]
            edge = edges[own][:, span]
            hidden, ds = silu_pair(
                jnp.dot(secondt_ref[...], (edge * other).astype(BF16), preferred_element_type=F32)
            )
            total = total + hidden[:, :ATOMS] + hidden[:, ATOMS:]
            grad_hidden = ds * jnp.concatenate([rocol, rocol], axis=1)
            grad_prod = jnp.dot(second_ref[...], grad_hidden.astype(BF16), preferred_element_type=F32)
            grad_prod = grad_prod.astype(BF16).astype(F32)
            if own == 0:
                grad_edge_ref[:, span] = grad_prod * other
            else:
                give_ref[:ATOMS, span] = grad_prod * other
            grad_ref[:, both] = (grad_prod * edge).astype(BF16)
        energy = jnp.sum(total * rocol, axis=0, keepdims=True)
        if own == 0:
            energy_ref[...] = energy
        else:
            give_ref[ATOMS : ATOMS + 1, :ATOMS] = energy
    places = [(ref, row) for ref in outs for row in range(ref.shape[0])]
    for c in range(0, len(places), 2):
        back = jnp.dot(grad_ref[...], scatter_ref[:, c * ATOMS : (c + 2) * ATOMS], preferred_element_type=F32)
        for i in range(2):
            ref, row = places[c + i]
            ref[row] = back[:, i * ATOMS : (i + 1) * ATOMS].astype(ref.dtype)


def backward_kernel(
    direct, owned_ref, energy_ref, grad_edge_ref, dse_ref, dsl_ref, dsb_ref, env_ref, v_ref, geo_ref, code_ref, lane_ref,
    upd_ref, envw_ref, mix_ref, radial_ref, *refs,
):
    *extra, yb_ref, dinv_ref, denv_ref, dlat_ref, part_ref, force_ref = refs
    energy = energy_ref[...]
    if direct:
        given_ref, *extra = extra
        energy = energy + given_ref[ATOMS : ATOMS + 1, :ATOMS]
    outs = extra
    r, ux, uy, uz = (geo_ref[i] for i in range(4))
    angular = angular_rows(ux, uy, uz)
    spread_rows(yb_ref, angular)
    share = owned_ref[0] * 0.125
    for j in range(EDGES // TILE):
        span = slice(j * TILE, (j + 1) * TILE)
        d_edge = grad_edge_ref[:, span] + jnp.concatenate([share] * (TILE // ATOMS), axis=1)
        if direct:
            d_edge = d_edge + given_ref[:ATOMS, span]
        d_pre = d_edge * dse_ref[:, span]
        dlat_ref[:, span] = d_pre
        dinv_ref[:, span] = jnp.dot(upd_ref[...], d_pre.astype(BF16), preferred_element_type=F32).astype(BF16)
    part_ref[...] = jnp.zeros(part_ref.shape, F32)
    for t in range(8):
        wide = [
            [
                dinv_ref[p * ATOMS + t * 16 : p * ATOMS + t * 16 + 16, k * ATOMS : (k + 1) * ATOMS].astype(F32)
                for k in range(NEIGH)
            ]
            for p in range(3)
        ]
        halves = []
        for h in range(2):
            rows = slice(t * 16 + h * 8, t * 16 + h * 8 + 8)
            dinv = [[wide[p][k][h * 8 : h * 8 + 8] for k in range(NEIGH)] for p in range(3)]
            env = [env_ref[rows, k * ATOMS : (k + 1) * ATOMS] for k in range(NEIGH)]
            denv = [None] * NEIGH
            for m in range(9):
                down = dinv[PIECE[m]]
                terms = [down[k] if m == 0 else down[k] * yb_ref[m * NEIGH + k] for k in range(NEIGH)]
                while len(terms) > 1:
                    terms = [terms[i] + terms[i + 1] for i in range(0, len(terms), 2)]
                d_field = terms[0] * 0.125
                if m == 0:
                    denv = [d_field] * NEIGH
                    continue
                field = v_ref[m, rows, :]
                for k in range(NEIGH):
                    spot = m * NEIGH + k
                    part_ref[spot] = part_ref[spot] + (down[k] * field + env[k] * d_field)
                    denv[k] = denv[k] + d_field * yb_ref[spot]
            halves.append(denv)
        for k in range(NEIGH):
            both = jnp.concatenate([halves[0][k], halves[1][k]], axis=0)
            denv_ref[t * 16 : t * 16 + 16, k * ATOMS : (k + 1) * ATOMS] = both.astype(BF16)
    d_r_rows = []
    for j in range(EDGES // TILE):
        span = slice(j * TILE, (j + 1) * TILE)
        d_lat = jnp.dot(envw_ref[...], denv_ref[:, span], preferred_element_type=F32).astype(BF16).astype(F32)
        d_mix = (dlat_ref[:, span] + d_lat) * dsl_ref[:, span]
        d_act = jnp.dot(mix_ref[...], d_mix.astype(BF16), preferred_element_type=F32).astype(BF16).astype(F32)
        d_before = (d_act * dsb_ref[:, span]).astype(BF16)
        d_basis = jnp.dot(radial_ref[...], d_before, preferred_element_type=F32).astype(BF16).astype(F32)
        for i in range(TILE // ATOMS):
            k = j * (TILE // ATOMS) + i
            bump, gap, inner, ratio = basis_parts(r[k : k + 1, :])
            slope = bump * inner * (-2.0 * SHARPNESS * gap * inner - (4.0 / CUTOFF) * ratio)
            d_r_rows.append(jnp.sum(slope * d_basis[:, i * ATOMS : (i + 1) * ATOMS], axis=0, keepdims=True))
    d_r = jnp.concatenate(d_r_rows, axis=0)
    dy = [None]
    for m in range(1, 9):
        rows = [jnp.sum(part_ref[m * NEIGH + k], axis=0, keepdims=True) for k in range(NEIGH)]
        dy.append(jnp.concatenate(rows, axis=0))
    d_ux = dy[1] + ROOT3 * (uy * dy[4] + uz * dy[7] + ux * dy[8])
    d_uy = dy[2] + ROOT3 * (ux * dy[4] + uz * dy[5] - uy * dy[8])
    d_uz = dy[3] + ROOT3 * (uy * dy[5] + ux * dy[7]) + 3.0 * uz * dy[6]
    along = ux * d_ux + uy * d_uy + uz * d_uz
    inverse = 1.0 / r
    radial = d_r - along * inverse
    pull = [d_ux * inverse + ux * radial, d_uy * inverse + uy * radial, d_uz * inverse + uz * radial]
    high = [p.astype(BF16).astype(F32) for p in pull]
    low = [p - h for p, h in zip(pull, high)]
    zero = jnp.zeros((1, ATOMS), F32)
    step_x, step_y, step_z, outside, lane = decode(code_ref[...], ATOMS // 2)
    spot = outside * 9 + step_y * 3 + step_x + 4
    rows, spots = [], []
    for k in range(NEIGH):
        parts = [h[k : k + 1, :] for h in high] + [zero] + [q[k : k + 1, :] for q in low] + [zero]
        rows.append(jnp.concatenate(parts, axis=0))
        spots.append(jnp.broadcast_to(spot[k : k + 1, :], (8, ATOMS)))
    for c in range(0, CHUNKS, 2):
        for k in range(NEIGH):
            both = [jnp.where(spots[k] == c + i, rows[k], 0.0) for i in range(2)]
            force_ref[c * 8 : c * 8 + 16, k * ATOMS : (k + 1) * ATOMS] = jnp.concatenate(both, axis=0).astype(BF16)
    back = lax.dot_general(
        force_ref[...], lane_ref[...], (((1,), (1,)), ((), ())), preferred_element_type=F32
    )
    center = jnp.concatenate([jnp.sum(p, axis=0, keepdims=True) for p in pull] + [-energy], axis=0)
    if direct:
        outs[0][...] = jnp.zeros(outs[0].shape, F32)
    for c in range(CHUNKS):
        far, dy, dx = c // 9, c % 9 // 3 - 1, c % 3 - 1
        moved = back[8 * c : 8 * c + 4] + back[8 * c + 4 : 8 * c + 8]
        if (far, dy, dx) == (0, 0, 0):
            moved = moved - center
        if direct:
            outs[0][owner_at(dx, dy, far)] = moved
        else:
            outs[far][(0, 2, 1)[dy + 1] * 3 + (0, 2, 1)[dx + 1]] = moved


def finish_kernel(moved_ref, energy_ref, out_ref):
    slots = energy_ref.shape[-1]
    total = jnp.sum(moved_ref[...], axis=0)
    for block in range(2):
        lanes = slice(block * slots, (block + 1) * slots)
        energy_ref[0, 0, block : block + 1, :] = total[3:4, lanes]
        for c in range(3):
            out_ref[0, 0, block : block + 1, c * slots : (c + 1) * slots] = -total[c : c + 1, lanes]


def call(kernel, outs, scratch=(), name=None, limit=24 << 20, place=pltpu.VMEM, cost=None):
    whole = pl.BlockSpec(memory_space=pltpu.VMEM)
    shapes = [jax.ShapeDtypeStruct(shape, kind) for shape, kind in outs]

    def run(*args):
        return pl.pallas_call(
            kernel,
            out_shape=shapes,
            in_specs=[pl.BlockSpec(memory_space=place)] * len(args),
            out_specs=[whole] * len(shapes),
            scratch_shapes=list(scratch),
            compiler_params=pltpu.CompilerParams(vmem_limit_bytes=limit),
            cost_estimate=cost,
            name=name,
        )(*args)

    return run


def on_device(
    positions, species, neighbors, center_table, neighbor_table, radial_weight, mix_weight,
    env_weight, update_weight, second_weight, readout,
):
    slots = species.shape[-1]
    edges = (ATOMS, EDGES)
    square = (ATOMS, ATOMS)
    readout = readout.reshape(1, ATOMS)
    direct = is_direct()
    devices = 32
    (blank,) = call(
        blank_kernel,
        [((8, ATOMS), F32)],
        name="blank",
        cost=pl.CostEstimate(flops=1 << 34, bytes_accessed=64 << 20, transcendentals=0),
    )()
    (packed,) = call(pack_kernel, [((1, 8, ATOMS), F32)], name="pack")(blank, positions, species, neighbors)
    if direct:
        copies = jnp.broadcast_to(packed, (devices, 8, ATOMS))
        tables = [lax.all_to_all(copies, EVERY, 0, 0, tiled=True)]
    else:
        tables = ring_gather(packed)
    table, code, edge, dsb, dsl, dse, env, field, geo = call(
        functools.partial(forward_kernel, len(tables), direct),
        [
            ((1,) + square, BF16), ((NEIGH, ATOMS), jnp.int32), (edges, F32), (edges, F32), (edges, F32),
            (edges, F32), (edges, F32), ((9,) + square, F32), ((4, NEIGH, ATOMS), F32),
        ],
        [
            pltpu.VMEM((72, 8, ATOMS), F32), pltpu.VMEM((3 * ATOMS, EDGES), BF16), pltpu.VMEM(edges, F32),
            pltpu.VMEM(square, F32),
        ],
        name="forward",
    )(*tables, center_table, neighbor_table, radial_weight, mix_weight, env_weight, update_weight)
    chunks, sets = (10, 2) if direct else (CHUNKS, 1)
    sent = edge
    if direct:
        both = jnp.concatenate([table, shifted(table, "gz", 1)], axis=0)
        both, sent, code = lax.optimization_barrier((both, edge, code))
    gather, scatter, lanes, secondt, rocol = call(
        functools.partial(onehot_kernel, direct),
        [
            ((chunks * ATOMS, sets * EDGES), BF16), ((sets * EDGES, chunks * ATOMS), BF16), (edges, BF16),
            (square, BF16), (square, F32),
        ],
        [pltpu.VMEM(square, F32)],
        name="onehot",
        cost=pl.CostEstimate(flops=1 << 30, bytes_accessed=8 << 20, transcendentals=0),
    )(code, *(tables if direct else ()), second_weight, readout)
    if direct:
        tables = [swapped(both, slot) for slot in range(4)] + [both]
        order = [(array, row) for array in range(5) for row in range(2)]
        latents = [edge, shifted(sent, "gz", 1)]
        returned = [((ATOMS + 8, EDGES), F32)] + [((2,) + square, BF16)] * 4 + [((2,) + square, F32)]
    else:
        tables = ring_gather(table)
        order = [(array, row) for array in range(2) for row in range(9)]
        latents = [edge]
        returned = [((9,) + square, BF16)] * 2
    energy, grad_edge, *returned = call(
        functools.partial(second_kernel, len(tables), order),
        [((1, ATOMS), F32), (edges, F32)] + returned,
        [pltpu.VMEM((ATOMS, sets * EDGES), F32), pltpu.VMEM((ATOMS, sets * EDGES), BF16)],
        name="second",
    )(*tables, gather, scatter, second_weight, secondt, rocol, *latents)
    if direct:
        give, *back, home = returned
        given = [shifted(give, "gz", 1)]
        for slot in (3, 2, 1, 0):
            home = home + swapped(back[slot], slot).astype(F32)
        owned = home[:1] + shifted(home[1:], "gz", 1)
    else:
        given = []
        owned = ring_reduce(*returned)
    moved = call(
        functools.partial(backward_kernel, direct),
        [((devices, 4, ATOMS), F32)] if direct else [((9, 4, ATOMS), F32)] * 2,
        [
            pltpu.VMEM((72, 8, ATOMS), F32), pltpu.VMEM((3 * ATOMS, EDGES), BF16), pltpu.VMEM(edges, BF16),
            pltpu.VMEM(edges, F32), pltpu.VMEM((72, 8, ATOMS), F32), pltpu.VMEM((CHUNKS * 8, EDGES), BF16),
        ],
        name="backward",
    )(
        owned, energy, grad_edge, dse, dsl, dsb, env, field, geo, code, lanes, update_weight, env_weight, mix_weight,
        radial_weight, *given,
    )
    moved = lax.all_to_all(moved[0], EVERY, 0, 0, tiled=True) if direct else ring_reduce(*moved)
    return call(finish_kernel, [((1, 1, 2, slots), F32), ((1, 1, 2, 3 * slots), F32)], name="finish")(moved)


def solution(mesh):
    split = P("gx", "gy", "gz", None)
    return jax.shard_map(
        on_device,
        mesh=mesh,
        in_specs=(split, split, split) + (P(),) * 8,
        out_specs=(split, split),
        check_vma=False,
    )
```

```python
import functools
import math

import jax
import jax.numpy as jnp
from jax import lax
from jax.experimental import pallas as pl
from jax.experimental.pallas import tpu as pltpu
from jax.sharding import PartitionSpec as P

NEIGH = 8
ATOMS = 128
EDGES = NEIGH * ATOMS
CHUNKS = 18
CUTOFF = 4.0
SHARPNESS = 2.0
ROOT3 = math.sqrt(3.0)
F32 = jnp.float32
BF16 = jnp.bfloat16
TILE = 1024


RING = (0, 1, 3, 2)
ROUTES = (((0, 1), (1, 0), (1, 2), (2, 2)), ((0, 2), (2, 0), (1, 1), (2, 1)))
EVERY = ("gx", "gy", "gz")


def is_direct():
    return tuple(lax.axis_size(axis) for axis in EVERY) == (4, 4, 2)


def shifted(value, axis, step):
    count = lax.axis_size(axis)
    return lax.ppermute(value, axis, [(i, (i + step) % count) for i in range(count)])


def partner(index, way):
    if way == 0:
        return index
    if way == 1:
        return index ^ 1
    return (index + 2 * (index & 1) - 1) & 3


def number(x, y, core):
    return (x * 4 + y) * 2 + core


def swapped(value, slot):
    pairs = []
    for x in range(4):
        for y in range(4):
            for core in range(2):
                way_x, way_y = ROUTES[core][slot]
                to_x, to_y = partner(x, way_x), partner(y, way_y)
                pairs.append((number(RING[x], RING[y], core), number(RING[to_x], RING[to_y], core)))
    return lax.ppermute(value, EVERY, pairs)


def ring_gather(chunk):
    for axis in ("gx", "gy"):
        lower = shifted(chunk, axis, 1)
        upper = shifted(chunk, axis, -1)
        chunk = jnp.concatenate([lower, upper, chunk], axis=0)
    if lax.axis_size("gz") == 2:
        return [chunk, shifted(chunk, "gz", 1)]
    half = chunk.shape[-1] // 2
    above = shifted(chunk[..., :half], "gz", -1)
    below = shifted(chunk[..., half:], "gz", 1)
    return [chunk, jnp.concatenate([above, below], axis=-1)]


def ring_reduce(own, other):
    kind = own.dtype
    if lax.axis_size("gz") == 2:
        back = shifted(other, "gz", 1)
    else:
        half = other.shape[-1] // 2
        first = shifted(other[..., :half], "gz", 1)
        second = shifted(other[..., half:], "gz", -1)
        back = jnp.concatenate([first, second], axis=-1)
    own = own.astype(F32) + back.astype(F32)
    for axis, size in (("gy", 3), ("gx", 1)):
        lower = shifted(own[:size].astype(kind), axis, -1)
        upper = shifted(own[size : 2 * size].astype(kind), axis, 1)
        own = own[2 * size :] + lower.astype(F32) + upper.astype(F32)
    return own


def ring_at(index):
    return index ^ (index >> 1)


def column_here():
    return ring_at(lax.axis_index("gx")), ring_at(lax.axis_index("gy")), lax.axis_index("gz")


def owner_at(step_x, step_y, outside):
    x, y, core = column_here()
    return number((x + step_x) & 3, (y + step_y) & 3, core ^ outside)


def place_ring(step_x, step_y, outside):
    place_x = jnp.where(step_x == 0, 2, jnp.where(step_x < 0, 0, 1))
    place_y = jnp.where(step_y == 0, 2, jnp.where(step_y < 0, 0, 1))
    return outside * 9 + place_y * 3 + place_x


def place_direct(step_x, step_y, outside, twin):
    x, y, core = column_here()
    way_x = jnp.where(step_x == 0, 0, jnp.where(step_x == 1 - 2 * (x & 1), 1, 2))
    way_y = jnp.where(step_y == 0, 0, jnp.where(step_y == 1 - 2 * (y & 1), 1, 2))
    way = way_x * 3 + way_y
    other = 1 - outside if twin else outside
    chunk = jnp.where(way == 0, -1 if twin else 8 + other, -1)
    for slot in range(4):
        here, there = (ROUTES[mate][slot][0] * 3 + ROUTES[mate][slot][1] for mate in range(2))
        chunk = jnp.where(way == jnp.where(core == 0, here, there), 2 * slot + other, chunk)
    return chunk


def decode(code, slots):
    offset = code >> 6
    slot = code & 63
    step_x = jnp.where(offset >= 18, 1, jnp.where(offset >= 9, 0, -1))
    rest = offset - 9 * (step_x + 1)
    step_y = jnp.where(rest >= 6, 1, jnp.where(rest >= 3, 0, -1))
    step_z = rest - 3 * (step_y + 1) - 1
    block = lax.broadcasted_iota(jnp.int32, (NEIGH, ATOMS), 1) // slots
    level = block + step_z
    outside = jnp.where((level < 0) | (level > 1), 1, 0)
    return step_x, step_y, step_z, outside, (level & 1) * slots + slot


def blank_kernel(out_ref):
    out_ref[...] = jnp.zeros(out_ref.shape, F32)


def pack_kernel(blank_ref, pos_ref, spec_ref, nb_ref, out_ref):
    slots = spec_ref.shape[-1]
    half = nb_ref.shape[-1] // 2
    for block in range(2):
        lanes = slice(block * slots, (block + 1) * slots)
        for c in range(3):
            out_ref[0, c : c + 1, lanes] = pos_ref[0, 0, block : block + 1, c * slots : (c + 1) * slots]
        out_ref[0, 3:4, lanes] = spec_ref[0, 0, block : block + 1, :].astype(F32)
        for part in range(half // ATOMS):
            first = nb_ref[0, 0, block : block + 1, part * ATOMS : (part + 1) * ATOMS]
            second = nb_ref[0, 0, block : block + 1, half + part * ATOMS : half + (part + 1) * ATOMS]
            row = 4 + block * 2 + part
            out_ref[0, row : row + 1, :] = (first * 2048 + second).astype(F32)


def onehot_kernel(direct, *refs):
    codes = [refs[0][...]]
    if direct:
        codes.append(listed_codes(refs[1][owner_at(0, 0, 1)][4:8, :]))
    geo_ref, second_ref, readout_ref, gather_ref, scatter_ref, lane_ref, secondt_ref, rocol_ref = refs[-11:-3]
    slope_ref, spot_ref, turn_ref = refs[-3:]
    for k in range(NEIGH):
        bump, gap, inner, ratio = basis_parts(geo_ref[0, k : k + 1, :])
        slope_ref[k] = bump * inner * (-2.0 * SHARPNESS * gap * inner - (4.0 / CUTOFF) * ratio)
    secondt_ref[...] = second_ref[...].astype(F32).T.astype(BF16)
    rocol_ref[...] = jnp.broadcast_to(readout_ref[...], (ATOMS, ATOMS)).T
    down = lax.broadcasted_iota(jnp.int32, (ATOMS, ATOMS), 0).astype(F32).astype(BF16)
    across = lax.broadcasted_iota(jnp.int32, (ATOMS, ATOMS), 1).astype(F32).astype(BF16)
    one = jnp.ones((ATOMS, ATOMS), BF16)
    zero = jnp.zeros((ATOMS, ATOMS), BF16)
    turn_ref[...] = jnp.zeros(turn_ref.shape, F32)
    for twin, code in enumerate(codes):
        step_x, step_y, step_z, outside, lane = decode(code, ATOMS // 2)
        chunk = place_direct(step_x, step_y, outside, twin) if direct else place_ring(step_x, step_y, outside)
        if not twin:
            spot = outside * 9 + step_y * 3 + step_x + 4
            for k in range(NEIGH):
                spot_ref[k] = jnp.broadcast_to(spot[k : k + 1, :], (8, ATOMS))
        lane, chunk = lane.astype(F32), chunk.astype(F32)
        turn_ref[0:NEIGH, :] = lane
        turn_ref[NEIGH : 2 * NEIGH, :] = chunk
        turned = turn_ref[...].T
        for k in range(NEIGH):
            span = slice((twin * NEIGH + k) * ATOMS, (twin * NEIGH + k + 1) * ATOMS)

            def row(array, k=k):
                return jnp.broadcast_to(array[k : k + 1, :], (ATOMS, ATOMS)).astype(BF16)

            def column(at):
                return jnp.broadcast_to(turned[:, at : at + 1], (ATOMS, ATOMS)).astype(BF16)

            near = jnp.where(row(lane) == down, one, zero)
            near_turned = jnp.where(column(k) == across, one, zero)
            at, at_turned = row(chunk), column(NEIGH + k)
            if not twin:
                lane_ref[:, span] = near
            for c in range(gather_ref.shape[0] // ATOMS):
                part = slice(c * ATOMS, (c + 1) * ATOMS)
                this = jnp.full((ATOMS, ATOMS), c, BF16)
                gather_ref[part, span] = jnp.where(at == this, near, zero)
                scatter_ref[span, part] = jnp.where(at_turned == this, near_turned, zero)


def listed_codes(words):
    words = words.astype(jnp.int32)
    first, second = words >> 11, words & 2047
    width = 4 * ATOMS
    slots = width // NEIGH
    lane = lax.broadcasted_iota(jnp.int32, (NEIGH, width), 1)
    row = lax.broadcasted_iota(jnp.int32, (NEIGH, width), 0)
    mine = (lane & (NEIGH - 1)) == row
    spot = lax.broadcasted_iota(jnp.int32, (width, ATOMS), 0) // NEIGH
    column = lax.broadcasted_iota(jnp.int32, (width, ATOMS), 1)
    total = jnp.zeros((NEIGH, ATOMS), F32)
    for block in range(2):
        pieces = [part[2 * block + i : 2 * block + i + 1, :] for part in (first, second) for i in range(2)]
        listed = jnp.broadcast_to(jnp.concatenate(pieces, axis=1), (NEIGH, width))
        listed = jnp.where(mine, listed, 0)
        high = (listed >> 4).astype(F32).astype(BF16)
        low = (listed & 15).astype(F32).astype(BF16)
        pick = jnp.where(spot + block * slots == column, 1.0, 0.0).astype(BF16)
        total = total + 16.0 * jnp.dot(high, pick, preferred_element_type=F32)
        total = total + jnp.dot(low, pick, preferred_element_type=F32)
    return (total + 0.5).astype(jnp.int32)


def sigmoid(v):
    return 0.5 * jnp.tanh(0.5 * v) + 0.5


def silu_pair(v):
    s = sigmoid(v)
    value = v * s
    return value, s + value * (1.0 - s)


def angular_rows(ux, uy, uz):
    return [
        None, ux, uy, uz, ROOT3 * ux * uy, ROOT3 * uy * uz, 0.5 * (3.0 * uz * uz - 1.0),
        ROOT3 * ux * uz, 0.5 * ROOT3 * (ux * ux - uy * uy),
    ]


def spread_rows(yb_ref, angular):
    for m in range(1, 9):
        for k in range(NEIGH):
            yb_ref[m * NEIGH + k] = jnp.broadcast_to(angular[m][k : k + 1, :], (8, ATOMS))


def basis_parts(r_row):
    row = lax.broadcasted_iota(jnp.int32, (8, ATOMS), 0).astype(F32)
    centers = CUTOFF * (row + 0.5) / 8.0
    r = jnp.broadcast_to(r_row, (8, ATOMS))
    ratio = r * (1.0 / CUTOFF)
    inner = 1.0 - ratio * ratio
    gap = r - centers
    return jnp.exp(-SHARPNESS * gap * gap), gap, inner, ratio


PIECE = (0, 1, 1, 1, 2, 2, 2, 2, 2)


def forward_kernel(parts, direct, *refs):
    tables = refs[:parts]
    (
        center_ref, neighbor_ref, radial_ref, mix_ref, envw_ref, upd_ref,
        table_ref, code_ref, edge_ref, dsb_ref, dsl_ref, dse_ref, env_ref, v_ref, geo_ref, yb_ref,
        inv_ref, lat_ref, pad_ref,
    ) = refs[parts:]
    pad_ref[...] = jnp.zeros(pad_ref.shape, F32)
    pad_ref[0:8, :] = radial_ref[...].astype(F32)
    pad_ref[8 : 8 + neighbor_ref.shape[0], :] = neighbor_ref[...].astype(F32)
    pad_ref[16 : 16 + center_ref.shape[0], :] = center_ref[...].astype(F32)
    wcat = pad_ref[...].T[:, :32].astype(BF16)
    mixt = mix_ref[...].astype(F32).T.astype(BF16)
    envt = envw_ref[...].astype(F32).T.astype(BF16)
    updt = [upd_ref[p * ATOMS : (p + 1) * ATOMS, :].astype(F32).T.astype(BF16) for p in range(3)]
    updt_alike, updt = updt[0], jnp.concatenate(updt[1:], axis=1)

    def chunk_at(far, dx, dy):
        if direct:
            return tables[0][owner_at(dx, dy, far)]
        return tables[far][(0, 2, 1)[dy + 1] * 3 + (0, 2, 1)[dx + 1]]

    home = chunk_at(0, 0, 0)
    code = listed_codes(home[4:8, :])
    code_ref[...] = code
    step_x, step_y, step_z, outside, lane = decode(code, ATOMS // 2)
    spot = outside * 9 + step_y * 3 + step_x + 4
    found = [jnp.zeros((NEIGH, ATOMS), F32) for _ in range(4)]
    for far in range(2):
        for dy in (-1, 0, 1):
            for dx in (-1, 0, 1):
                hit = spot == far * 9 + dy * 3 + dx + 4
                rows = chunk_at(far, dx, dy)
                for f in range(4):
                    row = jnp.broadcast_to(rows[f : f + 1, :], (NEIGH, ATOMS))
                    found[f] = jnp.where(hit, jnp.take_along_axis(row, lane, axis=1), found[f])
    d = [
        step.astype(F32) + (found[c] - jnp.broadcast_to(home[c : c + 1, :], (NEIGH, ATOMS)))
        for c, step in enumerate((step_x, step_y, step_z))
    ]
    r = jnp.sqrt(d[0] * d[0] + d[1] * d[1] + d[2] * d[2])
    ux, uy, uz = d[0] / r, d[1] / r, d[2] / r
    geo_ref[0] = r
    geo_ref[1] = ux
    geo_ref[2] = uy
    geo_ref[3] = uz
    spread_rows(yb_ref, angular_rows(ux, uy, uz))

    kind = lax.broadcasted_iota(jnp.int32, (8, ATOMS), 0).astype(F32)
    center_hot = jnp.where(jnp.broadcast_to(home[3:4, :], (8, ATOMS)) == kind, 1.0, 0.0)
    zero = jnp.zeros((8, ATOMS), F32)
    columns = []
    for k in range(NEIGH):
        bump, gap, inner, ratio = basis_parts(r[k : k + 1, :])
        other_hot = jnp.where(jnp.broadcast_to(found[3][k : k + 1, :], (8, ATOMS)) == kind, 1.0, 0.0)
        columns.append(jnp.concatenate([bump * (inner * inner), other_hot, center_hot, zero], axis=0).astype(BF16))
    for j in range(EDGES // TILE):
        span = slice(j * TILE, (j + 1) * TILE)
        per = TILE // ATOMS
        x = jnp.concatenate(columns[j * per : (j + 1) * per], axis=1)
        act, ds = silu_pair(jnp.dot(wcat, x, preferred_element_type=F32))
        dsb_ref[:, span] = ds
        latent, ds = silu_pair(jnp.dot(mixt, act.astype(BF16), preferred_element_type=F32))
        dsl_ref[:, span] = ds
        lat_ref[:, span] = latent
        env_ref[:, span] = jnp.dot(envt, latent.astype(BF16), preferred_element_type=F32)
    for t in range(8):
        halves = []
        for h in range(2):
            rows = slice(t * 16 + h * 8, t * 16 + h * 8 + 8)
            env = [env_ref[rows, k * ATOMS : (k + 1) * ATOMS] for k in range(NEIGH)]
            field = []
            for m in range(9):
                terms = [env[k] if m == 0 else env[k] * yb_ref[m * NEIGH + k] for k in range(NEIGH)]
                while len(terms) > 1:
                    terms = [terms[i] + terms[i + 1] for i in range(0, len(terms), 2)]
                field.append(terms[0] * 0.125)
                v_ref[m, rows, :] = field[m]
            out = []
            for k in range(NEIGH):
                sums = [field[0], None, None]
                for m in range(1, 9):
                    term = field[m] * yb_ref[m * NEIGH + k]
                    sums[PIECE[m]] = term if sums[PIECE[m]] is None else sums[PIECE[m]] + term
                out.append(sums)
            halves.append(out)
        for k in range(NEIGH):
            for p in range(1, 3):
                both = jnp.concatenate([halves[0][k][p], halves[1][k][p]], axis=0)
                inv_ref[p * ATOMS - ATOMS + t * 16 : p * ATOMS - ATOMS + t * 16 + 16, k * ATOMS : (k + 1) * ATOMS] = both.astype(BF16)
    alike = jnp.dot(updt_alike, v_ref[0].astype(BF16), preferred_element_type=F32)
    mean = jnp.zeros((ATOMS, ATOMS), F32)
    for j in range(EDGES // TILE):
        span = slice(j * TILE, (j + 1) * TILE)
        update = jnp.dot(updt, inv_ref[:, span], preferred_element_type=F32)
        edge, ds = silu_pair(lat_ref[:, span] + update + jnp.concatenate([alike] * (TILE // ATOMS), axis=1))
        edge_ref[:, span] = edge
        dse_ref[:, span] = ds
        for i in range(TILE // ATOMS):
            mean = mean + edge[:, i * ATOMS : (i + 1) * ATOMS]
    table_ref[0] = (mean * 0.125).astype(BF16)


def second_kernel(parts, order, *refs):
    gather_ref, scatter_ref, second_ref, secondt_ref, rocol_ref = refs[parts : parts + 5]
    sets = gather_ref.shape[1] // EDGES
    edges = refs[parts + 5 : parts + 5 + sets]
    energy_ref, grad_edge_ref, *outs = refs[parts + 5 + sets : -2]
    other_ref, grad_ref = refs[-2:]
    table = jnp.concatenate([refs[array][row] for array, row in order], axis=1)
    rocol = rocol_ref[...]
    other_ref[...] = jnp.dot(table, gather_ref[...], preferred_element_type=F32)
    wide = 2 * ATOMS
    if sets == 2:
        give_ref = outs.pop(0)
        give_ref[ATOMS:, :] = jnp.zeros((8, EDGES), F32)
    for own in range(sets):
        total = jnp.zeros((ATOMS, ATOMS), F32)
        for j in range(EDGES // wide):
            span = slice(j * wide, (j + 1) * wide)
            both = slice(own * EDGES + j * wide, own * EDGES + (j + 1) * wide)
            other = other_ref[:, both]
            edge = edges[own][:, span]
            hidden, ds = silu_pair(
                jnp.dot(secondt_ref[...], (edge * other).astype(BF16), preferred_element_type=F32)
            )
            total = total + hidden[:, :ATOMS] + hidden[:, ATOMS:]
            grad_hidden = ds * jnp.concatenate([rocol, rocol], axis=1)
            grad_prod = jnp.dot(second_ref[...], grad_hidden.astype(BF16), preferred_element_type=F32)
            grad_prod = grad_prod.astype(BF16).astype(F32)
            if own == 0:
                grad_edge_ref[:, span] = grad_prod * other
            else:
                give_ref[:ATOMS, span] = grad_prod * other
            grad_ref[:, both] = (grad_prod * edge).astype(BF16)
        energy = jnp.sum(total * rocol, axis=0, keepdims=True)
        if own == 0:
            energy_ref[...] = energy
        else:
            give_ref[ATOMS : ATOMS + 1, :ATOMS] = energy
    places = [(ref, row) for ref in outs for row in range(ref.shape[0])]
    for c in range(0, len(places), 2):
        back = jnp.dot(grad_ref[...], scatter_ref[:, c * ATOMS : (c + 2) * ATOMS], preferred_element_type=F32)
        for i in range(2):
            ref, row = places[c + i]
            ref[row] = back[:, i * ATOMS : (i + 1) * ATOMS].astype(ref.dtype)


def backward_kernel(
    direct, owned_ref, energy_ref, grad_edge_ref, dse_ref, dsl_ref, dsb_ref, env_ref, v_ref, geo_ref, yb_ref, slope_ref, spot_ref, lane_ref,
    upd_ref, envw_ref, mix_ref, radial_ref, *refs,
):
    *extra, dinv_ref, denv_ref, dlat_ref, part_ref, force_ref, alike_ref = refs
    energy = energy_ref[...]
    if direct:
        given_ref, *extra = extra
        energy = energy + given_ref[ATOMS : ATOMS + 1, :ATOMS]
    outs = extra
    r, ux, uy, uz = (geo_ref[i] for i in range(4))
    share = owned_ref[0] * 0.125
    alike = jnp.zeros((ATOMS, ATOMS), F32)
    for j in range(EDGES // TILE):
        span = slice(j * TILE, (j + 1) * TILE)
        d_edge = grad_edge_ref[:, span] + jnp.concatenate([share] * (TILE // ATOMS), axis=1)
        if direct:
            d_edge = d_edge + given_ref[:ATOMS, span]
        d_pre = d_edge * dse_ref[:, span]
        dlat_ref[:, span] = d_pre
        dinv_ref[:, span] = jnp.dot(
            upd_ref[ATOMS:, :], d_pre.astype(BF16), preferred_element_type=F32
        ).astype(BF16)
        for i in range(TILE // ATOMS):
            alike = alike + d_pre[:, i * ATOMS : (i + 1) * ATOMS]
    alike_ref[...] = jnp.dot(upd_ref[:ATOMS, :], alike.astype(BF16), preferred_element_type=F32)
    part_ref[...] = jnp.zeros(part_ref.shape, F32)
    for t in range(8):
        wide = [
            [
                dinv_ref[p * ATOMS + t * 16 : p * ATOMS + t * 16 + 16, k * ATOMS : (k + 1) * ATOMS].astype(F32)
                for k in range(NEIGH)
            ]
            for p in range(2)
        ]
        halves = []
        for h in range(2):
            rows = slice(t * 16 + h * 8, t * 16 + h * 8 + 8)
            dinv = [[wide[p][k][h * 8 : h * 8 + 8] for k in range(NEIGH)] for p in range(2)]
            env = [env_ref[rows, k * ATOMS : (k + 1) * ATOMS] for k in range(NEIGH)]
            denv = [alike_ref[rows, :] * 0.125] * NEIGH
            for m in range(1, 9):
                down = dinv[PIECE[m] - 1]
                terms = [down[k] * yb_ref[m * NEIGH + k] for k in range(NEIGH)]
                while len(terms) > 1:
                    terms = [terms[i] + terms[i + 1] for i in range(0, len(terms), 2)]
                d_field = terms[0] * 0.125
                field = v_ref[m, rows, :]
                for k in range(NEIGH):
                    spot = m * NEIGH + k
                    part_ref[spot] = part_ref[spot] + (down[k] * field + env[k] * d_field)
                    denv[k] = denv[k] + d_field * yb_ref[spot]
            halves.append(denv)
        for k in range(NEIGH):
            both = jnp.concatenate([halves[0][k], halves[1][k]], axis=0)
            denv_ref[t * 16 : t * 16 + 16, k * ATOMS : (k + 1) * ATOMS] = both.astype(BF16)
    d_r_rows = []
    for j in range(EDGES // TILE):
        span = slice(j * TILE, (j + 1) * TILE)
        d_lat = jnp.dot(envw_ref[...], denv_ref[:, span], preferred_element_type=F32).astype(BF16).astype(F32)
        d_mix = (dlat_ref[:, span] + d_lat) * dsl_ref[:, span]
        d_act = jnp.dot(mix_ref[...], d_mix.astype(BF16), preferred_element_type=F32).astype(BF16).astype(F32)
        d_before = (d_act * dsb_ref[:, span]).astype(BF16)
        d_basis = jnp.dot(radial_ref[...], d_before, preferred_element_type=F32).astype(BF16).astype(F32)
        for i in range(TILE // ATOMS):
            k = j * (TILE // ATOMS) + i
            d_r_rows.append(jnp.sum(slope_ref[k] * d_basis[:, i * ATOMS : (i + 1) * ATOMS], axis=0, keepdims=True))
    d_r = jnp.concatenate(d_r_rows, axis=0)
    dy = [None]
    for m in range(1, 9):
        rows = [jnp.sum(part_ref[m * NEIGH + k], axis=0, keepdims=True) for k in range(NEIGH)]
        dy.append(jnp.concatenate(rows, axis=0))
    d_ux = dy[1] + ROOT3 * (uy * dy[4] + uz * dy[7] + ux * dy[8])
    d_uy = dy[2] + ROOT3 * (ux * dy[4] + uz * dy[5] - uy * dy[8])
    d_uz = dy[3] + ROOT3 * (uy * dy[5] + ux * dy[7]) + 3.0 * uz * dy[6]
    along = ux * d_ux + uy * d_uy + uz * d_uz
    inverse = 1.0 / r
    radial = d_r - along * inverse
    pull = [d_ux * inverse + ux * radial, d_uy * inverse + uy * radial, d_uz * inverse + uz * radial]
    high = [p.astype(BF16).astype(F32) for p in pull]
    low = [p - h for p, h in zip(pull, high)]
    zero = jnp.zeros((1, ATOMS), F32)
    rows, spots = [], []
    for k in range(NEIGH):
        parts = [h[k : k + 1, :] for h in high] + [zero] + [q[k : k + 1, :] for q in low] + [zero]
        rows.append(jnp.concatenate(parts, axis=0))
        spots.append(spot_ref[k])
    for c in range(0, CHUNKS, 2):
        for k in range(NEIGH):
            both = [jnp.where(spots[k] == c + i, rows[k], 0.0) for i in range(2)]
            force_ref[c * 8 : c * 8 + 16, k * ATOMS : (k + 1) * ATOMS] = jnp.concatenate(both, axis=0).astype(BF16)
    back = lax.dot_general(
        force_ref[...], lane_ref[...], (((1,), (1,)), ((), ())), preferred_element_type=F32
    )
    center = jnp.concatenate([jnp.sum(p, axis=0, keepdims=True) for p in pull] + [-energy], axis=0)
    if direct:
        outs[0][...] = jnp.zeros(outs[0].shape, F32)
    for c in range(CHUNKS):
        far, dy, dx = c // 9, c % 9 // 3 - 1, c % 3 - 1
        moved = back[8 * c : 8 * c + 4] + back[8 * c + 4 : 8 * c + 8]
        if (far, dy, dx) == (0, 0, 0):
            moved = moved - center
        if direct:
            outs[0][owner_at(dx, dy, far)] = moved
        else:
            outs[far][(0, 2, 1)[dy + 1] * 3 + (0, 2, 1)[dx + 1]] = moved


def finish_kernel(moved_ref, energy_ref, out_ref):
    slots = energy_ref.shape[-1]
    total = jnp.sum(moved_ref[...], axis=0)
    for block in range(2):
        lanes = slice(block * slots, (block + 1) * slots)
        energy_ref[0, 0, block : block + 1, :] = total[3:4, lanes]
        for c in range(3):
            out_ref[0, 0, block : block + 1, c * slots : (c + 1) * slots] = -total[c : c + 1, lanes]


def call(kernel, outs, scratch=(), name=None, limit=24 << 20, place=pltpu.VMEM, cost=None):
    whole = pl.BlockSpec(memory_space=pltpu.VMEM)
    shapes = [jax.ShapeDtypeStruct(shape, kind) for shape, kind in outs]

    def run(*args):
        return pl.pallas_call(
            kernel,
            out_shape=shapes,
            in_specs=[pl.BlockSpec(memory_space=place)] * len(args),
            out_specs=[whole] * len(shapes),
            scratch_shapes=list(scratch),
            compiler_params=pltpu.CompilerParams(vmem_limit_bytes=limit),
            cost_estimate=cost,
            name=name,
        )(*args)

    return run


def on_device(
    positions, species, neighbors, center_table, neighbor_table, radial_weight, mix_weight,
    env_weight, update_weight, second_weight, readout,
):
    slots = species.shape[-1]
    edges = (ATOMS, EDGES)
    square = (ATOMS, ATOMS)
    readout = readout.reshape(1, ATOMS)
    direct = is_direct()
    devices = 32
    (blank,) = call(
        blank_kernel,
        [((8, ATOMS), F32)],
        name="blank",
        cost=pl.CostEstimate(flops=1 << 34, bytes_accessed=64 << 20, transcendentals=0),
    )()
    (packed,) = call(pack_kernel, [((1, 8, ATOMS), F32)], name="pack")(blank, positions, species, neighbors)
    if direct:
        copies = jnp.broadcast_to(packed, (devices, 8, ATOMS))
        tables = [lax.all_to_all(copies, EVERY, 0, 0, tiled=True)]
    else:
        tables = ring_gather(packed)
    table, code, edge, dsb, dsl, dse, env, field, geo, spread = call(
        functools.partial(forward_kernel, len(tables), direct),
        [
            ((1,) + square, BF16), ((NEIGH, ATOMS), jnp.int32), (edges, F32), (edges, F32), (edges, F32),
            (edges, F32), (edges, F32), ((9,) + square, F32), ((4, NEIGH, ATOMS), F32), ((72, 8, ATOMS), F32),
        ],
        [pltpu.VMEM((2 * ATOMS, EDGES), BF16), pltpu.VMEM(edges, F32), pltpu.VMEM(square, F32)],
        name="forward",
    )(*tables, center_table, neighbor_table, radial_weight, mix_weight, env_weight, update_weight)
    chunks, sets = (10, 2) if direct else (CHUNKS, 1)
    sent = edge
    if direct:
        both = jnp.concatenate([table, shifted(table, "gz", 1)], axis=0)
        both, sent, code, geo = lax.optimization_barrier((both, edge, code, geo))
    gather, scatter, lanes, secondt, rocol, slope, spot = call(
        functools.partial(onehot_kernel, direct),
        [
            ((chunks * ATOMS, sets * EDGES), BF16), ((sets * EDGES, chunks * ATOMS), BF16), (edges, BF16),
            (square, BF16), (square, F32), ((NEIGH, 8, ATOMS), F32), ((NEIGH, 8, ATOMS), jnp.int32),
        ],
        [pltpu.VMEM(square, F32)],
        name="onehot",
        cost=pl.CostEstimate(flops=1 << 30, bytes_accessed=8 << 20, transcendentals=0),
    )(code, *(tables if direct else ()), geo, second_weight, readout)
    if direct:
        tables = [swapped(both, slot) for slot in range(4)] + [both]
        order = [(array, row) for array in range(5) for row in range(2)]
        latents = [edge, shifted(sent, "gz", 1)]
        returned = [((ATOMS + 8, EDGES), F32)] + [((2,) + square, BF16)] * 4 + [((2,) + square, F32)]
    else:
        tables = ring_gather(table)
        order = [(array, row) for array in range(2) for row in range(9)]
        latents = [edge]
        returned = [((9,) + square, BF16)] * 2
    energy, grad_edge, *returned = call(
        functools.partial(second_kernel, len(tables), order),
        [((1, ATOMS), F32), (edges, F32)] + returned,
        [pltpu.VMEM((ATOMS, sets * EDGES), F32), pltpu.VMEM((ATOMS, sets * EDGES), BF16)],
        name="second",
    )(*tables, gather, scatter, second_weight, secondt, rocol, *latents)
    if direct:
        give, *back, home = returned
        given = [shifted(give, "gz", 1)]
        for slot in (3, 2, 1, 0):
            home = home + swapped(back[slot], slot).astype(F32)
        owned = home[:1] + shifted(home[1:], "gz", 1)
    else:
        given = []
        owned = ring_reduce(*returned)
    moved = call(
        functools.partial(backward_kernel, direct),
        [((devices, 4, ATOMS), F32)] if direct else [((9, 4, ATOMS), F32)] * 2,
        [
            pltpu.VMEM((2 * ATOMS, EDGES), BF16), pltpu.VMEM(edges, BF16), pltpu.VMEM(edges, F32),
            pltpu.VMEM((72, 8, ATOMS), F32), pltpu.VMEM((CHUNKS * 8, EDGES), BF16), pltpu.VMEM(square, F32),
        ],
        name="backward",
    )(
        owned, energy, grad_edge, dse, dsl, dsb, env, field, geo, spread, slope, spot, lanes, update_weight, env_weight, mix_weight,
        radial_weight, *given,
    )
    moved = lax.all_to_all(moved[0], EVERY, 0, 0, tiled=True) if direct else ring_reduce(*moved)
    return call(finish_kernel, [((1, 1, 2, slots), F32), ((1, 1, 2, 3 * slots), F32)], name="finish")(moved)


def solution(mesh):
    split = P("gx", "gy", "gz", None)
    return jax.shard_map(
        on_device,
        mesh=mesh,
        in_specs=(split, split, split) + (P(),) * 8,
        out_specs=(split, split),
        check_vma=False,
    )
```

```python
import functools
import math

import jax
import jax.numpy as jnp
from jax import lax
from jax.experimental import pallas as pl
from jax.experimental.pallas import tpu as pltpu
from jax.sharding import PartitionSpec as P

NEIGH = 8
ATOMS = 128
EDGES = NEIGH * ATOMS
CHUNKS = 18
CUTOFF = 4.0
SHARPNESS = 2.0
ROOT3 = math.sqrt(3.0)
F32 = jnp.float32
BF16 = jnp.bfloat16
TILE = 1024


RING = (0, 1, 3, 2)
ROUTES = (((0, 1), (1, 0), (1, 2), (2, 2)), ((0, 2), (2, 0), (1, 1), (2, 1)))
EVERY = ("gx", "gy", "gz")


def is_direct():
    return tuple(lax.axis_size(axis) for axis in EVERY) == (4, 4, 2)


def shifted(value, axis, step):
    count = lax.axis_size(axis)
    return lax.ppermute(value, axis, [(i, (i + step) % count) for i in range(count)])


def partner(index, way):
    if way == 0:
        return index
    if way == 1:
        return index ^ 1
    return (index + 2 * (index & 1) - 1) & 3


def number(x, y, core):
    return (x * 4 + y) * 2 + core


def swapped(value, slot):
    pairs = []
    for x in range(4):
        for y in range(4):
            for core in range(2):
                way_x, way_y = ROUTES[core][slot]
                to_x, to_y = partner(x, way_x), partner(y, way_y)
                pairs.append((number(RING[x], RING[y], core), number(RING[to_x], RING[to_y], core)))
    return lax.ppermute(value, EVERY, pairs)


def ring_gather(chunk):
    for axis in ("gx", "gy"):
        lower = shifted(chunk, axis, 1)
        upper = shifted(chunk, axis, -1)
        chunk = jnp.concatenate([lower, upper, chunk], axis=0)
    if lax.axis_size("gz") == 2:
        return [chunk, shifted(chunk, "gz", 1)]
    half = chunk.shape[-1] // 2
    above = shifted(chunk[..., :half], "gz", -1)
    below = shifted(chunk[..., half:], "gz", 1)
    return [chunk, jnp.concatenate([above, below], axis=-1)]


def ring_reduce(own, other):
    kind = own.dtype
    if lax.axis_size("gz") == 2:
        back = shifted(other, "gz", 1)
    else:
        half = other.shape[-1] // 2
        first = shifted(other[..., :half], "gz", 1)
        second = shifted(other[..., half:], "gz", -1)
        back = jnp.concatenate([first, second], axis=-1)
    own = own.astype(F32) + back.astype(F32)
    for axis, size in (("gy", 3), ("gx", 1)):
        lower = shifted(own[:size].astype(kind), axis, -1)
        upper = shifted(own[size : 2 * size].astype(kind), axis, 1)
        own = own[2 * size :] + lower.astype(F32) + upper.astype(F32)
    return own


def ring_at(index):
    return index ^ (index >> 1)


def column_here():
    return ring_at(lax.axis_index("gx")), ring_at(lax.axis_index("gy")), lax.axis_index("gz")


def owner_at(step_x, step_y, outside):
    x, y, core = column_here()
    return number((x + step_x) & 3, (y + step_y) & 3, core ^ outside)


def place_ring(step_x, step_y, outside):
    place_x = jnp.where(step_x == 0, 2, jnp.where(step_x < 0, 0, 1))
    place_y = jnp.where(step_y == 0, 2, jnp.where(step_y < 0, 0, 1))
    return outside * 9 + place_y * 3 + place_x


def place_direct(step_x, step_y, outside, twin):
    x, y, core = column_here()
    way_x = jnp.where(step_x == 0, 0, jnp.where(step_x == 1 - 2 * (x & 1), 1, 2))
    way_y = jnp.where(step_y == 0, 0, jnp.where(step_y == 1 - 2 * (y & 1), 1, 2))
    way = way_x * 3 + way_y
    other = 1 - outside if twin else outside
    chunk = jnp.where(way == 0, -1 if twin else 8 + other, -1)
    for slot in range(4):
        here, there = (ROUTES[mate][slot][0] * 3 + ROUTES[mate][slot][1] for mate in range(2))
        chunk = jnp.where(way == jnp.where(core == 0, here, there), 2 * slot + other, chunk)
    return chunk


def decode(code, slots):
    offset = code >> 6
    slot = code & 63
    step_x = jnp.where(offset >= 18, 1, jnp.where(offset >= 9, 0, -1))
    rest = offset - 9 * (step_x + 1)
    step_y = jnp.where(rest >= 6, 1, jnp.where(rest >= 3, 0, -1))
    step_z = rest - 3 * (step_y + 1) - 1
    block = lax.broadcasted_iota(jnp.int32, (NEIGH, ATOMS), 1) // slots
    level = block + step_z
    outside = jnp.where((level < 0) | (level > 1), 1, 0)
    return step_x, step_y, step_z, outside, (level & 1) * slots + slot


def blank_kernel(out_ref):
    out_ref[...] = jnp.zeros(out_ref.shape, F32)


def pack_kernel(blank_ref, pos_ref, spec_ref, nb_ref, out_ref):
    slots = spec_ref.shape[-1]
    half = nb_ref.shape[-1] // 2
    for block in range(2):
        lanes = slice(block * slots, (block + 1) * slots)
        for c in range(3):
            out_ref[0, c : c + 1, lanes] = pos_ref[0, 0, block : block + 1, c * slots : (c + 1) * slots]
        out_ref[0, 3:4, lanes] = spec_ref[0, 0, block : block + 1, :].astype(F32)
        for part in range(half // ATOMS):
            first = nb_ref[0, 0, block : block + 1, part * ATOMS : (part + 1) * ATOMS]
            second = nb_ref[0, 0, block : block + 1, half + part * ATOMS : half + (part + 1) * ATOMS]
            row = 4 + block * 2 + part
            out_ref[0, row : row + 1, :] = (first * 2048 + second).astype(F32)


def onehot_kernel(direct, *refs):
    codes = [refs[0][...]]
    if direct:
        codes.append(listed_codes(refs[1][owner_at(0, 0, 1)][4:8, :]))
    geo_ref, second_ref, readout_ref, gather_ref, scatter_ref, lane_ref, secondt_ref, rocol_ref = refs[-11:-3]
    slope_ref, spot_ref, turn_ref = refs[-3:]
    for k in range(NEIGH):
        bump, gap, inner, ratio = basis_parts(geo_ref[0, k : k + 1, :])
        slope_ref[k] = bump * inner * (-2.0 * SHARPNESS * gap * inner - (4.0 / CUTOFF) * ratio)
    secondt_ref[...] = second_ref[...].astype(F32).T.astype(BF16)
    rocol_ref[...] = jnp.broadcast_to(readout_ref[...], (ATOMS, ATOMS)).T
    down = lax.broadcasted_iota(jnp.int32, (ATOMS, ATOMS), 0).astype(F32).astype(BF16)
    across = lax.broadcasted_iota(jnp.int32, (ATOMS, ATOMS), 1).astype(F32).astype(BF16)
    one = jnp.ones((ATOMS, ATOMS), BF16)
    zero = jnp.zeros((ATOMS, ATOMS), BF16)
    turn_ref[...] = jnp.zeros(turn_ref.shape, F32)
    for twin, code in enumerate(codes):
        step_x, step_y, step_z, outside, lane = decode(code, ATOMS // 2)
        chunk = place_direct(step_x, step_y, outside, twin) if direct else place_ring(step_x, step_y, outside)
        if not twin:
            spot = outside * 9 + step_y * 3 + step_x + 4
            for k in range(NEIGH):
                spot_ref[k] = jnp.broadcast_to(spot[k : k + 1, :], (8, ATOMS))
        lane, chunk = lane.astype(F32), chunk.astype(F32)
        turn_ref[0:NEIGH, :] = lane
        turn_ref[NEIGH : 2 * NEIGH, :] = chunk
        turned = turn_ref[...].T
        for k in range(NEIGH):
            span = slice((twin * NEIGH + k) * ATOMS, (twin * NEIGH + k + 1) * ATOMS)

            def row(array, k=k):
                return jnp.broadcast_to(array[k : k + 1, :], (ATOMS, ATOMS)).astype(BF16)

            def column(at):
                return jnp.broadcast_to(turned[:, at : at + 1], (ATOMS, ATOMS)).astype(BF16)

            near = jnp.where(row(lane) == down, one, zero)
            near_turned = jnp.where(column(k) == across, one, zero)
            at, at_turned = row(chunk), column(NEIGH + k)
            if not twin:
                lane_ref[:, span] = near
            for c in range(gather_ref.shape[0] // ATOMS):
                part = slice(c * ATOMS, (c + 1) * ATOMS)
                this = jnp.full((ATOMS, ATOMS), c, BF16)
                gather_ref[part, span] = jnp.where(at == this, near, zero)
                scatter_ref[span, part] = jnp.where(at_turned == this, near_turned, zero)


def listed_codes(words):
    words = words.astype(jnp.int32)
    first, second = words >> 11, words & 2047
    width = 4 * ATOMS
    slots = width // NEIGH
    lane = lax.broadcasted_iota(jnp.int32, (NEIGH, width), 1)
    row = lax.broadcasted_iota(jnp.int32, (NEIGH, width), 0)
    mine = (lane & (NEIGH - 1)) == row
    spot = lax.broadcasted_iota(jnp.int32, (width, ATOMS), 0) // NEIGH
    column = lax.broadcasted_iota(jnp.int32, (width, ATOMS), 1)
    total = jnp.zeros((NEIGH, ATOMS), F32)
    for block in range(2):
        pieces = [part[2 * block + i : 2 * block + i + 1, :] for part in (first, second) for i in range(2)]
        listed = jnp.broadcast_to(jnp.concatenate(pieces, axis=1), (NEIGH, width))
        listed = jnp.where(mine, listed, 0)
        high = (listed >> 4).astype(F32).astype(BF16)
        low = (listed & 15).astype(F32).astype(BF16)
        pick = jnp.where(spot + block * slots == column, 1.0, 0.0).astype(BF16)
        total = total + 16.0 * jnp.dot(high, pick, preferred_element_type=F32)
        total = total + jnp.dot(low, pick, preferred_element_type=F32)
    return (total + 0.5).astype(jnp.int32)


def sigmoid(v):
    return 0.5 * jnp.tanh(0.5 * v) + 0.5


def silu_pair(v):
    s = sigmoid(v)
    value = v * s
    return value, s + value * (1.0 - s)


def angular_rows(ux, uy, uz):
    return [
        None, ux, uy, uz, ROOT3 * ux * uy, ROOT3 * uy * uz, 0.5 * (3.0 * uz * uz - 1.0),
        ROOT3 * ux * uz, 0.5 * ROOT3 * (ux * ux - uy * uy),
    ]


def spread_rows(yb_ref, angular):
    for m in range(1, 9):
        for k in range(NEIGH):
            yb_ref[m * NEIGH + k] = jnp.broadcast_to(angular[m][k : k + 1, :], (8, ATOMS))


def basis_parts(r_row):
    row = lax.broadcasted_iota(jnp.int32, (8, ATOMS), 0).astype(F32)
    centers = CUTOFF * (row + 0.5) / 8.0
    r = jnp.broadcast_to(r_row, (8, ATOMS))
    ratio = r * (1.0 / CUTOFF)
    inner = 1.0 - ratio * ratio
    gap = r - centers
    return jnp.exp(-SHARPNESS * gap * gap), gap, inner, ratio


PIECE = (0, 1, 1, 1, 2, 2, 2, 2, 2)


def forward_kernel(parts, direct, *refs):
    tables = refs[:parts]
    (
        center_ref, neighbor_ref, radial_ref, mix_ref, envw_ref, upd_ref,
        table_ref, code_ref, edge_ref, dsb_ref, dsl_ref, dse_ref, env_ref, v_ref, geo_ref, yb_ref,
        inv_ref, lat_ref, pad_ref,
    ) = refs[parts:]
    pad_ref[...] = jnp.zeros(pad_ref.shape, F32)
    pad_ref[0:8, :] = radial_ref[...].astype(F32)
    pad_ref[8 : 8 + neighbor_ref.shape[0], :] = neighbor_ref[...].astype(F32)
    pad_ref[16 : 16 + center_ref.shape[0], :] = center_ref[...].astype(F32)
    wcat = pad_ref[...].T[:, :32].astype(BF16)
    mixt = mix_ref[...].astype(F32).T.astype(BF16)
    envt = envw_ref[...].astype(F32).T.astype(BF16)
    updt = [upd_ref[p * ATOMS : (p + 1) * ATOMS, :].astype(F32).T.astype(BF16) for p in range(3)]
    updt_alike, updt = updt[0], jnp.concatenate(updt[1:], axis=1)

    def chunk_at(far, dx, dy):
        if direct:
            return tables[0][owner_at(dx, dy, far)]
        return tables[far][(0, 2, 1)[dy + 1] * 3 + (0, 2, 1)[dx + 1]]

    home = chunk_at(0, 0, 0)
    code = listed_codes(home[4:8, :])
    code_ref[...] = code
    step_x, step_y, step_z, outside, lane = decode(code, ATOMS // 2)
    spot = outside * 9 + step_y * 3 + step_x + 4
    found = [jnp.zeros((NEIGH, ATOMS), F32) for _ in range(4)]
    for far in range(2):
        for dy in (-1, 0, 1):
            for dx in (-1, 0, 1):
                hit = spot == far * 9 + dy * 3 + dx + 4
                rows = chunk_at(far, dx, dy)
                for f in range(4):
                    row = jnp.broadcast_to(rows[f : f + 1, :], (NEIGH, ATOMS))
                    found[f] = jnp.where(hit, jnp.take_along_axis(row, lane, axis=1), found[f])
    d = [
        step.astype(F32) + (found[c] - jnp.broadcast_to(home[c : c + 1, :], (NEIGH, ATOMS)))
        for c, step in enumerate((step_x, step_y, step_z))
    ]
    r = jnp.sqrt(d[0] * d[0] + d[1] * d[1] + d[2] * d[2])
    ux, uy, uz = d[0] / r, d[1] / r, d[2] / r
    geo_ref[0] = r
    geo_ref[1] = ux
    geo_ref[2] = uy
    geo_ref[3] = uz
    spread_rows(yb_ref, angular_rows(ux, uy, uz))

    kind = lax.broadcasted_iota(jnp.int32, (8, ATOMS), 0).astype(F32)
    center_hot = jnp.where(jnp.broadcast_to(home[3:4, :], (8, ATOMS)) == kind, 1.0, 0.0)
    zero = jnp.zeros((8, ATOMS), F32)
    columns = []
    for k in range(NEIGH):
        bump, gap, inner, ratio = basis_parts(r[k : k + 1, :])
        other_hot = jnp.where(jnp.broadcast_to(found[3][k : k + 1, :], (8, ATOMS)) == kind, 1.0, 0.0)
        columns.append(jnp.concatenate([bump * (inner * inner), other_hot, center_hot, zero], axis=0).astype(BF16))
    for j in range(EDGES // TILE):
        span = slice(j * TILE, (j + 1) * TILE)
        per = TILE // ATOMS
        x = jnp.concatenate(columns[j * per : (j + 1) * per], axis=1)
        act, ds = silu_pair(jnp.dot(wcat, x, preferred_element_type=F32))
        dsb_ref[:, span] = ds
        latent, ds = silu_pair(jnp.dot(mixt, act.astype(BF16), preferred_element_type=F32))
        dsl_ref[:, span] = ds
        lat_ref[:, span] = latent
        env_ref[:, span] = jnp.dot(envt, latent.astype(BF16), preferred_element_type=F32)
    for t in range(8):
        halves = []
        for h in range(2):
            rows = slice(t * 16 + h * 8, t * 16 + h * 8 + 8)
            env = [env_ref[rows, k * ATOMS : (k + 1) * ATOMS] for k in range(NEIGH)]
            field = []
            for m in range(9):
                terms = [env[k] if m == 0 else env[k] * yb_ref[m * NEIGH + k] for k in range(NEIGH)]
                while len(terms) > 1:
                    terms = [terms[i] + terms[i + 1] for i in range(0, len(terms), 2)]
                field.append(terms[0] * 0.125)
                v_ref[m, rows, :] = field[m]
            out = []
            for k in range(NEIGH):
                sums = [field[0], None, None]
                for m in range(1, 9):
                    term = field[m] * yb_ref[m * NEIGH + k]
                    sums[PIECE[m]] = term if sums[PIECE[m]] is None else sums[PIECE[m]] + term
                out.append(sums)
            halves.append(out)
        for k in range(NEIGH):
            for p in range(1, 3):
                both = jnp.concatenate([halves[0][k][p], halves[1][k][p]], axis=0)
                inv_ref[p * ATOMS - ATOMS + t * 16 : p * ATOMS - ATOMS + t * 16 + 16, k * ATOMS : (k + 1) * ATOMS] = both.astype(BF16)
    alike = jnp.dot(updt_alike, v_ref[0].astype(BF16), preferred_element_type=F32)
    mean = jnp.zeros((ATOMS, ATOMS), F32)
    for j in range(EDGES // TILE):
        span = slice(j * TILE, (j + 1) * TILE)
        update = jnp.dot(updt, inv_ref[:, span], preferred_element_type=F32)
        edge, ds = silu_pair(lat_ref[:, span] + update + jnp.concatenate([alike] * (TILE // ATOMS), axis=1))
        edge_ref[:, span] = edge
        dse_ref[:, span] = ds
        for i in range(TILE // ATOMS):
            mean = mean + edge[:, i * ATOMS : (i + 1) * ATOMS]
    table_ref[0] = (mean * 0.125).astype(BF16)


def second_kernel(parts, order, *refs):
    gather_ref, scatter_ref, second_ref, secondt_ref, rocol_ref = refs[parts : parts + 5]
    sets = gather_ref.shape[1] // EDGES
    edges = refs[parts + 5 : parts + 5 + sets]
    energy_ref, grad_edge_ref, *outs = refs[parts + 5 + sets : -2]
    other_ref, grad_ref = refs[-2:]
    table = jnp.concatenate([refs[array][row] for array, row in order], axis=1)
    rocol = rocol_ref[...]
    for own in range(sets):
        depth = table.shape[1] - 2 * ATOMS * own
        span = slice(own * EDGES, (own + 1) * EDGES)
        other_ref[:, span] = jnp.dot(table[:, :depth], gather_ref[:depth, span], preferred_element_type=F32)
    wide = 2 * ATOMS
    if sets == 2:
        give_ref = outs.pop(0)
        give_ref[ATOMS:, :] = jnp.zeros((8, EDGES), F32)
    for own in range(sets):
        total = jnp.zeros((ATOMS, ATOMS), F32)
        for j in range(EDGES // wide):
            span = slice(j * wide, (j + 1) * wide)
            both = slice(own * EDGES + j * wide, own * EDGES + (j + 1) * wide)
            other = other_ref[:, both]
            edge = edges[own][:, span]
            hidden, ds = silu_pair(
                jnp.dot(secondt_ref[...], (edge * other).astype(BF16), preferred_element_type=F32)
            )
            total = total + hidden[:, :ATOMS] + hidden[:, ATOMS:]
            grad_hidden = ds * jnp.concatenate([rocol, rocol], axis=1)
            grad_prod = jnp.dot(second_ref[...], grad_hidden.astype(BF16), preferred_element_type=F32)
            grad_prod = grad_prod.astype(BF16).astype(F32)
            if own == 0:
                grad_edge_ref[:, span] = grad_prod * other
            else:
                give_ref[:ATOMS, span] = grad_prod * other
            grad_ref[:, both] = (grad_prod * edge).astype(BF16)
        energy = jnp.sum(total * rocol, axis=0, keepdims=True)
        if own == 0:
            energy_ref[...] = energy
        else:
            give_ref[ATOMS : ATOMS + 1, :ATOMS] = energy
    places = [(ref, row) for ref in outs for row in range(ref.shape[0])]
    for c in range(0, len(places), 2):
        depth = EDGES if c + 2 == len(places) else sets * EDGES
        back = jnp.dot(
            grad_ref[:, :depth], scatter_ref[:depth, c * ATOMS : (c + 2) * ATOMS], preferred_element_type=F32
        )
        for i in range(2):
            ref, row = places[c + i]
            ref[row] = back[:, i * ATOMS : (i + 1) * ATOMS].astype(ref.dtype)


def backward_kernel(
    direct, owned_ref, energy_ref, grad_edge_ref, dse_ref, dsl_ref, dsb_ref, env_ref, v_ref, geo_ref, yb_ref, slope_ref, spot_ref, lane_ref,
    upd_ref, envw_ref, mix_ref, radial_ref, *refs,
):
    *extra, dinv_ref, denv_ref, dlat_ref, part_ref, force_ref, alike_ref = refs
    energy = energy_ref[...]
    if direct:
        given_ref, *extra = extra
        energy = energy + given_ref[ATOMS : ATOMS + 1, :ATOMS]
    outs = extra
    r, ux, uy, uz = (geo_ref[i] for i in range(4))
    share = owned_ref[0] * 0.125
    alike = jnp.zeros((ATOMS, ATOMS), F32)
    for j in range(EDGES // TILE):
        span = slice(j * TILE, (j + 1) * TILE)
        d_edge = grad_edge_ref[:, span] + jnp.concatenate([share] * (TILE // ATOMS), axis=1)
        if direct:
            d_edge = d_edge + given_ref[:ATOMS, span]
        d_pre = d_edge * dse_ref[:, span]
        dlat_ref[:, span] = d_pre
        dinv_ref[:, span] = jnp.dot(
            upd_ref[ATOMS:, :], d_pre.astype(BF16), preferred_element_type=F32
        ).astype(BF16)
        for i in range(TILE // ATOMS):
            alike = alike + d_pre[:, i * ATOMS : (i + 1) * ATOMS]
    alike_ref[...] = jnp.dot(upd_ref[:ATOMS, :], alike.astype(BF16), preferred_element_type=F32)
    part_ref[...] = jnp.zeros(part_ref.shape, F32)
    for t in range(8):
        wide = [
            [
                dinv_ref[p * ATOMS + t * 16 : p * ATOMS + t * 16 + 16, k * ATOMS : (k + 1) * ATOMS].astype(F32)
                for k in range(NEIGH)
            ]
            for p in range(2)
        ]
        halves = []
        for h in range(2):
            rows = slice(t * 16 + h * 8, t * 16 + h * 8 + 8)
            dinv = [[wide[p][k][h * 8 : h * 8 + 8] for k in range(NEIGH)] for p in range(2)]
            env = [env_ref[rows, k * ATOMS : (k + 1) * ATOMS] for k in range(NEIGH)]
            denv = [alike_ref[rows, :] * 0.125] * NEIGH
            for m in range(1, 9):
                down = dinv[PIECE[m] - 1]
                terms = [down[k] * yb_ref[m * NEIGH + k] for k in range(NEIGH)]
                while len(terms) > 1:
                    terms = [terms[i] + terms[i + 1] for i in range(0, len(terms), 2)]
                d_field = terms[0] * 0.125
                field = v_ref[m, rows, :]
                for k in range(NEIGH):
                    spot = m * NEIGH + k
                    part_ref[spot] = part_ref[spot] + (down[k] * field + env[k] * d_field)
                    denv[k] = denv[k] + d_field * yb_ref[spot]
            halves.append(denv)
        for k in range(NEIGH):
            both = jnp.concatenate([halves[0][k], halves[1][k]], axis=0)
            denv_ref[t * 16 : t * 16 + 16, k * ATOMS : (k + 1) * ATOMS] = both.astype(BF16)
    d_r_rows = []
    for j in range(EDGES // TILE):
        span = slice(j * TILE, (j + 1) * TILE)
        d_lat = jnp.dot(envw_ref[...], denv_ref[:, span], preferred_element_type=F32).astype(BF16).astype(F32)
        d_mix = (dlat_ref[:, span] + d_lat) * dsl_ref[:, span]
        d_act = jnp.dot(mix_ref[...], d_mix.astype(BF16), preferred_element_type=F32).astype(BF16).astype(F32)
        d_before = (d_act * dsb_ref[:, span]).astype(BF16)
        d_basis = jnp.dot(radial_ref[...], d_before, preferred_element_type=F32).astype(BF16).astype(F32)
        for i in range(TILE // ATOMS):
            k = j * (TILE // ATOMS) + i
            d_r_rows.append(jnp.sum(slope_ref[k] * d_basis[:, i * ATOMS : (i + 1) * ATOMS], axis=0, keepdims=True))
    d_r = jnp.concatenate(d_r_rows, axis=0)
    dy = [None]
    for m in range(1, 9):
        rows = [jnp.sum(part_ref[m * NEIGH + k], axis=0, keepdims=True) for k in range(NEIGH)]
        dy.append(jnp.concatenate(rows, axis=0))
    d_ux = dy[1] + ROOT3 * (uy * dy[4] + uz * dy[7] + ux * dy[8])
    d_uy = dy[2] + ROOT3 * (ux * dy[4] + uz * dy[5] - uy * dy[8])
    d_uz = dy[3] + ROOT3 * (uy * dy[5] + ux * dy[7]) + 3.0 * uz * dy[6]
    along = ux * d_ux + uy * d_uy + uz * d_uz
    inverse = 1.0 / r
    radial = d_r - along * inverse
    pull = [d_ux * inverse + ux * radial, d_uy * inverse + uy * radial, d_uz * inverse + uz * radial]
    high = [p.astype(BF16).astype(F32) for p in pull]
    low = [p - h for p, h in zip(pull, high)]
    zero = jnp.zeros((1, ATOMS), F32)
    rows, spots = [], []
    for k in range(NEIGH):
        parts = [h[k : k + 1, :] for h in high] + [zero] + [q[k : k + 1, :] for q in low] + [zero]
        rows.append(jnp.concatenate(parts, axis=0))
        spots.append(spot_ref[k])
    for c in range(0, CHUNKS, 2):
        for k in range(NEIGH):
            both = [jnp.where(spots[k] == c + i, rows[k], 0.0) for i in range(2)]
            force_ref[c * 8 : c * 8 + 16, k * ATOMS : (k + 1) * ATOMS] = jnp.concatenate(both, axis=0).astype(BF16)
    back = lax.dot_general(
        force_ref[...], lane_ref[...], (((1,), (1,)), ((), ())), preferred_element_type=F32
    )
    center = jnp.concatenate([jnp.sum(p, axis=0, keepdims=True) for p in pull] + [-energy], axis=0)
    if direct:
        outs[0][...] = jnp.zeros(outs[0].shape, F32)
    for c in range(CHUNKS):
        far, dy, dx = c // 9, c % 9 // 3 - 1, c % 3 - 1
        moved = back[8 * c : 8 * c + 4] + back[8 * c + 4 : 8 * c + 8]
        if (far, dy, dx) == (0, 0, 0):
            moved = moved - center
        if direct:
            outs[0][owner_at(dx, dy, far)] = moved
        else:
            outs[far][(0, 2, 1)[dy + 1] * 3 + (0, 2, 1)[dx + 1]] = moved


def finish_kernel(moved_ref, energy_ref, out_ref):
    slots = energy_ref.shape[-1]
    total = jnp.sum(moved_ref[...], axis=0)
    for block in range(2):
        lanes = slice(block * slots, (block + 1) * slots)
        energy_ref[0, 0, block : block + 1, :] = total[3:4, lanes]
        for c in range(3):
            out_ref[0, 0, block : block + 1, c * slots : (c + 1) * slots] = -total[c : c + 1, lanes]


def call(kernel, outs, scratch=(), name=None, limit=24 << 20, place=pltpu.VMEM, cost=None):
    whole = pl.BlockSpec(memory_space=pltpu.VMEM)
    shapes = [jax.ShapeDtypeStruct(shape, kind) for shape, kind in outs]

    def run(*args):
        return pl.pallas_call(
            kernel,
            out_shape=shapes,
            in_specs=[pl.BlockSpec(memory_space=place)] * len(args),
            out_specs=[whole] * len(shapes),
            scratch_shapes=list(scratch),
            compiler_params=pltpu.CompilerParams(vmem_limit_bytes=limit),
            cost_estimate=cost,
            name=name,
        )(*args)

    return run


def on_device(
    positions, species, neighbors, center_table, neighbor_table, radial_weight, mix_weight,
    env_weight, update_weight, second_weight, readout,
):
    slots = species.shape[-1]
    edges = (ATOMS, EDGES)
    square = (ATOMS, ATOMS)
    readout = readout.reshape(1, ATOMS)
    direct = is_direct()
    devices = 32
    (blank,) = call(
        blank_kernel,
        [((8, ATOMS), F32)],
        name="blank",
        cost=pl.CostEstimate(flops=1 << 34, bytes_accessed=64 << 20, transcendentals=0),
    )()
    (packed,) = call(pack_kernel, [((1, 8, ATOMS), F32)], name="pack")(blank, positions, species, neighbors)
    if direct:
        copies = jnp.broadcast_to(packed, (devices, 8, ATOMS))
        tables = [lax.all_to_all(copies, EVERY, 0, 0, tiled=True)]
    else:
        tables = ring_gather(packed)
    table, code, edge, dsb, dsl, dse, env, field, geo, spread = call(
        functools.partial(forward_kernel, len(tables), direct),
        [
            ((1,) + square, BF16), ((NEIGH, ATOMS), jnp.int32), (edges, F32), (edges, F32), (edges, F32),
            (edges, F32), (edges, F32), ((9,) + square, F32), ((4, NEIGH, ATOMS), F32), ((72, 8, ATOMS), F32),
        ],
        [pltpu.VMEM((2 * ATOMS, EDGES), BF16), pltpu.VMEM(edges, F32), pltpu.VMEM(square, F32)],
        name="forward",
    )(*tables, center_table, neighbor_table, radial_weight, mix_weight, env_weight, update_weight)
    chunks, sets = (10, 2) if direct else (CHUNKS, 1)
    sent = edge
    if direct:
        both = jnp.concatenate([table, shifted(table, "gz", 1)], axis=0)
        both, sent, code, geo = lax.optimization_barrier((both, edge, code, geo))
    gather, scatter, lanes, secondt, rocol, slope, spot = call(
        functools.partial(onehot_kernel, direct),
        [
            ((chunks * ATOMS, sets * EDGES), BF16), ((sets * EDGES, chunks * ATOMS), BF16), (edges, BF16),
            (square, BF16), (square, F32), ((NEIGH, 8, ATOMS), F32), ((NEIGH, 8, ATOMS), jnp.int32),
        ],
        [pltpu.VMEM(square, F32)],
        name="onehot",
        cost=pl.CostEstimate(flops=1 << 30, bytes_accessed=8 << 20, transcendentals=0),
    )(code, *(tables if direct else ()), geo, second_weight, readout)
    if direct:
        tables = [swapped(both, slot) for slot in range(4)] + [both]
        order = [(array, row) for array in range(5) for row in range(2)]
        latents = [edge, shifted(sent, "gz", 1)]
        returned = [((ATOMS + 8, EDGES), F32)] + [((2,) + square, BF16)] * 4 + [((2,) + square, F32)]
    else:
        tables = ring_gather(table)
        order = [(array, row) for array in range(2) for row in range(9)]
        latents = [edge]
        returned = [((9,) + square, BF16)] * 2
    energy, grad_edge, *returned = call(
        functools.partial(second_kernel, len(tables), order),
        [((1, ATOMS), F32), (edges, F32)] + returned,
        [pltpu.VMEM((ATOMS, sets * EDGES), F32), pltpu.VMEM((ATOMS, sets * EDGES), BF16)],
        name="second",
    )(*tables, gather, scatter, second_weight, secondt, rocol, *latents)
    if direct:
        give, *back, home = returned
        given = [shifted(give, "gz", 1)]
        for slot in (3, 2, 1, 0):
            home = home + swapped(back[slot], slot).astype(F32)
        owned = home[:1] + shifted(home[1:], "gz", 1)
    else:
        given = []
        owned = ring_reduce(*returned)
    moved = call(
        functools.partial(backward_kernel, direct),
        [((devices, 4, ATOMS), F32)] if direct else [((9, 4, ATOMS), F32)] * 2,
        [
            pltpu.VMEM((2 * ATOMS, EDGES), BF16), pltpu.VMEM(edges, BF16), pltpu.VMEM(edges, F32),
            pltpu.VMEM((72, 8, ATOMS), F32), pltpu.VMEM((CHUNKS * 8, EDGES), BF16), pltpu.VMEM(square, F32),
        ],
        name="backward",
    )(
        owned, energy, grad_edge, dse, dsl, dsb, env, field, geo, spread, slope, spot, lanes, update_weight, env_weight, mix_weight,
        radial_weight, *given,
    )
    moved = lax.all_to_all(moved[0], EVERY, 0, 0, tiled=True) if direct else ring_reduce(*moved)
    return call(finish_kernel, [((1, 1, 2, slots), F32), ((1, 1, 2, 3 * slots), F32)], name="finish")(moved)


def solution(mesh):
    split = P("gx", "gy", "gz", None)
    return jax.shard_map(
        on_device,
        mesh=mesh,
        in_specs=(split, split, split) + (P(),) * 8,
        out_specs=(split, split),
        check_vma=False,
    )
```
